128 devices in a mesh: dp: 8 (over y, core), mp: 16 (over x, z).
Axes of the slice: x: 4, y: 4, z: 4, core: 2. Of those that a mesh axis runs over, the one named last changes fastest.
Arguments:
- tokens: bfloat16 [1024, 5120], P(None, 'dp'), may hold values from -6 to 6
- gate_a: bfloat16 [27648, 5120], P('mp', 'dp'), may hold values from -0.078125 to 0.078125
- up_a: bfloat16 [27648, 5120], P('mp', 'dp'), may hold values from -0.078125 to 0.078125
- down_a: bfloat16 [27648, 5120], P('mp', 'dp'), may hold values from -0.0390625 to 0.0390625
- gate_b: bfloat16 [27648, 5120], P('mp', 'dp'), may hold values from -0.078125 to 0.078125
- up_b: bfloat16 [27648, 5120], P('mp', 'dp'), may hold values from -0.078125 to 0.078125
- down_b: bfloat16 [27648, 5120], P('mp', 'dp'), may hold values from -0.0390625 to 0.0390625
- perm: int32 [27648], replicated, may hold values from 0 to 27647, as said below
Outputs:
- merged_gate: bfloat16 [27648, 5120], P('mp', 'dp')
- merged_up: bfloat16 [27648, 5120], P('mp', 'dp')
- merged_down: bfloat16 [27648, 5120], P('mp', 'dp')
- match_corr: float32 [27648], P('mp')
The draws below stay inside these ranges and needn't reach their ends.
Inputs may be any that keep to these rules, and one draw needn't show every extreme that they name: perm is a permutation of the 27648 neurons. Cut positions and values into 16 consecutive blocks of 1728: for any block of positions and any block of values, at most 216 positions of the first hold a value of the second, and this bound is reached by some pair of blocks.
All inputs are finite; a program needn't handle non-finite values.
Results may differ from the reference program's by a relative error of at most 0.001.
Values may be sent and summed in bfloat16 or wider, within the bound.
No kernel may reach another device: no remote copies, remote signals or barrier semaphores. Data moves between devices by JAX's collectives and lax.ppermute only.
A program may use at most 192 MiB of HBM per device.

```python
import jax
import jax.numpy as jnp
from jax import lax

D = 5120
FF = 27648
TOKENS = 1024
BLOCKS = 16
LOCAL = 1728


def draw_perm(key, part):
    keys = jax.random.split(key, 4)
    blocks = BLOCKS
    local_rows = LOCAL
    base_count = local_rows // blocks
    offset_one = jax.random.randint(keys[0], (), 0, blocks)
    offset_two = (offset_one + 1 + jax.random.randint(keys[1], (), 0, blocks - 1)) % blocks
    source_ids = jnp.arange(blocks, dtype=jnp.int32)[:, None]
    target_ids = jnp.arange(blocks, dtype=jnp.int32)[None, :]
    plus_mask = ((target_ids - source_ids - offset_one) % blocks == 0).astype(jnp.int32)
    minus_mask = ((target_ids - source_ids - offset_two) % blocks == 0).astype(jnp.int32)
    counts = base_count + base_count * plus_mask - base_count * minus_mask
    cumulative = jnp.cumsum(counts, axis=0)
    within = jnp.arange(local_rows, dtype=jnp.int32)
    source_of = jnp.sum((cumulative.T[:, :, None] <= within[None, None, :]).astype(jnp.int32), axis=1)
    shuffles = jax.vmap(lambda one_key: jax.random.permutation(one_key, local_rows))(jax.random.split(keys[2], blocks))
    source_of = jnp.take_along_axis(source_of, shuffles.astype(jnp.int32), axis=1).reshape(-1).astype(jnp.int32)
    total = blocks * local_rows
    order = jnp.argsort(source_of * total + jnp.arange(total, dtype=jnp.int32), stable=True)
    local_perm = jax.vmap(lambda one_key: jax.random.permutation(one_key, local_rows))(jax.random.split(keys[3], blocks))
    values = jnp.arange(total, dtype=jnp.int32) // local_rows * local_rows + local_perm.reshape(-1).astype(jnp.int32)
    return jnp.zeros((total,), jnp.int32).at[order].set(values)


def levels(own_key, extent, pieces, low, top_value):
    loudness = 1.0
    for dim, parts in pieces:
        draws = jax.random.uniform(jax.random.fold_in(jax.random.fold_in(own_key, 6), dim), (parts,), jnp.float32, low / len(pieces), top_value / len(pieces))
        loudness = loudness * jnp.repeat(jnp.exp(draws), extent[dim] // parts).reshape((-1,) + (1,) * (len(extent) - 1 - dim))
    return loudness


def centred(own_key, dims, width, bound, cuts=(), kind=jnp.bfloat16):
    values = width * jax.random.normal(own_key, dims, jnp.float32)
    if cuts:
        values = values * levels(own_key, dims, cuts, -0.22, 0.18)
    return jnp.clip(values, -bound, bound).astype(kind)


def setup_inputs(seed: int = 0) -> dict:
    key_of = jax.random.split(jax.random.key(seed), 9)
    return {
        "tokens": centred(key_of[0], (TOKENS, D), 1.0, 6.0, ((1, 8),)),
        "gate_a": centred(key_of[1], (FF, D), D ** -0.5, 0.078125, ((0, 16), (1, 8))),
        "up_a": centred(key_of[2], (FF, D), D ** -0.5, 0.078125, ((0, 16), (1, 8))),
        "down_a": centred(key_of[3], (FF, D), FF ** -0.5, 0.0390625, ((0, 16), (1, 8))),
        "gate_b": centred(key_of[4], (FF, D), D ** -0.5, 0.078125, ((0, 16), (1, 8))),
        "up_b": centred(key_of[5], (FF, D), D ** -0.5, 0.078125, ((0, 16), (1, 8))),
        "down_b": centred(key_of[6], (FF, D), FF ** -0.5, 0.0390625, ((0, 16), (1, 8))),
        "perm": draw_perm(jax.random.fold_in(key_of[8], 71), 0),
    }


def pre_act(tokens, weight):
    return lax.dot_general(tokens, weight, (((1,), (1,)), ((), ())), preferred_element_type=jnp.float32)

def merge_rows(first, second):
    return ((first.astype(jnp.float32) + second.astype(jnp.float32)) * 0.5).astype(jnp.bfloat16)

def reference(tokens, gate_a, up_a, down_a, gate_b, up_b, down_b, perm):
    hidden_a = jax.nn.silu(pre_act(tokens, gate_a)) * pre_act(tokens, up_a)
    hidden_b = jax.nn.silu(pre_act(tokens, gate_b)) * pre_act(tokens, up_b)
    matched_b = jnp.take(hidden_b, perm, axis=1)
    first = hidden_a
    second = matched_b
    ntok = TOKENS * 1.0
    sum_a = lax.optimization_barrier(jnp.sum(first, axis=0))
    sum_b = lax.optimization_barrier(jnp.sum(second, axis=0))
    sum_aa = lax.optimization_barrier(jnp.sum(first * first, axis=0))
    sum_bb = lax.optimization_barrier(jnp.sum(second * second, axis=0))
    sum_ab = lax.optimization_barrier(jnp.sum(first * second, axis=0))
    covar = sum_ab - sum_a * sum_b / ntok
    var_a = sum_aa - sum_a * sum_a / ntok
    var_b = sum_bb - sum_b * sum_b / ntok
    match_corr = covar / jnp.sqrt(var_a * var_b + 1e-05)
    merged_gate = merge_rows(gate_a, jnp.take(gate_b, perm, axis=0))
    merged_up = merge_rows(up_a, jnp.take(up_b, perm, axis=0))
    merged_down = merge_rows(down_a, jnp.take(down_b, perm, axis=0))
    return (merged_gate, merged_up, merged_down, match_corr)
```

```python
import functools

import jax
import jax.numpy as jnp
from jax import lax
from jax.experimental import pallas as pl
from jax.experimental.pallas import tpu as pltpu
from jax.sharding import PartitionSpec as P

F32 = jnp.float32
BF16 = jnp.bfloat16
F16 = jnp.float16
NB = 16
CAP = 112
ONE = 64
TWO = CAP - ONE
HOP = 8
OVER = 4 * HOP
SLOTS = 2 * (CAP + HOP)
SCALE = 16.0
VMEM = pl.BlockSpec(memory_space=pltpu.VMEM)
SMEM = pl.BlockSpec(memory_space=pltpu.SMEM)
PARAMS = pltpu.CompilerParams(vmem_limit_bytes=48 * 2**20)


def iota(shape, dim):
    return lax.broadcasted_iota(jnp.int32, shape, dim).astype(F32)


def onehot(keys, ids):
    return jnp.where(keys == ids, 1.0, 0.0).astype(BF16)


def pick(hot, rows):
    return jnp.dot(hot, rows, preferred_element_type=F32)


def ranks(member):
    width = member.shape[1]
    before = (
        lax.broadcasted_iota(jnp.int32, (128, 128), 0)
        < lax.broadcasted_iota(jnp.int32, (128, 128), 1)
    )
    before = jnp.where(before, 1.0, 0.0).astype(BF16)
    carry = jnp.zeros((member.shape[0], 1), F32)
    tiles = []
    for j in range(width // 128):
        tile = member[:, j * 128 : (j + 1) * 128]
        tiles.append(jnp.dot(tile.astype(BF16), before, preferred_element_type=F32) + carry)
        carry = carry + jnp.sum(tile, axis=1, keepdims=True)
    return jnp.concatenate(tiles, axis=1)


def block_of(perm, local):
    block = jnp.zeros(perm.shape, F32)
    for k in range(1, NB + 1):
        block = block + jnp.where(perm >= k * local, 1.0, 0.0)
    return block


def send_one(local, me_ref, perm_ref, gate, up, down, send_ref, index_ref, table_ref, bad_ref):
    me = me_ref[0].astype(F32)
    perm = perm_ref[...]
    width = perm.shape[1]
    block = block_of(perm, local)
    value = perm.astype(F32) - block * local + 1.0
    mine = jnp.where(block == me, 1.0, 0.0)
    lane = iota((NB, 128), 1)
    row = iota((NB, 128), 0)
    count = jnp.zeros((NB, 128), F32)
    for s in range(NB):
        col = jnp.sum(jnp.where(block == s, 1.0, 0.0), axis=1, keepdims=True)
        count = count + jnp.where(lane == s, col, 0.0)
    layers = jnp.maximum(count - CAP, 0.0).astype(jnp.int32)
    layers = ((layers + (NB - 1)) >> 4).astype(F32)
    by_target = jnp.zeros((NB, 128), F32)
    by_source = jnp.zeros((NB, 128), F32)
    for k in range(NB):
        by_target = by_target + jnp.where(row > k, layers[k : k + 1, :], 0.0)
        by_source = by_source + jnp.where(lane > k, layers[:, k : k + 1], 0.0)
    table_ref[0] = by_target
    table_ref[1] = by_source
    table_ref[2] = layers
    most = jnp.maximum(
        jnp.max(jnp.sum(layers, axis=0, keepdims=True)), jnp.max(jnp.sum(layers, axis=1, keepdims=True))
    )
    bad_ref[0] = jnp.where(most > HOP, 1, 0).astype(jnp.int32)

    rank = ranks(mine)
    base = jnp.where(lane == me, by_target, 0.0)
    base = jnp.sum(base, axis=1, keepdims=True)
    extra = (rank - CAP).astype(jnp.int32)
    mid = (extra & (NB - 1)).astype(F32)
    layer = (extra >> 4).astype(F32)
    direct = jnp.where(mine * jnp.where(rank < CAP, 1.0, 0.0) > 0, rank, -1.0)
    detour = jnp.where(mine * jnp.where(rank < CAP, 0.0, 1.0) > 0, mid * HOP + base + layer, -1.0)
    slot = iota((CAP, width), 0)
    hop_slot = iota((NB * HOP, width), 0)
    hop = jnp.zeros((NB * HOP, width), F32)
    for t in range(NB):
        v = value[t : t + 1, :]
        col = jnp.sum(jnp.where(direct[t : t + 1, :] == slot, v, 0.0), axis=1, keepdims=True) - 1.0
        index_ref[t] = col
        hop = hop + jnp.where(detour[t : t + 1, :] == hop_slot, v, 0.0)
    hop = jnp.sum(hop, axis=1, keepdims=True) - 1.0

    ids = iota((4 * ONE, local), 1)
    for i in range(NB // 4):
        keys = jnp.concatenate([index_ref[4 * i + k][:ONE] for k in range(4)], axis=0)
        hot = onehot(keys, ids)
        for j, rows in enumerate((gate, up)):
            out = pick(hot, rows[...]).astype(BF16)
            for k in range(4):
                send_ref[4 * i + k, j * ONE : (j + 1) * ONE] = out[k * ONE : (k + 1) * ONE]
    hot = onehot(hop, iota((NB * HOP, local), 1))
    parts = [pick(hot, rows[...]).reshape(NB, HOP, -1) for rows in (gate, up, down)]
    parts.append(jnp.zeros_like(parts[0]))
    send_ref[:, 2 * ONE :] = jnp.concatenate(parts, axis=1).astype(BF16)


def receive_keys(local, me_ref, perm_ref, table_ref, keys_ref):
    me = me_ref[0].astype(F32)
    block = block_of(perm_ref[...], local)
    width = block.shape[1]
    source = jnp.sum(jnp.where(iota(block.shape, 0) == me, block, 0.0), axis=0, keepdims=True)
    member = jnp.where(source == iota((NB, width), 0), 1.0, 0.0)
    rank = jnp.sum(member * ranks(member), axis=0, keepdims=True)
    mine = jnp.where(iota((NB, 128), 0) == me, table_ref[1], 0.0)
    mine = jnp.sum(mine, axis=0, keepdims=True)
    square = jnp.where(iota((NB, 128), 0) == iota((NB, 128), 1), mine, 0.0)
    base = jnp.sum(square, axis=1, keepdims=True)
    base = jnp.sum(member * base, axis=0, keepdims=True)
    extra = (rank - CAP).astype(jnp.int32)
    mid = (extra & (NB - 1)).astype(F32)
    over = base + (extra >> 4).astype(F32)
    first = rank < ONE
    straight = rank < CAP
    k1 = jnp.where(first, source * ONE + rank, -1.0)
    k2 = jnp.where(first, -1.0, jnp.where(straight, source * TWO + (rank - ONE), -1.0))
    ko = jnp.where(straight, -1.0, mid * HOP + over)
    far = NB * CAP + mid * OVER + over
    near = jnp.where(first, source * ONE + rank, NB * ONE + source * TWO + (rank - ONE))
    keys_ref[0:1] = jnp.where(straight, near, far)
    keys_ref[1:2] = jnp.where(straight, near, far + HOP)
    keys_ref[2:3] = jnp.where(straight, source * CAP + rank, far + 2 * HOP)
    keys_ref[3:4] = k1
    keys_ref[4:5] = k2
    keys_ref[5:6] = ko
    holder = jnp.where(straight, source, mid).astype(jnp.int32)
    piece = (holder & 1).astype(F32)
    device = ((holder >> 1) & 3) * 2 + (holder >> 3)
    keys_ref[6:7] = device.astype(F32)
    keys_ref[7:8] = jnp.where(
        first,
        piece * ONE + rank,
        jnp.where(straight, 2 * ONE + piece * TWO + rank - ONE, 2 * CAP + piece * HOP + over),
    )


def send_rest(local, index_ref, table_ref, gate, up, down, two_ref, three_ref, forward_ref):
    ids = iota((4 * CAP, local), 1)
    for i in range(NB // 4):
        keys = jnp.concatenate([index_ref[4 * i + k] for k in range(4)], axis=0)
        hot = onehot(keys, ids)
        out = pick(hot, down[...]).astype(BF16)
        for k in range(4):
            three_ref[4 * i + k] = out[k * CAP : (k + 1) * CAP]
        hot = jnp.concatenate([hot[k * CAP + ONE : (k + 1) * CAP] for k in range(4)], axis=0)
        for j, rows in enumerate((gate, up)):
            out = pick(hot, rows[...]).astype(BF16)
            for k in range(4):
                two_ref[4 * i + k, j * TWO : (j + 1) * TWO] = out[k * TWO : (k + 1) * TWO]
    two_ref[:, 2 * TWO :] = jnp.zeros((NB, OVER, gate.shape[1]), BF16)
    n = NB * OVER
    tall = lax.broadcasted_iota(jnp.int32, (n, NB), 0) >> 5
    tall = onehot(tall, lax.broadcasted_iota(jnp.int32, (n, NB), 1))
    wide = lax.broadcasted_iota(jnp.int32, (128, n), 1) >> 5
    wide = onehot(wide, lax.broadcasted_iota(jnp.int32, (128, n), 0))

    def spread(x):
        part = jnp.dot(tall, x.astype(BF16), preferred_element_type=F32)
        return jnp.dot(part.astype(BF16), wide, preferred_element_type=F32)

    by_target, by_source, layers = table_ref[0], table_ref[1], table_ref[2]
    r = lax.broadcasted_iota(jnp.int32, (n, n), 0)
    c = lax.broadcasted_iota(jnp.int32, (n, n), 1)
    matrix = jnp.where(((r >> 3) & 3) == ((c >> 3) & 3), 1.0, 0.0)
    depth = (c & 7).astype(F32) - spread(by_target)
    same = jnp.where((r & 7).astype(F32) - spread(by_source) == depth, 1.0, 0.0)
    inside = jnp.where(depth >= 0, 1.0, 0.0) * jnp.where(depth < spread(layers), 1.0, 0.0)
    forward_ref[...] = (matrix * same * inside).astype(BF16)


def fill_forward(forward_ref, one_ref, two_in, two_ref):
    del two_in
    hops = one_ref[...].reshape(NB * OVER, -1)
    out = pick(forward_ref[...], hops).astype(BF16)
    two_ref[...] = out.reshape(NB, OVER, -1)


def order_a(local, keys_ref, gate, up, out_ref):
    pair = (gate, up)
    for size, start, line in ((ONE, 0, 3), (TWO, 2 * ONE, 4)):
        key = keys_ref[line : line + 1, :local]
        for i in range(NB // 4):
            hot = onehot(iota((4 * size, local), 0) + 4 * size * i, key)
            for j, rows in enumerate(pair):
                out = pick(hot, rows[...]).astype(BF16)
                for k in range(4):
                    out_ref[4 * i + k, start + j * size : start + (j + 1) * size] = out[
                        k * size : (k + 1) * size
                    ]
    hot = onehot(iota((NB * HOP, local), 0), keys_ref[5:6, :local])
    parts = [pick(hot, rows[...]).reshape(NB, HOP, -1) for rows in pair]
    out_ref[:, 2 * CAP :] = jnp.concatenate(parts, axis=1).astype(BF16)


def preact(rows, place, own_ref, other_ref, tok_ref, tok_other_ref, plus, minus, hold, own_out):
    y = place[1]

    def product(step):
        chunk = pl.ds(2 * lax.rem(y + step, 4), 2)
        total = None
        for x, tok in ((own_ref, tok_ref), (other_ref, tok_other_ref)):
            block = x[chunk][:, :rows].reshape(2 * rows, -1)
            part = lax.dot_general(
                block, tok[...], (((1,), (1,)), ((), ())), preferred_element_type=F32
            )
            total = part if total is None else total + part
        return total[:rows], total[rows:]

    low, high = product(2)
    plus[0] = low * SCALE
    minus[0] = high * SCALE
    low, high = product(1)
    hold[0] = low * SCALE
    plus[1] = high * SCALE
    low, high = product(3)
    minus[1] = low * SCALE
    hold[1] = high * SCALE
    low, high = product(0)
    own_out[0] = low
    own_out[1] = high


def merge(matrix, local, key_ref, a_ref, *refs):
    *sources, out_ref, held = refs
    if matrix < 2:
        one, two = sources
        for s in range(NB):
            held[s * ONE : (s + 1) * ONE] = one[s, matrix * ONE : (matrix + 1) * ONE]
            start = NB * ONE + s * TWO
            held[start : start + TWO] = two[s, matrix * TWO : (matrix + 1) * TWO]
    else:
        three, two = sources
        for s in range(NB):
            held[s * CAP : (s + 1) * CAP] = three[s]
    for s in range(NB):
        start = NB * CAP + s * OVER
        held[start : start + OVER] = two[s, 2 * TWO :]
    chunk = 192
    for i in range(local // chunk):
        key = key_ref[i * chunk : (i + 1) * chunk, matrix : matrix + 1]
        hot = onehot(key, iota((chunk, held.shape[0]), 1))
        got = pick(hot, held[...])
        a = a_ref[i * chunk : (i + 1) * chunk].astype(F32)
        out_ref[i * chunk : (i + 1) * chunk] = ((a + got) * 0.5).astype(BF16)


def correlate(parts, a_ref, b_ref, *out_refs):
    tokens = a_ref.shape[2]
    for (start_a, start_b, size), out_ref in zip(parts, out_refs):
        for piece in range(2):

            def hidden(ref, start):
                g = ref[piece, start : start + size]
                u = ref[piece, start + size : start + 2 * size]
                return g / (1.0 + jnp.exp(-g)) * u

            a, b = hidden(a_ref, start_a), hidden(b_ref, start_b)
            sa, sb, saa, sbb, sab = (
                jnp.sum(x, axis=1, keepdims=True) for x in (a, b, a * a, b * b, a * b)
            )
            covar = sab - sa * sb / tokens
            var = (saa - sa * sa / tokens) * (sbb - sb * sb / tokens)
            out_ref[piece] = covar / jnp.sqrt(var + 1e-5)


def unorder(local, keys_ref, corr_ref, out_ref):
    place = iota((corr_ref.shape[1], local), 0)
    hot = jnp.where(keys_ref[7:8, :local] == place, 1.0, 0.0)
    rest = corr_ref[...]
    total = jnp.zeros((8, local), F32)
    for _ in range(3):
        part = rest.astype(BF16)
        total = total + jnp.dot(part, hot.astype(BF16), preferred_element_type=F32)
        rest = rest - part.astype(F32)
    keep = jnp.where(keys_ref[6:7, :local] == iota((8, local), 0), total, 0.0)
    out_ref[...] = jnp.sum(keep, axis=0, keepdims=True)


def call(kernel, outs, args, in_specs=None, out_specs=None, flops=0, **more):
    specs = in_specs or [VMEM] * len(args)
    out_bytes = sum(o.size * o.dtype.itemsize for o in outs)
    in_bytes = sum(a.size * a.dtype.itemsize for a in args)
    made = pl.pallas_call(
        kernel,
        out_shape=outs,
        in_specs=specs,
        out_specs=out_specs or [VMEM] * len(outs),
        compiler_params=PARAMS,
        cost_estimate=pl.CostEstimate(
            flops=flops, bytes_accessed=in_bytes + out_bytes, transcendentals=0
        ),
        **more,
    )(*args)
    return made


def shape(dims, dtype=F32):
    return jax.ShapeDtypeStruct(dims, dtype)


def exchange(x):
    return lax.all_to_all(x, "mp", split_axis=0, concat_axis=0, tiled=True)


def swap_cores(x):
    return lax.ppermute(x, "dp", [(i, i ^ 1) for i in range(8)])


def along_y(x, step):
    return lax.ppermute(
        x, "dp", [(i, ((i // 2 + step) % 4) * 2 + i % 2) for i in range(8)]
    )


def reduce_scatter(rows, core, y, mine, other, tokens, tokens_other):
    width = tokens.shape[1]
    ntok = tokens.shape[0]
    block_rows = rows
    made = [shape((2, rows, ntok))] * 4
    grid_spec = pltpu.PrefetchScalarGridSpec(
        num_scalar_prefetch=1,
        grid=(1,),
        in_specs=[
            pl.BlockSpec((8, block_rows, width), lambda i, place: (place[0], 0, 0)),
            pl.BlockSpec((8, rows, width), lambda i, place: (0, 0, 0)),
            pl.BlockSpec((ntok, width), lambda i, place: (0, 0)),
            pl.BlockSpec((ntok, width), lambda i, place: (0, 0)),
        ],
        out_specs=[pl.BlockSpec((2, rows, ntok), lambda i, place: (0, 0, 0))] * 4,
    )
    plus, minus, hold, own = pl.pallas_call(
        functools.partial(preact, rows),
        grid_spec=grid_spec,
        out_shape=made,
        compiler_params=PARAMS,
        cost_estimate=pl.CostEstimate(
            flops=2 * 8 * rows * ntok * 2 * width, bytes_accessed=40 * rows * ntok, transcendentals=0
        ),
    )(jnp.stack([core, y]), mine, other, tokens, tokens_other)
    from_prev = along_y(plus.astype(F16), 1)
    from_next = along_y(minus.astype(F16), 3)
    plus = (hold[0] + from_prev[0].astype(F32)).astype(F16)
    minus = (hold[1] + from_next[0].astype(F32)).astype(F16)
    far_prev = along_y(plus, 1)
    far_next = along_y(minus, 3)
    low = own[0] + (far_prev.astype(F32) + from_next[1].astype(F32)) * (1.0 / SCALE)
    high = own[1] + (far_next.astype(F32) + from_prev[1].astype(F32)) * (1.0 / SCALE)
    return jnp.stack([low, high])


def half_for_partner(x, core, rows):
    return lax.dynamic_slice(x, (8 * (1 - core), 0, 0), (8, rows, x.shape[2]))


def fast(tokens, gate_a, up_a, down_a, gate_b, up_b, down_b, perm):
    local, width = gate_a.shape
    ntok = tokens.shape[0]
    me = lax.axis_index("mp").astype(jnp.int32).reshape(1)
    dp = lax.axis_index("dp").astype(jnp.int32)
    core, y = dp % 2, dp // 2
    padded = -(-local // 128) * 128
    grid = jnp.pad(
        perm.reshape(NB, local), ((0, 0), (0, padded - local)), constant_values=NB * local
    )
    tokens_other = swap_cores(tokens)

    send, index, table, bad = call(
        functools.partial(send_one, local),
        [
            shape((NB, 2 * ONE + OVER, width), BF16),
            shape((NB, CAP, 1)),
            shape((3, NB, 128)),
            shape((1,), jnp.int32),
        ],
        (me, grid, gate_b, up_b, down_b),
        in_specs=[SMEM] + [VMEM] * 4,
        out_specs=[VMEM] * 3 + [SMEM],
        flops=2 * 2432 * local * width,
    )
    one = exchange(send)

    (keys,) = call(
        functools.partial(receive_keys, local),
        [shape((8, padded))],
        (me, grid, table),
        in_specs=[SMEM, VMEM, VMEM],
    )
    (ordered,) = call(
        functools.partial(order_a, local),
        [shape((NB, SLOTS, width), BF16)],
        (keys, gate_a, up_a),
        flops=2 * NB * SLOTS * local * width,
    )
    ordered_other = swap_cores(half_for_partner(ordered, core, SLOTS))
    two, three, forward = call(
        functools.partial(send_rest, local),
        [
            shape((NB, 2 * TWO + OVER, width), BF16),
            shape((NB, CAP, width), BF16),
            shape((NB * OVER, NB * OVER), BF16),
        ],
        (index, table, gate_b, up_b, down_b),
        flops=2 * NB * (CAP + 2 * TWO) * local * width,
    )
    pre_a = reduce_scatter(SLOTS, core, y, ordered, ordered_other, tokens, tokens_other)

    two = pl.pallas_call(
        fill_forward,
        grid=(1,),
        in_specs=[
            pl.BlockSpec((NB * OVER, NB * OVER), lambda i: (0, 0)),
            pl.BlockSpec((NB, OVER, width), lambda i: (0, 2 * ONE // OVER, 0)),
            pl.BlockSpec(memory_space=pl.ANY),
        ],
        out_specs=pl.BlockSpec((NB, OVER, width), lambda i: (0, 2 * TWO // OVER, 0)),
        out_shape=shape(two.shape, BF16),
        input_output_aliases={2: 0},
        compiler_params=PARAMS,
    )(forward, one, two)
    two = exchange(two)

    one_other = swap_cores(half_for_partner(one, core, 2 * ONE))
    pre_one = reduce_scatter(2 * ONE, core, y, one, one_other, tokens, tokens_other)
    two_other = swap_cores(half_for_partner(two, core, CAP))
    pre_two = reduce_scatter(CAP, core, y, two, two_other, tokens, tokens_other)
    three = exchange(three)

    (corr_one,) = call(
        functools.partial(correlate, ((0, 0, ONE),)), [shape((2, ONE, 1))], (pre_a, pre_one)
    )
    corr_two, corr_three = call(
        functools.partial(correlate, ((2 * ONE, 0, TWO), (2 * CAP, 2 * TWO, HOP))),
        [shape((2, TWO, 1)), shape((2, HOP, 1))],
        (pre_a, pre_two),
    )
    corr = jnp.concatenate([c.reshape(-1) for c in (corr_one, corr_two, corr_three)])[None]
    for bit in (1, 2, 4):
        got = lax.ppermute(corr, "dp", [(i, i ^ bit) for i in range(8)])
        upper = (dp // bit) % 2 == 1
        corr = jnp.concatenate(
            [jnp.where(upper, got, corr), jnp.where(upper, corr, got)], axis=0
        )
    (match_corr,) = call(
        functools.partial(unorder, local), [shape((1, local))], (keys, corr)
    )

    tall = keys[:, :local].T
    merged = []
    for matrix, (a, sources) in enumerate(
        ((gate_a, (one, two)), (up_a, (one, two)), (down_a, (three, two)))
    ):
        held = pltpu.VMEM((NB * (CAP + OVER), width), BF16)
        (out,) = call(
            functools.partial(merge, matrix, local),
            [shape((local, width), BF16)],
            (tall, a) + sources,
            scratch_shapes=[held],
            flops=2 * NB * (CAP + OVER) * local * width,
        )
        merged.append(out)
    return tuple(merged) + (match_corr.reshape(-1),), bad[0]


def merge_rows(first, second):
    return ((first.astype(F32) + second.astype(F32)) * 0.5).astype(BF16)


def general(tokens, gate_a, up_a, down_a, gate_b, up_b, down_b, perm):
    me = lax.axis_index("mp")
    local = gate_a.shape[0]
    capacity = 2 * local // NB
    source = perm // local
    before = (jnp.arange(local)[:, None] < jnp.arange(local)[None, :]).astype(BF16)

    def rank_of(member):
        return jnp.dot(member.astype(BF16), before, preferred_element_type=F32).astype(jnp.int32)

    mine = (source == me).reshape(NB, local)
    hit = jnp.logical_and(
        mine[:, None, :], rank_of(mine)[:, None, :] == jnp.arange(capacity)[None, :, None]
    ).astype(jnp.int32)
    send_index = jnp.sum(hit * (perm % local).reshape(NB, 1, local), axis=2).reshape(-1)
    arrived = lax.dynamic_slice_in_dim(source, me * local, local)
    member = (jnp.arange(NB)[:, None] == arrived[None, :]).astype(jnp.int32)
    recv_index = arrived * capacity + jnp.sum(member * rank_of(member), axis=0)

    def matched(rows):
        moved = exchange(jnp.take(rows, send_index, axis=0))
        return jnp.take(moved, recv_index, axis=0)

    gate_match, up_match, down_match = matched(gate_b), matched(up_b), matched(down_b)

    def hidden(gate, up):
        g, u = (
            lax.psum_scatter(
                lax.dot_general(
                    tokens, w, (((1,), (1,)), ((), ())), preferred_element_type=F32
                ),
                "dp",
                scatter_dimension=0,
                tiled=True,
            )
            for w in (gate, up)
        )
        return jax.nn.silu(g) * u

    a, b = hidden(gate_a, up_a), hidden(gate_match, up_match)
    sa, sb, saa, sbb, sab = lax.psum(
        tuple(jnp.sum(x, axis=0) for x in (a, b, a * a, b * b, a * b)), "dp"
    )
    ntok = tokens.shape[0] * 1.0
    covar = sab - sa * sb / ntok
    var = (saa - sa * sa / ntok) * (sbb - sb * sb / ntok)
    return (
        merge_rows(gate_a, gate_match),
        merge_rows(up_a, up_match),
        merge_rows(down_a, down_match),
        covar / jnp.sqrt(var + 1e-05),
    )


def local_program(*args):
    outs, bad = fast(*args)
    return lax.cond(bad > 0, lambda outs, args: general(*args), lambda outs, args: outs, outs, args)


def solution(mesh):
    return jax.shard_map(
        local_program,
        mesh=mesh,
        in_specs=(P(None, "dp"),) + (P("mp", "dp"),) * 6 + (P(),),
        out_specs=(P("mp", "dp"),) * 3 + (P("mp"),),
        check_vma=False,
    )
```

```python
import functools

import jax
import jax.numpy as jnp
from jax import lax
from jax.experimental import pallas as pl
from jax.experimental.pallas import tpu as pltpu
from jax.sharding import PartitionSpec as P

F32 = jnp.float32
BF16 = jnp.bfloat16
F16 = jnp.float16
NB = 16
CAP = 112
ONE = 64
TWO = CAP - ONE
HOP = 8
OVER = 4 * HOP
SLOTS = 2 * (CAP + HOP)
SCALE = 16.0
VMEM = pl.BlockSpec(memory_space=pltpu.VMEM)
SMEM = pl.BlockSpec(memory_space=pltpu.SMEM)
CHEAP = pl.CostEstimate(flops=0, bytes_accessed=0, transcendentals=0)
ALONE = pltpu.CompilerParams(vmem_limit_bytes=58 * 2**20)
PARAMS = pltpu.CompilerParams(vmem_limit_bytes=48 * 2**20)


def iota(shape, dim):
    return lax.broadcasted_iota(jnp.int32, shape, dim).astype(F32)


def onehot(keys, ids):
    return jnp.where(keys == ids, 1.0, 0.0).astype(BF16)


def pick(hot, rows):
    return jnp.dot(hot, rows, preferred_element_type=F32)


def ranks(member):
    width = member.shape[1]
    before = (
        lax.broadcasted_iota(jnp.int32, (128, 128), 0)
        < lax.broadcasted_iota(jnp.int32, (128, 128), 1)
    )
    before = jnp.where(before, 1.0, 0.0).astype(BF16)
    carry = jnp.zeros((member.shape[0], 1), F32)
    tiles = []
    for j in range(width // 128):
        tile = member[:, j * 128 : (j + 1) * 128]
        tiles.append(jnp.dot(tile.astype(BF16), before, preferred_element_type=F32) + carry)
        carry = carry + jnp.sum(tile, axis=1, keepdims=True)
    return jnp.concatenate(tiles, axis=1)


def block_of(perm, local):
    block = jnp.zeros(perm.shape, F32)
    for k in range(1, NB + 1):
        block = block + jnp.where(perm >= k * local, 1.0, 0.0)
    return block


def tables(local, block):
    lane = iota((NB, 128), 1)
    row = iota((NB, 128), 0)
    count = jnp.zeros((NB, 128), F32)
    for s in range(NB):
        col = jnp.sum(jnp.where(block == s, 1.0, 0.0), axis=1, keepdims=True)
        count = count + jnp.where(lane == s, col, 0.0)
    layers = jnp.maximum(count - CAP, 0.0).astype(jnp.int32)
    layers = ((layers + (NB - 1)) >> 4).astype(F32)
    by_target = jnp.zeros((NB, 128), F32)
    by_source = jnp.zeros((NB, 128), F32)
    for k in range(NB):
        by_target = by_target + jnp.where(row > k, layers[k : k + 1, :], 0.0)
        by_source = by_source + jnp.where(lane > k, layers[:, k : k + 1], 0.0)
    return by_target, by_source, layers


def slot_values(keys, value, first, size):
    slot = iota((size, keys.shape[1]), 0) + first
    return [
        jnp.sum(jnp.where(keys[t : t + 1, :] == slot, value[t : t + 1, :], 0.0), axis=1, keepdims=True)
        - 1.0
        for t in range(NB)
    ]


def send_one(
    local, me_ref, perm_ref, gate, up, down, send_ref, key_ref, table_ref, bad_ref, *scratch
):
    *held, sem = scratch
    copies = [
        pltpu.make_async_copy(rows, buffer, sem.at[i])
        for i, (rows, buffer) in enumerate(zip((gate, up, down), held))
    ]
    for copy in copies:
        copy.start()
    me = me_ref[0].astype(F32)
    perm = perm_ref[...]
    width = perm.shape[1]
    block = block_of(perm, local)
    value = perm.astype(F32) - block * local + 1.0
    mine = jnp.where(block == me, 1.0, 0.0)
    by_target, by_source, layers = tables(local, block)
    table_ref[0] = by_target
    table_ref[1] = by_source
    table_ref[2] = layers
    most = jnp.maximum(
        jnp.max(jnp.sum(layers, axis=0, keepdims=True)), jnp.max(jnp.sum(layers, axis=1, keepdims=True))
    )
    bad_ref[0] = jnp.where(most > HOP, 1, 0).astype(jnp.int32)

    rank = ranks(mine)
    base = jnp.where(iota((NB, 128), 1) == me, by_target, 0.0)
    base = jnp.sum(base, axis=1, keepdims=True)
    extra = (rank - CAP).astype(jnp.int32)
    mid = (extra & (NB - 1)).astype(F32)
    layer = (extra >> 4).astype(F32)
    direct = jnp.where(mine * jnp.where(rank < CAP, 1.0, 0.0) > 0, rank, -1.0)
    detour = jnp.where(mine * jnp.where(rank < CAP, 0.0, 1.0) > 0, mid * HOP + base + layer, -1.0)
    key_ref[0] = direct
    key_ref[1] = value
    cols = slot_values(direct, value, 0, ONE)
    hop_slot = iota((NB * HOP, width), 0)
    hop = jnp.zeros((NB * HOP, width), F32)
    for t in range(NB):
        hop = hop + jnp.where(detour[t : t + 1, :] == hop_slot, value[t : t + 1, :], 0.0)
    hop = jnp.sum(hop, axis=1, keepdims=True) - 1.0

    for copy in copies:
        copy.wait()
    ids = iota((4 * ONE, local), 1)
    for i in range(NB // 4):
        hot = onehot(jnp.concatenate(cols[4 * i : 4 * i + 4], axis=0), ids)
        for j, rows in enumerate(held[:2]):
            out = pick(hot, rows[...]).astype(BF16)
            for k in range(4):
                send_ref[4 * i + k, j * ONE : (j + 1) * ONE] = out[k * ONE : (k + 1) * ONE]
    hot = onehot(hop, iota((NB * HOP, local), 1))
    parts = [pick(hot, rows[...]).reshape(NB, HOP, -1) for rows in held]
    parts.append(jnp.zeros_like(parts[0]))
    send_ref[:, 2 * ONE :] = jnp.concatenate(parts, axis=1).astype(BF16)


def receive_keys(local, me_ref, perm_ref, table_ref, keys_ref):
    me = me_ref[0].astype(F32)
    block = block_of(perm_ref[...], local)
    width = block.shape[1]
    source = jnp.sum(jnp.where(iota(block.shape, 0) == me, block, 0.0), axis=0, keepdims=True)
    member = jnp.where(source == iota((NB, width), 0), 1.0, 0.0)
    rank = jnp.sum(member * ranks(member), axis=0, keepdims=True)
    mine = jnp.where(iota((NB, 128), 0) == me, table_ref[1], 0.0)
    mine = jnp.sum(mine, axis=0, keepdims=True)
    square = jnp.where(iota((NB, 128), 0) == iota((NB, 128), 1), mine, 0.0)
    base = jnp.sum(square, axis=1, keepdims=True)
    base = jnp.sum(member * base, axis=0, keepdims=True)
    extra = (rank - CAP).astype(jnp.int32)
    mid = (extra & (NB - 1)).astype(F32)
    over = base + (extra >> 4).astype(F32)
    first = rank < ONE
    straight = rank < CAP
    k1 = jnp.where(first, source * ONE + rank, -1.0)
    k2 = jnp.where(first, -1.0, jnp.where(straight, source * TWO + (rank - ONE), -1.0))
    ko = jnp.where(straight, -1.0, mid * HOP + over)
    keys_ref[0:1] = jnp.where(straight, source * CAP + rank, NB * CAP + mid * HOP + over)
    keys_ref[1:3] = jnp.zeros((2, width), F32)
    keys_ref[3:4] = k1
    keys_ref[4:5] = k2
    keys_ref[5:6] = ko
    holder = jnp.where(straight, source, mid).astype(jnp.int32)
    piece = (holder & 1).astype(F32)
    device = ((holder >> 1) & 3) * 2 + (holder >> 3)
    keys_ref[6:7] = device.astype(F32)
    keys_ref[7:8] = jnp.where(
        first,
        piece * ONE + rank,
        jnp.where(straight, 2 * ONE + piece * TWO + rank - ONE, 2 * CAP + piece * HOP + over),
    )


def send_rest(local, key_ref, table_ref, gate, up, down, two_ref, three_ref, forward_ref):
    low = slot_values(key_ref[0], key_ref[1], 0, ONE)
    top = slot_values(key_ref[0], key_ref[1], ONE, TWO)
    ids = iota((4 * CAP, local), 1)
    for i in range(NB // 4):
        keys = [x for t in range(4 * i, 4 * i + 4) for x in (low[t], top[t])]
        hot = onehot(jnp.concatenate(keys, axis=0), ids)
        out = pick(hot, down[...]).astype(BF16)
        for k in range(4):
            three_ref[4 * i + k] = out[k * CAP : (k + 1) * CAP]
        hot = jnp.concatenate([hot[k * CAP + ONE : (k + 1) * CAP] for k in range(4)], axis=0)
        for j, rows in enumerate((gate, up)):
            out = pick(hot, rows[...]).astype(BF16)
            for k in range(4):
                two_ref[4 * i + k, j * TWO : (j + 1) * TWO] = out[k * TWO : (k + 1) * TWO]
    n = NB * OVER
    tall = lax.broadcasted_iota(jnp.int32, (n, NB), 0) >> 5
    tall = onehot(tall, lax.broadcasted_iota(jnp.int32, (n, NB), 1))
    wide = lax.broadcasted_iota(jnp.int32, (128, n), 1) >> 5
    wide = onehot(wide, lax.broadcasted_iota(jnp.int32, (128, n), 0))

    def spread(x):
        part = jnp.dot(tall, x.astype(BF16), preferred_element_type=F32)
        return jnp.dot(part.astype(BF16), wide, preferred_element_type=F32)

    by_target, by_source, layers = table_ref[0], table_ref[1], table_ref[2]
    r = lax.broadcasted_iota(jnp.int32, (n, n), 0)
    c = lax.broadcasted_iota(jnp.int32, (n, n), 1)
    matrix = jnp.where(((r >> 3) & 3) == ((c >> 3) & 3), 1.0, 0.0)
    depth = (c & 7).astype(F32) - spread(by_target)
    same = jnp.where((r & 7).astype(F32) - spread(by_source) == depth, 1.0, 0.0)
    inside = jnp.where(depth >= 0, 1.0, 0.0) * jnp.where(depth < spread(layers), 1.0, 0.0)
    forward_ref[...] = (matrix * same * inside).astype(BF16)


def fill_forward(forward_ref, one_ref, two_in, two_ref):
    two_ref[:, : 2 * TWO] = two_in[...]
    hops = one_ref[...].reshape(NB * OVER, -1)
    out = pick(forward_ref[...], hops).astype(BF16)
    two_ref[:, 2 * TWO :] = out.reshape(-1, OVER, out.shape[1])


def order_a(local, keys_ref, gate, up, out_ref):
    pair = (gate, up)
    for size, start, line in ((ONE, 0, 3), (TWO, 2 * ONE, 4)):
        key = keys_ref[line : line + 1, :local]
        for i in range(NB // 4):
            hot = onehot(iota((4 * size, local), 0) + 4 * size * i, key)
            for j, rows in enumerate(pair):
                out = pick(hot, rows[...]).astype(BF16)
                for k in range(4):
                    out_ref[4 * i + k, start + j * size : start + (j + 1) * size] = out[
                        k * size : (k + 1) * size
                    ]
    hot = onehot(iota((NB * HOP, local), 0), keys_ref[5:6, :local])
    parts = [pick(hot, rows[...]).reshape(NB, HOP, -1) for rows in pair]
    out_ref[:, 2 * CAP :] = jnp.concatenate(parts, axis=1).astype(BF16)


def preact(rows, place, own_ref, other_ref, tok_ref, tok_other_ref, out_ref):
    del place
    total = None
    for x, tok in ((own_ref, tok_ref), (other_ref, tok_other_ref)):
        part = lax.dot_general(
            x[:, :rows].reshape(2 * rows, -1),
            tok[...],
            (((1,), (1,)), ((), ())),
            preferred_element_type=F32,
        )
        total = part if total is None else total + part
    out_ref[...] = total.reshape(out_ref.shape)


def compact(matrix, sources, held):
    if matrix < 2:
        one, two = sources
        for s in range(NB):
            start = s * CAP
            held[start : start + ONE] = one[s, matrix * ONE : (matrix + 1) * ONE]
            held[start + ONE : start + CAP] = two[s, matrix * TWO : (matrix + 1) * TWO]
    else:
        three, two = sources
        for s in range(NB):
            held[s * CAP : (s + 1) * CAP] = three[s]
    far = two[:, 2 * TWO :].astype(F32)[:, matrix * HOP : (matrix + 1) * HOP]
    held[NB * CAP :] = far.reshape(NB * HOP, -1).astype(BF16)


def merge(matrices, local, key_ref, *refs):
    n = len(matrices)
    rows_a, sources, outs, helds = refs[:n], refs[n : n + 2], refs[n + 2 : 2 * n + 2], refs[2 * n + 2 :]
    for matrix, held in zip(matrices, helds):
        compact(matrix, sources, held)
    chunk = 192
    for i in range(local // chunk):
        part = slice(i * chunk, (i + 1) * chunk)
        hot = onehot(key_ref[part, 0:1], iota((chunk, NB * (CAP + HOP)), 1))
        for a, out, held in zip(rows_a, outs, helds):
            got = pick(hot, held[...])
            out[part] = ((a[part].astype(F32) + got) * 0.5).astype(BF16)


def correlate(parts, *refs):
    a_refs, b_refs, out_refs = refs[:2], refs[2:4], refs[-len(parts) :]
    tokens = a_refs[0].shape[1]

    def hidden(ref, start, size):
        g = ref[start : start + size]
        u = ref[start + size : start + 2 * size]
        return g / (1.0 + jnp.exp(-g)) * u

    for (start_a, start_b, size), out_ref in zip(parts, out_refs):
        for piece in range(2):
            a = hidden(a_refs[piece], start_a, size)
            b = hidden(b_refs[piece], start_b, size)
            sa, sb, saa, sbb, sab = (
                jnp.sum(x, axis=1, keepdims=True) for x in (a, b, a * a, b * b, a * b)
            )
            covar = sab - sa * sb / tokens
            var = (saa - sa * sa / tokens) * (sbb - sb * sb / tokens)
            out_ref[piece] = covar / jnp.sqrt(var + 1e-5)


def unorder(local, me_ref, keys_ref, corr_ref, out_ref):
    place = iota((corr_ref.shape[1], local), 0)
    hot = jnp.where(keys_ref[7:8, :local] == place, 1.0, 0.0)
    rest = corr_ref[...]
    total = jnp.zeros((8, local), F32)
    for _ in range(3):
        part = rest.astype(BF16)
        total = total + jnp.dot(part, hot.astype(BF16), preferred_element_type=F32)
        rest = rest - part.astype(F32)
    owner = lax.broadcasted_iota(jnp.int32, (8, local), 0) ^ me_ref[0]
    keep = jnp.where(keys_ref[6:7, :local] == owner.astype(F32), total, 0.0)
    out_ref[...] = jnp.sum(keep, axis=0, keepdims=True)


def call(kernel, outs, args, in_specs=None, out_specs=None, params=PARAMS, **more):
    specs = in_specs or [VMEM] * len(args)
    made = pl.pallas_call(
        kernel,
        out_shape=outs,
        in_specs=specs,
        out_specs=out_specs or [VMEM] * len(outs),
        compiler_params=params,
        cost_estimate=CHEAP,
        **more,
    )(*args)
    return made


def shape(dims, dtype=F32):
    return jax.ShapeDtypeStruct(dims, dtype)


def exchange(x):
    return lax.all_to_all(x, "mp", split_axis=0, concat_axis=0, tiled=True)


def swap_cores(x):
    return lax.ppermute(x, "dp", [(i, i ^ 1) for i in range(8)])


def along_y(x, step):
    return lax.ppermute(
        x, "dp", [(i, ((i // 2 + step) % 4) * 2 + i % 2) for i in range(8)]
    )


def reduce_scatter(rows, core, y, mine, other, tokens, tokens_other):
    width = tokens.shape[1]
    ntok = tokens.shape[0]

    def chunk(i, place):
        return lax.rem(place[1] + i + 1, 4)

    pre = pl.pallas_call(
        functools.partial(preact, rows),
        grid_spec=pltpu.PrefetchScalarGridSpec(
            num_scalar_prefetch=1,
            grid=(4,),
            in_specs=[
                pl.BlockSpec((2, rows, width), lambda i, p: (4 * p[0] + chunk(i, p), 0, 0)),
                pl.BlockSpec((2, rows, width), lambda i, p: (chunk(i, p), 0, 0)),
                pl.BlockSpec((ntok, width), lambda i, p: (0, 0)),
                pl.BlockSpec((ntok, width), lambda i, p: (0, 0)),
            ],
            out_specs=pl.BlockSpec((2, rows, ntok), lambda i, p: (i, 0, 0)),
        ),
        out_shape=shape((8, rows, ntok)),
        compiler_params=PARAMS,
        cost_estimate=CHEAP,
    )(jnp.stack([core, y]), mine, other, tokens, tokens_other)
    from_prev = along_y((pre[1:3] * SCALE).astype(F16), 1)
    from_next = along_y((pre[3:5] * SCALE).astype(F16), 3)
    far_prev = along_y((pre[0] * SCALE + from_prev[1].astype(F32)).astype(F16), 1)
    far_next = along_y((pre[5] * SCALE + from_next[0].astype(F32)).astype(F16), 3)
    low = pre[6] + (far_prev.astype(F32) + from_next[1].astype(F32)) * (1.0 / SCALE)
    high = pre[7] + (far_next.astype(F32) + from_prev[0].astype(F32)) * (1.0 / SCALE)
    return low, high


def half_for_partner(x, core, rows):
    return lax.dynamic_slice(x, (8 * (1 - core), 0, 0), (8, rows, x.shape[2]))


def fast(tokens, gate_a, up_a, down_a, gate_b, up_b, down_b, perm):
    local, width = gate_a.shape
    ntok = tokens.shape[0]
    me = lax.axis_index("mp").astype(jnp.int32).reshape(1)
    dp = lax.axis_index("dp").astype(jnp.int32)
    core, y = dp & 1, dp >> 1
    padded = -(-local // 128) * 128
    grid = jnp.pad(
        perm.reshape(NB, local), ((0, 0), (0, padded - local)), constant_values=NB * local
    )
    tokens_other = swap_cores(tokens)

    send, slot_keys, table, bad = call(
        functools.partial(send_one, local),
        [
            shape((NB, 2 * ONE + OVER, width), BF16),
            shape((2, NB, padded)),
            shape((3, NB, 128)),
            shape((1,), jnp.int32),
        ],
        (me, grid, gate_b, up_b, down_b),
        in_specs=[SMEM, VMEM] + [pl.BlockSpec(memory_space=pl.ANY)] * 3,
        out_specs=[VMEM] * 3 + [SMEM],
        scratch_shapes=[pltpu.VMEM((local, width), BF16)] * 3 + [pltpu.SemaphoreType.DMA((3,))],
        params=ALONE,
    )
    one = exchange(send)

    (keys,) = call(
        functools.partial(receive_keys, local),
        [shape((8, padded))],
        (me, grid, table),
        in_specs=[SMEM, VMEM, VMEM],
    )
    (ordered,) = call(
        functools.partial(order_a, local),
        [shape((NB, SLOTS, width), BF16)],
        (keys, gate_a, up_a),
    )
    ordered_other = swap_cores(half_for_partner(ordered, core, SLOTS))
    two, three, forward = call(
        functools.partial(send_rest, local),
        [
            shape((NB, 2 * TWO, width), BF16),
            shape((NB, CAP, width), BF16),
            shape((NB * OVER, NB * OVER), BF16),
        ],
        (slot_keys, table, gate_b, up_b, down_b),
    )
    pre_a = reduce_scatter(SLOTS, core, y, ordered, ordered_other, tokens, tokens_other)

    steps = 4
    two = pl.pallas_call(
        fill_forward,
        grid=(steps,),
        in_specs=[
            pl.BlockSpec((NB * OVER // steps, NB * OVER), lambda i: (i, 0)),
            pl.BlockSpec((NB, OVER, width), lambda i: (0, 2 * ONE // OVER, 0)),
            pl.BlockSpec((NB // steps, 2 * TWO, width), lambda i: (i, 0, 0)),
        ],
        out_specs=pl.BlockSpec((NB // steps, 2 * TWO + OVER, width), lambda i: (i, 0, 0)),
        out_shape=shape((NB, 2 * TWO + OVER, width), BF16),
        compiler_params=ALONE,
        cost_estimate=CHEAP,
    )(forward, one, two)
    two = exchange(two)

    one_other = swap_cores(half_for_partner(one, core, 2 * ONE))
    pre_one = reduce_scatter(2 * ONE, core, y, one, one_other, tokens, tokens_other)
    two_other = swap_cores(half_for_partner(two, core, CAP))
    pre_two = reduce_scatter(CAP, core, y, two, two_other, tokens, tokens_other)
    three = exchange(three)

    tall = keys[:, :local].T
    held = pltpu.VMEM((NB * (CAP + HOP), width), BF16)
    merged_gate, merged_up = call(
        functools.partial(merge, (0, 1), local),
        [shape((local, width), BF16)] * 2,
        (tall, gate_a, up_a, one, two),
        scratch_shapes=[held] * 2,
    )
    (corr_one,) = call(
        functools.partial(correlate, ((0, 0, ONE),)), [shape((2, ONE, 1))], pre_a + pre_one
    )
    corr_two, corr_three = call(
        functools.partial(correlate, ((2 * ONE, 0, TWO), (2 * CAP, 2 * TWO, HOP))),
        [shape((2, TWO, 1)), shape((2, HOP, 1))],
        pre_a + pre_two + (merged_gate,),
        in_specs=[VMEM] * 4 + [pl.BlockSpec(memory_space=pl.ANY)],
    )
    corr = jnp.concatenate([c.reshape(-1) for c in (corr_one, corr_two, corr_three)])[None]
    for bit in (1, 2, 4):
        got = lax.ppermute(corr, "dp", [(i, i ^ bit) for i in range(8)])
        corr = jnp.concatenate([corr, got], axis=0)
    (match_corr,) = call(
        functools.partial(unorder, local), [shape((1, local))],
        (dp.reshape(1), keys, corr),
        in_specs=[SMEM, VMEM, VMEM],
    )

    (merged_down,) = call(
        functools.partial(merge, (2,), local),
        [shape((local, width), BF16)],
        (tall, down_a, three, two),
        scratch_shapes=[held],
    )
    return (merged_gate, merged_up, merged_down, match_corr.reshape(-1)), bad[0]


def merge_rows(first, second):
    return ((first.astype(F32) + second.astype(F32)) * 0.5).astype(BF16)


def general(tokens, gate_a, up_a, down_a, gate_b, up_b, down_b, perm):
    me = lax.axis_index("mp")
    local = gate_a.shape[0]
    capacity = 2 * local // NB
    source = perm // local
    before = (jnp.arange(local)[:, None] < jnp.arange(local)[None, :]).astype(BF16)

    def rank_of(member):
        return jnp.dot(member.astype(BF16), before, preferred_element_type=F32).astype(jnp.int32)

    mine = (source == me).reshape(NB, local)
    hit = jnp.logical_and(
        mine[:, None, :], rank_of(mine)[:, None, :] == jnp.arange(capacity)[None, :, None]
    ).astype(jnp.int32)
    send_index = jnp.sum(hit * (perm % local).reshape(NB, 1, local), axis=2).reshape(-1)
    arrived = lax.dynamic_slice_in_dim(source, me * local, local)
    member = (jnp.arange(NB)[:, None] == arrived[None, :]).astype(jnp.int32)
    recv_index = arrived * capacity + jnp.sum(member * rank_of(member), axis=0)

    def matched(rows):
        moved = exchange(jnp.take(rows, send_index, axis=0))
        return jnp.take(moved, recv_index, axis=0)

    gate_match, up_match, down_match = matched(gate_b), matched(up_b), matched(down_b)

    def hidden(gate, up):
        g, u = (
            jnp.sum(
                lax.all_to_all(
                    lax.dot_general(
                        tokens, w, (((1,), (1,)), ((), ())), preferred_element_type=F32
                    ).reshape(8, -1, local),
                    "dp",
                    split_axis=0,
                    concat_axis=0,
                    tiled=True,
                ),
                axis=0,
            )
            for w in (gate, up)
        )
        return jax.nn.silu(g) * u

    a, b = hidden(gate_a, up_a), hidden(gate_match, up_match)
    sums = jnp.stack([jnp.sum(x, axis=0) for x in (a, b, a * a, b * b, a * b)])
    for bit in (1, 2, 4):
        sums = sums + lax.ppermute(sums, "dp", [(i, i ^ bit) for i in range(8)])
    sa, sb, saa, sbb, sab = sums
    ntok = tokens.shape[0] * 1.0
    covar = sab - sa * sb / ntok
    var = (saa - sa * sa / ntok) * (sbb - sb * sb / ntok)
    return (
        merge_rows(gate_a, gate_match),
        merge_rows(up_a, up_match),
        merge_rows(down_a, down_match),
        covar / jnp.sqrt(var + 1e-05),
    )


def local_program(*args):
    outs, bad = fast(*args)
    return lax.cond(bad > 0, lambda outs, args: general(*args), lambda outs, args: outs, outs, args)


def solution(mesh):
    return jax.shard_map(
        local_program,
        mesh=mesh,
        in_specs=(P(None, "dp"),) + (P("mp", "dp"),) * 6 + (P(),),
        out_specs=(P("mp", "dp"),) * 3 + (P("mp"),),
        check_vma=False,
    )
```

```python
import functools

import jax
import jax.numpy as jnp
from jax import lax
from jax.experimental import pallas as pl
from jax.experimental.pallas import tpu as pltpu
from jax.sharding import PartitionSpec as P

F32 = jnp.float32
BF16 = jnp.bfloat16
F16 = jnp.float16
NB = 16
CAP = 112
ONE = 64
TWO = CAP - ONE
HOP = 8
OVER = 4 * HOP
SLOTS = 2 * (CAP + HOP)
SCALE = 16.0
VMEM = pl.BlockSpec(memory_space=pltpu.VMEM)
SMEM = pl.BlockSpec(memory_space=pltpu.SMEM)
CHEAP = pl.CostEstimate(flops=0, bytes_accessed=0, transcendentals=0)
ALONE = pltpu.CompilerParams(vmem_limit_bytes=58 * 2**20)
PARAMS = pltpu.CompilerParams(vmem_limit_bytes=48 * 2**20)


def iota(shape, dim):
    return lax.broadcasted_iota(jnp.int32, shape, dim).astype(F32)


def onehot(keys, ids):
    return jnp.where(keys == ids, 1.0, 0.0).astype(BF16)


def pick(hot, rows):
    return jnp.dot(hot, rows, preferred_element_type=F32)


def ranks(member):
    width = member.shape[1]
    before = (
        lax.broadcasted_iota(jnp.int32, (128, 128), 0)
        < lax.broadcasted_iota(jnp.int32, (128, 128), 1)
    )
    before = jnp.where(before, 1.0, 0.0).astype(BF16)
    carry = jnp.zeros((member.shape[0], 1), F32)
    tiles = []
    for j in range(width // 128):
        tile = member[:, j * 128 : (j + 1) * 128]
        tiles.append(jnp.dot(tile.astype(BF16), before, preferred_element_type=F32) + carry)
        carry = carry + jnp.sum(tile, axis=1, keepdims=True)
    return jnp.concatenate(tiles, axis=1)


def block_of(perm, local):
    block = jnp.zeros(perm.shape, F32)
    for k in range(1, NB + 1):
        block = block + jnp.where(perm >= k * local, 1.0, 0.0)
    return block


def tables(local, block):
    lane = iota((NB, 128), 1)
    row = iota((NB, 128), 0)
    count = jnp.zeros((NB, 128), F32)
    for s in range(NB):
        col = jnp.sum(jnp.where(block == s, 1.0, 0.0), axis=1, keepdims=True)
        count = count + jnp.where(lane == s, col, 0.0)
    layers = jnp.maximum(count - CAP, 0.0).astype(jnp.int32)
    layers = ((layers + (NB - 1)) >> 4).astype(F32)
    by_target = jnp.zeros((NB, 128), F32)
    by_source = jnp.zeros((NB, 128), F32)
    for k in range(NB):
        by_target = by_target + jnp.where(row > k, layers[k : k + 1, :], 0.0)
        by_source = by_source + jnp.where(lane > k, layers[:, k : k + 1], 0.0)
    return by_target, by_source, layers


def slot_values(keys, value, first, size):
    slot = iota((size, keys.shape[1]), 0) + first
    return [
        jnp.sum(jnp.where(keys[t : t + 1, :] == slot, value[t : t + 1, :], 0.0), axis=1, keepdims=True)
        - 1.0
        for t in range(keys.shape[0])
    ]


def send_one(
    local, me_ref, perm_ref, gate, up, down, send_ref, key_ref, table_ref, bad_ref, *scratch
):
    *held, sem = scratch
    copies = [
        pltpu.make_async_copy(rows, buffer, sem.at[i])
        for i, (rows, buffer) in enumerate(zip((gate, up, down), held))
    ]
    for copy in copies:
        copy.start()
    me = me_ref[0].astype(F32)
    perm = perm_ref[...]
    width = perm.shape[1]
    block = block_of(perm, local)
    value = perm.astype(F32) - block * local + 1.0
    mine = jnp.where(block == me, 1.0, 0.0)
    by_target, by_source, layers = tables(local, block)
    table_ref[0] = by_target
    table_ref[1] = by_source
    table_ref[2] = layers
    most = jnp.maximum(
        jnp.max(jnp.sum(layers, axis=0, keepdims=True)), jnp.max(jnp.sum(layers, axis=1, keepdims=True))
    )
    bad_ref[0] = jnp.where(most > HOP, 1, 0).astype(jnp.int32)

    rank = ranks(mine)
    base = jnp.where(iota((NB, 128), 1) == me, by_target, 0.0)
    base = jnp.sum(base, axis=1, keepdims=True)
    extra = (rank - CAP).astype(jnp.int32)
    mid = (extra & (NB - 1)).astype(F32)
    layer = (extra >> 4).astype(F32)
    direct = jnp.where(mine * jnp.where(rank < CAP, 1.0, 0.0) > 0, rank, -1.0)
    detour = jnp.where(mine * jnp.where(rank < CAP, 0.0, 1.0) > 0, mid * HOP + base + layer, -1.0)
    for i in range(NB // 4):
        key_ref[i, 0, :4] = direct[4 * i : 4 * i + 4]
        key_ref[i, 1, :4] = value[4 * i : 4 * i + 4]
    cols = slot_values(direct, value, 0, ONE)
    hop_slot = iota((NB * HOP, width), 0)
    hop = jnp.zeros((NB * HOP, width), F32)
    for t in range(NB):
        hop = hop + jnp.where(detour[t : t + 1, :] == hop_slot, value[t : t + 1, :], 0.0)
    hop = jnp.sum(hop, axis=1, keepdims=True) - 1.0

    for copy in copies:
        copy.wait()
    ids = iota((4 * ONE, local), 1)
    for i in range(NB // 4):
        hot = onehot(jnp.concatenate(cols[4 * i : 4 * i + 4], axis=0), ids)
        for j, rows in enumerate(held[:2]):
            out = pick(hot, rows[...]).astype(BF16)
            for k in range(4):
                send_ref[4 * i + k, j * ONE : (j + 1) * ONE] = out[k * ONE : (k + 1) * ONE]
    hot = onehot(hop, iota((NB * HOP, local), 1))
    parts = [pick(hot, rows[...]).reshape(NB, HOP, -1) for rows in held]
    parts.append(jnp.zeros_like(parts[0]))
    send_ref[:, 2 * ONE :] = jnp.concatenate(parts, axis=1).astype(BF16)


def receive_keys(local, me_ref, perm_ref, table_ref, keys_ref):
    me = me_ref[0].astype(F32)
    block = block_of(perm_ref[...], local)
    width = block.shape[1]
    source = jnp.sum(jnp.where(iota(block.shape, 0) == me, block, 0.0), axis=0, keepdims=True)
    member = jnp.where(source == iota((NB, width), 0), 1.0, 0.0)
    rank = jnp.sum(member * ranks(member), axis=0, keepdims=True)
    mine = jnp.where(iota((NB, 128), 0) == me, table_ref[1], 0.0)
    mine = jnp.sum(mine, axis=0, keepdims=True)
    square = jnp.where(iota((NB, 128), 0) == iota((NB, 128), 1), mine, 0.0)
    base = jnp.sum(square, axis=1, keepdims=True)
    base = jnp.sum(member * base, axis=0, keepdims=True)
    extra = (rank - CAP).astype(jnp.int32)
    mid = (extra & (NB - 1)).astype(F32)
    over = base + (extra >> 4).astype(F32)
    first = rank < ONE
    straight = rank < CAP
    k1 = jnp.where(first, source * ONE + rank, -1.0)
    k2 = jnp.where(first, -1.0, jnp.where(straight, source * TWO + (rank - ONE), -1.0))
    ko = jnp.where(straight, -1.0, mid * HOP + over)
    keys_ref[0:1] = jnp.where(straight, source * CAP + rank, NB * CAP + mid * HOP + over)
    keys_ref[1:3] = jnp.zeros((2, width), F32)
    keys_ref[3:4] = k1
    keys_ref[4:5] = k2
    keys_ref[5:6] = ko
    holder = jnp.where(straight, source, mid).astype(jnp.int32)
    piece = (holder & 1).astype(F32)
    device = ((holder >> 1) & 3) * 2 + (holder >> 3)
    keys_ref[6:7] = device.astype(F32)
    keys_ref[7:8] = jnp.where(
        first,
        piece * ONE + rank,
        jnp.where(straight, 2 * ONE + piece * TWO + rank - ONE, 2 * CAP + piece * HOP + over),
    )


def send_rest(local, key_ref, table_ref, gate, up, down, two_ref, three_ref, forward_ref):
    step = pl.program_id(0)
    keys, value = key_ref[0, 0, :4], key_ref[0, 1, :4]
    low = slot_values(keys, value, 0, ONE)
    top = slot_values(keys, value, ONE, TWO)
    ids = iota((4 * CAP, local), 1)
    hot = onehot(jnp.concatenate([x for pair in zip(low, top) for x in pair], axis=0), ids)
    out = pick(hot, down[...]).astype(BF16)
    three_ref[...] = out.reshape(three_ref.shape)
    hot = jnp.concatenate([hot[k * CAP + ONE : (k + 1) * CAP] for k in range(4)], axis=0)
    for j, rows in enumerate((gate, up)):
        out = pick(hot, rows[...]).astype(BF16)
        two_ref[:, j * TWO : (j + 1) * TWO] = out.reshape(4, TWO, -1)
    two_ref[:, 2 * TWO :] = jnp.zeros((4, OVER, gate.shape[1]), BF16)

    @pl.when(step == 0)
    def _():
        forward_ref[...] = forwarding(table_ref)


def forwarding(table_ref):
    n = NB * OVER
    tall = lax.broadcasted_iota(jnp.int32, (n, NB), 0) >> 5
    tall = onehot(tall, lax.broadcasted_iota(jnp.int32, (n, NB), 1))
    wide = lax.broadcasted_iota(jnp.int32, (128, n), 1) >> 5
    wide = onehot(wide, lax.broadcasted_iota(jnp.int32, (128, n), 0))

    def spread(x):
        part = jnp.dot(tall, x.astype(BF16), preferred_element_type=F32)
        return jnp.dot(part.astype(BF16), wide, preferred_element_type=F32)

    by_target, by_source, layers = table_ref[0], table_ref[1], table_ref[2]
    r = lax.broadcasted_iota(jnp.int32, (n, n), 0)
    c = lax.broadcasted_iota(jnp.int32, (n, n), 1)
    matrix = jnp.where(((r >> 3) & 3) == ((c >> 3) & 3), 1.0, 0.0)
    depth = (c & 7).astype(F32) - spread(by_target)
    same = jnp.where((r & 7).astype(F32) - spread(by_source) == depth, 1.0, 0.0)
    inside = jnp.where(depth >= 0, 1.0, 0.0) * jnp.where(depth < spread(layers), 1.0, 0.0)
    return (matrix * same * inside).astype(BF16)


def fill_forward(forward_ref, one_ref, *refs):
    two_ref = refs[-1]
    hops = one_ref[...].reshape(NB * OVER, -1)
    out = pick(forward_ref[...], hops).astype(BF16)
    two_ref[...] = out.reshape(two_ref.shape)


def order_a(local, keys_ref, gate, up, out_ref):
    step = pl.program_id(0)
    pair = (gate, up)

    def hot_rows(size, line):
        slot = lax.broadcasted_iota(jnp.int32, (4 * size, local), 0) + 4 * size * step
        return onehot(slot.astype(F32), keys_ref[line : line + 1, :local])

    for size, start, line in ((ONE, 0, 3), (TWO, 2 * ONE, 4)):
        hot = hot_rows(size, line)
        for j, rows in enumerate(pair):
            out = pick(hot, rows[...]).astype(BF16)
            out_ref[:, start + j * size : start + (j + 1) * size] = out.reshape(4, size, -1)
    hot = hot_rows(HOP, 5)
    parts = [pick(hot, rows[...]).reshape(4, HOP, -1) for rows in pair]
    out_ref[:, 2 * CAP :] = jnp.concatenate(parts, axis=1).astype(BF16)


def take_half(place, x_ref, *refs):
    del place
    refs[-1][...] = x_ref[...]


def preact(rows, place, own_ref, other_ref, tok_ref, tok_other_ref, out_ref):
    del place
    total = None
    for x, tok in ((own_ref, tok_ref), (other_ref, tok_other_ref)):
        part = lax.dot_general(
            x[:, :rows].reshape(2 * rows, -1),
            tok[...],
            (((1,), (1,)), ((), ())),
            preferred_element_type=F32,
        )
        total = part if total is None else total + part
    out_ref[...] = total.reshape(out_ref.shape)


def compact(matrix, sources, held):
    if matrix < 2:
        one, two = sources
        for s in range(NB):
            start = s * CAP
            held[start : start + ONE] = one[s, matrix * ONE : (matrix + 1) * ONE]
            held[start + ONE : start + CAP] = two[s, matrix * TWO : (matrix + 1) * TWO]
    else:
        three, two = sources
        for s in range(NB):
            held[s * CAP : (s + 1) * CAP] = three[s]
    far = two[:, 2 * TWO :].astype(F32)[:, matrix * HOP : (matrix + 1) * HOP]
    held[NB * CAP :] = far.reshape(NB * HOP, -1).astype(BF16)


def merge(matrices, tied, key_ref, *refs):
    n = len(matrices)
    rows_a, sources = refs[:n], refs[n : n + 2]
    outs, scale_ref, helds = refs[n + 2 + tied : 2 * n + 2 + tied], refs[-n - 1], refs[-n:]

    @pl.when(pl.program_id(0) == 0)
    def _():
        for matrix, held in zip(matrices, helds):
            compact(matrix, sources, held)
        scale_ref[0] = SCALE

    hot = onehot(key_ref[:, 0:1], iota((key_ref.shape[0], NB * (CAP + HOP)), 1))
    for a, out, held in zip(rows_a, outs, helds):
        got = pick(hot, held[...])
        out[...] = ((a[...].astype(F32) + got) * 0.5).astype(BF16)


def merged_rows(matrices, key, rows_a, sources, tied=()):
    n = len(matrices)
    local, width = rows_a[0].shape
    chunk = local // 4
    block = pl.BlockSpec((chunk, width), lambda i: (i, 0))
    return pl.pallas_call(
        functools.partial(merge, matrices, len(tied)),
        grid=(4,),
        in_specs=[pl.BlockSpec((chunk, key.shape[1]), lambda i: (i, 0))]
        + [block] * n
        + [pl.BlockSpec(x.shape, lambda i: (0, 0, 0)) for x in sources]
        + [pl.BlockSpec(memory_space=pl.ANY)] * len(tied),
        out_specs=[block] * n + [SMEM],
        out_shape=[shape((local, width), BF16)] * n + [shape((1,))],
        scratch_shapes=[pltpu.VMEM((NB * (CAP + HOP), width), BF16)] * n,
        compiler_params=PARAMS,
        cost_estimate=CHEAP,
    )(key, *rows_a, *sources, *tied)


def correlate(parts, *refs):
    a_refs, b_refs, out_refs = refs[:2], refs[2:4], refs[-len(parts) :]
    tokens = a_refs[0].shape[1]

    def hidden(ref, start, size):
        g = ref[start : start + size]
        u = ref[start + size : start + 2 * size]
        return g / (1.0 + jnp.exp(-g)) * u

    for (start_a, start_b, size), out_ref in zip(parts, out_refs):
        for piece in range(2):
            a = hidden(a_refs[piece], start_a, size)
            b = hidden(b_refs[piece], start_b, size)
            sa, sb, saa, sbb, sab = (
                jnp.sum(x, axis=1, keepdims=True) for x in (a, b, a * a, b * b, a * b)
            )
            covar = sab - sa * sb / tokens
            var = (saa - sa * sa / tokens) * (sbb - sb * sb / tokens)
            out_ref[piece] = covar / jnp.sqrt(var + 1e-5)


def unorder(local, me_ref, keys_ref, corr_ref, out_ref):
    place = iota((corr_ref.shape[1], local), 0)
    hot = jnp.where(keys_ref[7:8, :local] == place, 1.0, 0.0)
    rest = corr_ref[...]
    total = jnp.zeros((8, local), F32)
    for _ in range(3):
        part = rest.astype(BF16)
        total = total + jnp.dot(part, hot.astype(BF16), preferred_element_type=F32)
        rest = rest - part.astype(F32)
    owner = lax.broadcasted_iota(jnp.int32, (8, local), 0) ^ me_ref[0]
    keep = jnp.where(keys_ref[6:7, :local] == owner.astype(F32), total, 0.0)
    out_ref[...] = jnp.sum(keep, axis=0, keepdims=True)


def call(kernel, outs, args, in_specs=None, out_specs=None, params=PARAMS, **more):
    specs = in_specs or [VMEM] * len(args)
    made = pl.pallas_call(
        kernel,
        out_shape=outs,
        in_specs=specs,
        out_specs=out_specs or [VMEM] * len(outs),
        compiler_params=params,
        cost_estimate=CHEAP,
        **more,
    )(*args)
    return made


def shape(dims, dtype=F32):
    return jax.ShapeDtypeStruct(dims, dtype)


def exchange(x):
    return lax.all_to_all(x, "mp", split_axis=0, concat_axis=0, tiled=True)


def swap_cores(x):
    return lax.ppermute(x, "dp", [(i, i ^ 1) for i in range(8)])


def along_y(x, step):
    return lax.ppermute(
        x, "dp", [(i, ((i // 2 + step) % 4) * 2 + i % 2) for i in range(8)]
    )


def pre_activations(rows, core, y, mine, other, tokens, tokens_other):
    width = tokens.shape[1]
    ntok = tokens.shape[0]

    def chunk(i, place):
        return lax.rem(place[1] + i + 1, 4)

    pre = pl.pallas_call(
        functools.partial(preact, rows),
        grid_spec=pltpu.PrefetchScalarGridSpec(
            num_scalar_prefetch=1,
            grid=(4,),
            in_specs=[
                pl.BlockSpec((2, rows, width), lambda i, p: (4 * p[0] + chunk(i, p), 0, 0)),
                pl.BlockSpec((2, rows, width), lambda i, p: (chunk(i, p), 0, 0)),
                pl.BlockSpec((ntok, width), lambda i, p: (0, 0)),
                pl.BlockSpec((ntok, width), lambda i, p: (0, 0)),
            ],
            out_specs=pl.BlockSpec((2, rows, ntok), lambda i, p: (i, 0, 0)),
        ),
        out_shape=shape((8, rows, ntok)),
        compiler_params=PARAMS,
        cost_estimate=CHEAP,
    )(jnp.stack([core, y]), mine, other, tokens, tokens_other)
    return pre, (pre[1:3] * SCALE).astype(F16), (pre[3:5] * SCALE).astype(F16)


def second_messages(pre, plus, minus, scale):
    from_prev, from_next = along_y(plus, 1), along_y(minus, 3)
    far_plus = (pre[0] * scale + from_prev[1].astype(F32)).astype(F16)
    far_minus = (pre[5] * scale + from_next[0].astype(F32)).astype(F16)
    return from_prev[0], from_next[1], far_plus, far_minus


def totals(pre, from_prev, from_next, far_plus, far_minus):
    far_prev, far_next = along_y(far_plus, 1), along_y(far_minus, 3)
    low = pre[6] + (far_prev.astype(F32) + from_next.astype(F32)) * (1.0 / SCALE)
    high = pre[7] + (far_next.astype(F32) + from_prev.astype(F32)) * (1.0 / SCALE)
    return low, high


def from_partner(x, core, rows, tied=()):
    block = (2, rows, x.shape[2])
    half = pl.pallas_call(
        take_half,
        grid_spec=pltpu.PrefetchScalarGridSpec(
            num_scalar_prefetch=1,
            grid=(4,),
            in_specs=[pl.BlockSpec(block, lambda i, p: (4 * (1 - p[0]) + i, 0, 0))]
            + [pl.BlockSpec(memory_space=pl.ANY)] * len(tied),
            out_specs=pl.BlockSpec(block, lambda i, p: (i, 0, 0)),
        ),
        out_shape=shape((8, rows, x.shape[2]), BF16),
        compiler_params=PARAMS,
        cost_estimate=CHEAP,
    )(core.reshape(1), x, *tied)
    return swap_cores(half)


def fast(tokens, gate_a, up_a, down_a, gate_b, up_b, down_b, perm):
    local, width = gate_a.shape
    ntok = tokens.shape[0]
    me = lax.axis_index("mp").astype(jnp.int32).reshape(1)
    dp = lax.axis_index("dp").astype(jnp.int32)
    core, y = dp & 1, dp >> 1
    padded = -(-local // 128) * 128
    grid = jnp.pad(
        perm.reshape(NB, local), ((0, 0), (0, padded - local)), constant_values=NB * local
    )
    tokens_other = swap_cores(tokens)

    send, slot_keys, table, bad = call(
        functools.partial(send_one, local),
        [
            shape((NB, 2 * ONE + OVER, width), BF16),
            shape((NB // 4, 2, 8, padded)),
            shape((3, NB, 128)),
            shape((1,), jnp.int32),
        ],
        (me, grid, gate_b, up_b, down_b),
        in_specs=[SMEM, VMEM] + [pl.BlockSpec(memory_space=pl.ANY)] * 3,
        out_specs=[VMEM] * 3 + [SMEM],
        scratch_shapes=[pltpu.VMEM((local, width), BF16)] * 3 + [pltpu.SemaphoreType.DMA((3,))],
        params=ALONE,
    )
    one = exchange(send)

    (keys,) = call(
        functools.partial(receive_keys, local),
        [shape((8, padded))],
        (me, grid, table),
        in_specs=[SMEM, VMEM, VMEM],
    )
    whole = pl.BlockSpec((local, width), lambda i: (0, 0))
    keys_whole = pl.BlockSpec((8, padded), lambda i: (0, 0))
    ordered = pl.pallas_call(
        functools.partial(order_a, local),
        grid=(4,),
        in_specs=[keys_whole, whole, whole],
        out_specs=pl.BlockSpec((4, SLOTS, width), lambda i: (i, 0, 0)),
        out_shape=shape((NB, SLOTS, width), BF16),
        compiler_params=PARAMS,
        cost_estimate=CHEAP,
    )(keys, gate_a, up_a)
    ordered_other = from_partner(ordered, core, SLOTS)
    two, three, forward = pl.pallas_call(
        functools.partial(send_rest, local),
        grid=(4,),
        in_specs=[
            pl.BlockSpec((1, 2, 8, padded), lambda i: (i, 0, 0, 0)),
            pl.BlockSpec((3, NB, 128), lambda i: (0, 0, 0)),
            whole,
            whole,
            whole,
        ],
        out_specs=[
            pl.BlockSpec((4, 2 * TWO + OVER, width), lambda i: (i, 0, 0)),
            pl.BlockSpec((4, CAP, width), lambda i: (i, 0, 0)),
            pl.BlockSpec((NB * OVER, NB * OVER), lambda i: (0, 0)),
        ],
        out_shape=[
            shape((NB, 2 * TWO + OVER, width), BF16),
            shape((NB, CAP, width), BF16),
            shape((NB * OVER, NB * OVER), BF16),
        ],
        compiler_params=ALONE,
        cost_estimate=CHEAP,
    )(slot_keys, table, gate_b, up_b, down_b)
    pre_a, plus_a, minus_a = pre_activations(
        SLOTS, core, y, ordered, ordered_other, tokens, tokens_other
    )

    two = pl.pallas_call(
        fill_forward,
        grid=(1,),
        in_specs=[
            pl.BlockSpec((NB * OVER, NB * OVER), lambda i: (0, 0)),
            pl.BlockSpec((NB, OVER, width), lambda i: (0, 2 * ONE // OVER, 0)),
        ]
        + [pl.BlockSpec(memory_space=pl.ANY)] * 2,
        out_specs=pl.BlockSpec((NB, OVER, width), lambda i: (0, 2 * TWO // OVER, 0)),
        out_shape=shape(two.shape, BF16),
        input_output_aliases={2: 0},
        compiler_params=ALONE,
        cost_estimate=CHEAP,
    )(forward, one, two, pre_a)
    one_other = from_partner(one, core, 2 * ONE, (two,))
    two = exchange(two)
    waiting_a = second_messages(pre_a, plus_a, minus_a, SCALE)
    pre_one, plus, minus = pre_activations(
        2 * ONE, core, y, one, one_other, tokens, tokens_other
    )
    waiting_one = second_messages(pre_one, plus, minus, SCALE)
    sums_a = totals(pre_a, *waiting_a)
    sums_one = totals(pre_one, *waiting_one)

    tied = [x[2][:8, :128].astype(F32) for x in (waiting_a, waiting_one)]
    two_other = from_partner(two, core, CAP, tied)
    three = exchange(three)
    pre_two, plus, minus = pre_activations(
        CAP, core, y, two, two_other, tokens, tokens_other
    )
    tall = keys[:, :local].T
    merged_gate, merged_up, scale = merged_rows(
        (0, 1), tall, (gate_a, up_a), (one, two), (pre_two,)
    )
    sums_two = totals(pre_two, *second_messages(pre_two, plus, minus, scale))

    (corr_one,) = call(
        functools.partial(correlate, ((0, 0, ONE),)), [shape((2, ONE, 1))], sums_a + sums_one
    )
    corr_two, corr_three = call(
        functools.partial(correlate, ((2 * ONE, 0, TWO), (2 * CAP, 2 * TWO, HOP))),
        [shape((2, TWO, 1)), shape((2, HOP, 1))],
        sums_a + sums_two,
    )
    corr = jnp.concatenate([c.reshape(-1) for c in (corr_one, corr_two, corr_three)])[None]
    for bit in (1, 2, 4):
        got = lax.ppermute(corr, "dp", [(i, i ^ bit) for i in range(8)])
        corr = jnp.concatenate([corr, got], axis=0)
    (match_corr,) = call(
        functools.partial(unorder, local), [shape((1, local))],
        (dp.reshape(1), keys, corr),
        in_specs=[SMEM, VMEM, VMEM],
    )

    merged_down, _ = merged_rows((2,), tall, (down_a,), (three, two))
    return (merged_gate, merged_up, merged_down, match_corr.reshape(-1)), bad[0]


def merge_rows(first, second):
    return ((first.astype(F32) + second.astype(F32)) * 0.5).astype(BF16)


def general(tokens, gate_a, up_a, down_a, gate_b, up_b, down_b, perm):
    me = lax.axis_index("mp")
    local = gate_a.shape[0]
    capacity = 2 * local // NB
    source = perm // local
    before = (jnp.arange(local)[:, None] < jnp.arange(local)[None, :]).astype(BF16)

    def rank_of(member):
        return jnp.dot(member.astype(BF16), before, preferred_element_type=F32).astype(jnp.int32)

    mine = (source == me).reshape(NB, local)
    hit = jnp.logical_and(
        mine[:, None, :], rank_of(mine)[:, None, :] == jnp.arange(capacity)[None, :, None]
    ).astype(jnp.int32)
    send_index = jnp.sum(hit * (perm % local).reshape(NB, 1, local), axis=2).reshape(-1)
    arrived = lax.dynamic_slice_in_dim(source, me * local, local)
    member = (jnp.arange(NB)[:, None] == arrived[None, :]).astype(jnp.int32)
    recv_index = arrived * capacity + jnp.sum(member * rank_of(member), axis=0)

    def matched(rows):
        moved = exchange(jnp.take(rows, send_index, axis=0))
        return jnp.take(moved, recv_index, axis=0)

    gate_match, up_match, down_match = matched(gate_b), matched(up_b), matched(down_b)

    def hidden(gate, up):
        g, u = (
            jnp.sum(
                lax.all_to_all(
                    lax.dot_general(
                        tokens, w, (((1,), (1,)), ((), ())), preferred_element_type=F32
                    ).reshape(8, -1, local),
                    "dp",
                    split_axis=0,
                    concat_axis=0,
                    tiled=True,
                ),
                axis=0,
            )
            for w in (gate, up)
        )
        return jax.nn.silu(g) * u

    a, b = hidden(gate_a, up_a), hidden(gate_match, up_match)
    sums = jnp.stack([jnp.sum(x, axis=0) for x in (a, b, a * a, b * b, a * b)])
    for bit in (1, 2, 4):
        sums = sums + lax.ppermute(sums, "dp", [(i, i ^ bit) for i in range(8)])
    sa, sb, saa, sbb, sab = sums
    ntok = tokens.shape[0] * 1.0
    covar = sab - sa * sb / ntok
    var = (saa - sa * sa / ntok) * (sbb - sb * sb / ntok)
    return (
        merge_rows(gate_a, gate_match),
        merge_rows(up_a, up_match),
        merge_rows(down_a, down_match),
        covar / jnp.sqrt(var + 1e-05),
    )


def local_program(*args):
    outs, bad = fast(*args)
    return lax.cond(bad > 0, lambda outs, args: general(*args), lambda outs, args: outs, outs, args)


def solution(mesh):
    return jax.shard_map(
        local_program,
        mesh=mesh,
        in_specs=(P(None, "dp"),) + (P("mp", "dp"),) * 6 + (P(),),
        out_specs=(P("mp", "dp"),) * 3 + (P("mp"),),
        check_vma=False,
    )
```

```python
import functools

import jax
import jax.numpy as jnp
from jax import lax
from jax.experimental import pallas as pl
from jax.experimental.pallas import tpu as pltpu
from jax.sharding import PartitionSpec as P

F32 = jnp.float32
BF16 = jnp.bfloat16
F16 = jnp.float16
NB = 16
CAP = 112
ONE = 64
TWO = CAP - ONE
HOP = 8
OVER = 4 * HOP
SLOTS = 2 * (CAP + HOP)
SCALE = 16.0
VMEM = pl.BlockSpec(memory_space=pltpu.VMEM)
SMEM = pl.BlockSpec(memory_space=pltpu.SMEM)
ANY = pl.BlockSpec(memory_space=pl.ANY)
CHEAP = pl.CostEstimate(flops=0, bytes_accessed=0, transcendentals=0)
ALONE = pltpu.CompilerParams(vmem_limit_bytes=58 * 2**20)
PARAMS = pltpu.CompilerParams(vmem_limit_bytes=48 * 2**20)


def iota(shape, dim):
    return lax.broadcasted_iota(jnp.int32, shape, dim).astype(F32)


def onehot(keys, ids):
    return jnp.where(keys == ids, 1.0, 0.0).astype(BF16)


def pick(hot, rows):
    return jnp.dot(hot, rows, preferred_element_type=F32)


def ranks(member):
    width = member.shape[1]
    before = (
        lax.broadcasted_iota(jnp.int32, (128, 128), 0)
        < lax.broadcasted_iota(jnp.int32, (128, 128), 1)
    )
    before = jnp.where(before, 1.0, 0.0).astype(BF16)
    carry = jnp.zeros((member.shape[0], 1), F32)
    tiles = []
    for j in range(width // 128):
        tile = member[:, j * 128 : (j + 1) * 128]
        tiles.append(jnp.dot(tile.astype(BF16), before, preferred_element_type=F32) + carry)
        carry = carry + jnp.sum(tile, axis=1, keepdims=True)
    return jnp.concatenate(tiles, axis=1)


def widened(perm_ref, wide):
    local = perm_ref.shape[1]
    wide[...] = jnp.full(wide.shape, NB * local, jnp.int32)
    wide[:, :local] = perm_ref[...]
    return wide[...]


def block_of(perm, local):
    block = jnp.zeros(perm.shape, F32)
    for k in range(1, NB + 1):
        block = block + jnp.where(perm >= k * local, 1.0, 0.0)
    return block


def tables(local, block):
    lane = iota((NB, 128), 1)
    row = iota((NB, 128), 0)
    count = jnp.zeros((NB, 128), F32)
    for s in range(NB):
        col = jnp.sum(jnp.where(block == s, 1.0, 0.0), axis=1, keepdims=True)
        count = count + jnp.where(lane == s, col, 0.0)
    layers = jnp.maximum(count - CAP, 0.0).astype(jnp.int32)
    layers = ((layers + (NB - 1)) >> 4).astype(F32)
    by_target = jnp.zeros((NB, 128), F32)
    by_source = jnp.zeros((NB, 128), F32)
    for k in range(NB):
        by_target = by_target + jnp.where(row > k, layers[k : k + 1, :], 0.0)
        by_source = by_source + jnp.where(lane > k, layers[:, k : k + 1], 0.0)
    return by_target, by_source, layers


def slot_values(keys, value, first, size):
    slot = iota((size, keys.shape[1]), 0) + first
    return [
        jnp.sum(jnp.where(keys[t : t + 1, :] == slot, value[t : t + 1, :], 0.0), axis=1, keepdims=True)
        - 1.0
        for t in range(keys.shape[0])
    ]


def send_one(
    local, me_ref, perm_ref, gate, up, down, send_ref, key_ref, table_ref, bad_ref, *scratch
):
    *held, sem, wide = scratch
    copies = [
        pltpu.make_async_copy(rows, buffer, sem.at[i])
        for i, (rows, buffer) in enumerate(zip((gate, up, down), held))
    ]
    for copy in copies:
        copy.start()
    me = me_ref[0].astype(F32)
    perm = widened(perm_ref, wide)
    width = perm.shape[1]
    block = block_of(perm, local)
    value = perm.astype(F32) - block * local + 1.0
    mine = jnp.where(block == me, 1.0, 0.0)
    by_target, by_source, layers = tables(local, block)
    table_ref[0] = by_target
    table_ref[1] = by_source
    table_ref[2] = layers
    most = jnp.maximum(
        jnp.max(jnp.sum(layers, axis=0, keepdims=True)), jnp.max(jnp.sum(layers, axis=1, keepdims=True))
    )
    bad_ref[0] = jnp.where(most > HOP, 1, 0).astype(jnp.int32)

    rank = ranks(mine)
    base = jnp.where(iota((NB, 128), 1) == me, by_target, 0.0)
    base = jnp.sum(base, axis=1, keepdims=True)
    extra = (rank - CAP).astype(jnp.int32)
    mid = (extra & (NB - 1)).astype(F32)
    layer = (extra >> 4).astype(F32)
    direct = jnp.where(mine * jnp.where(rank < CAP, 1.0, 0.0) > 0, rank, -1.0)
    detour = jnp.where(mine * jnp.where(rank < CAP, 0.0, 1.0) > 0, mid * HOP + base + layer, -1.0)
    for i in range(NB // 4):
        key_ref[i, 0, :4] = direct[4 * i : 4 * i + 4]
        key_ref[i, 1, :4] = value[4 * i : 4 * i + 4]
    hop_slot = iota((NB * HOP, width), 0)
    hop = jnp.zeros((NB * HOP, width), F32)
    ids = iota((4 * ONE, local), 1)
    for i in range(NB // 4):
        group = slice(4 * i, 4 * i + 4)
        cols = slot_values(direct[group], value[group], 0, ONE)
        hot = onehot(jnp.concatenate(cols, axis=0), ids)
        if i == 0:
            for copy in copies:
                copy.wait()
        for j, rows in enumerate(held[:2]):
            out = pick(hot, rows[...]).astype(BF16)
            send_ref[group, j * ONE : (j + 1) * ONE] = out.reshape(4, ONE, -1)
        for t in range(4 * i, 4 * i + 4):
            hop = hop + jnp.where(detour[t : t + 1, :] == hop_slot, value[t : t + 1, :], 0.0)
    hop = jnp.sum(hop, axis=1, keepdims=True) - 1.0
    hot = onehot(hop, iota((NB * HOP, local), 1))
    parts = [pick(hot, rows[...]).reshape(NB, HOP, -1) for rows in held]
    parts.append(jnp.zeros_like(parts[0]))
    send_ref[:, 2 * ONE :] = jnp.concatenate(parts, axis=1).astype(BF16)


def receive_keys(local, me_ref, perm_ref, table_ref, keys_ref, wide):
    me = me_ref[0].astype(F32)
    block = block_of(widened(perm_ref, wide), local)
    width = block.shape[1]
    source = jnp.sum(jnp.where(iota(block.shape, 0) == me, block, 0.0), axis=0, keepdims=True)
    member = jnp.where(source == iota((NB, width), 0), 1.0, 0.0)
    rank = jnp.sum(member * ranks(member), axis=0, keepdims=True)
    mine = jnp.where(iota((NB, 128), 0) == me, table_ref[1], 0.0)
    mine = jnp.sum(mine, axis=0, keepdims=True)
    square = jnp.where(iota((NB, 128), 0) == iota((NB, 128), 1), mine, 0.0)
    base = jnp.sum(square, axis=1, keepdims=True)
    base = jnp.sum(member * base, axis=0, keepdims=True)
    extra = (rank - CAP).astype(jnp.int32)
    mid = (extra & (NB - 1)).astype(F32)
    over = base + (extra >> 4).astype(F32)
    first = rank < ONE
    straight = rank < CAP
    k1 = jnp.where(first, source * ONE + rank, -1.0)
    k2 = jnp.where(first, -1.0, jnp.where(straight, source * TWO + (rank - ONE), -1.0))
    ko = jnp.where(straight, -1.0, mid * HOP + over)
    keys_ref[0:1] = jnp.where(straight, source * CAP + rank, NB * CAP + mid * HOP + over)
    keys_ref[1:3] = jnp.zeros((2, width), F32)
    keys_ref[3:4] = k1
    keys_ref[4:5] = k2
    keys_ref[5:6] = ko
    holder = jnp.where(straight, source, mid).astype(jnp.int32)
    piece = (holder & 1).astype(F32)
    device = ((holder >> 1) & 3) * 2 + (holder >> 3)
    keys_ref[6:7] = device.astype(F32)
    keys_ref[7:8] = jnp.where(
        first,
        piece * ONE + rank,
        jnp.where(straight, 2 * ONE + piece * TWO + rank - ONE, 2 * CAP + piece * HOP + over),
    )


def send_two(local, key_ref, table_ref, gate, up, two_ref, forward_ref):
    ids = iota((4 * TWO, local), 1)
    for i in range(NB // 4):
        cols = slot_values(key_ref[i, 0, :4], key_ref[i, 1, :4], ONE, TWO)
        hot = onehot(jnp.concatenate(cols, axis=0), ids)
        for j, rows in enumerate((gate, up)):
            out = pick(hot, rows[...]).astype(BF16)
            two_ref[4 * i : 4 * i + 4, j * TWO : (j + 1) * TWO] = out.reshape(4, TWO, -1)
    two_ref[:, 2 * TWO :] = jnp.zeros((NB, OVER, gate.shape[1]), BF16)
    forward_ref[...] = forwarding(table_ref)


def send_three(local, key_ref, down, *refs):
    three_ref = refs[-1]
    ids = iota((4 * CAP, local), 1)
    for i in range(NB // 4):
        cols = slot_values(key_ref[i, 0, :4], key_ref[i, 1, :4], 0, CAP)
        out = pick(onehot(jnp.concatenate(cols, axis=0), ids), down[...]).astype(BF16)
        three_ref[4 * i : 4 * i + 4] = out.reshape(4, CAP, -1)


def forwarding(table_ref):
    n = NB * OVER
    tall = lax.broadcasted_iota(jnp.int32, (n, NB), 0) >> 5
    tall = onehot(tall, lax.broadcasted_iota(jnp.int32, (n, NB), 1))
    wide = lax.broadcasted_iota(jnp.int32, (128, n), 1) >> 5
    wide = onehot(wide, lax.broadcasted_iota(jnp.int32, (128, n), 0))

    def spread(x):
        part = jnp.dot(tall, x.astype(BF16), preferred_element_type=F32)
        return jnp.dot(part.astype(BF16), wide, preferred_element_type=F32)

    by_target, by_source, layers = table_ref[0], table_ref[1], table_ref[2]
    r = lax.broadcasted_iota(jnp.int32, (n, n), 0)
    c = lax.broadcasted_iota(jnp.int32, (n, n), 1)
    matrix = jnp.where(((r >> 3) & 3) == ((c >> 3) & 3), 1.0, 0.0)
    depth = (c & 7).astype(F32) - spread(by_target)
    same = jnp.where((r & 7).astype(F32) - spread(by_source) == depth, 1.0, 0.0)
    inside = jnp.where(depth >= 0, 1.0, 0.0) * jnp.where(depth < spread(layers), 1.0, 0.0)
    return (matrix * same * inside).astype(BF16)


def fill_forward(forward_ref, one_ref, *refs):
    two_ref, zero_ref = refs[-2:]
    hops = one_ref[...].reshape(NB * OVER, -1)
    out = pick(forward_ref[...], hops).astype(BF16)
    two_ref[...] = out.reshape(two_ref.shape)
    zero_ref[0] = 0


def order_a(local, keys_ref, gate, up, out_ref):
    pair = (gate, up)
    for size, start, line in ((ONE, 0, 3), (TWO, 2 * ONE, 4)):
        key = keys_ref[line : line + 1, :local]
        for i in range(NB // 4):
            hot = onehot(iota((4 * size, local), 0) + 4 * size * i, key)
            for j, rows in enumerate(pair):
                out = pick(hot, rows[...]).astype(BF16)
                out_ref[4 * i : 4 * i + 4, start + j * size : start + (j + 1) * size] = out.reshape(
                    4, size, -1
                )
    hot = onehot(iota((NB * HOP, local), 0), keys_ref[5:6, :local])
    parts = [pick(hot, rows[...]).reshape(NB, HOP, -1) for rows in pair]
    out_ref[:, 2 * CAP :] = jnp.concatenate(parts, axis=1).astype(BF16)


def constant(value, *refs):
    refs[-1][0] = value


def preact(rows, place, own_ref, other_ref, tok_ref, tok_other_ref, out_ref):
    del place
    total = None
    for x, tok in ((own_ref, tok_ref), (other_ref, tok_other_ref)):
        part = lax.dot_general(
            x[:, :rows].reshape(2 * rows, -1),
            tok[...],
            (((1,), (1,)), ((), ())),
            preferred_element_type=F32,
        )
        total = part if total is None else total + part
    out_ref[...] = total.reshape(out_ref.shape)


def compact(matrix, sources, held):
    if matrix < 2:
        one, two = sources
        for s in range(NB):
            start = s * CAP
            held[start : start + ONE] = one[s, matrix * ONE : (matrix + 1) * ONE]
            held[start + ONE : start + CAP] = two[s, matrix * TWO : (matrix + 1) * TWO]
    else:
        three, two = sources
        for s in range(NB):
            held[s * CAP : (s + 1) * CAP] = three[s]
    far = two[:, 2 * TWO :].astype(F32)[:, matrix * HOP : (matrix + 1) * HOP]
    held[NB * CAP :] = far.reshape(NB * HOP, -1).astype(BF16)


def merge(matrices, tied, key_ref, *refs):
    n = len(matrices)
    rows_a, sources = refs[:n], refs[n : n + 2]
    outs, scale_ref, helds = refs[n + 2 + tied : 2 * n + 2 + tied], refs[-n - 1], refs[-n:]

    @pl.when(pl.program_id(0) == 0)
    def _():
        for matrix, held in zip(matrices, helds):
            compact(matrix, sources, held)
        scale_ref[0] = SCALE

    hot = onehot(key_ref[:, 0:1], iota((key_ref.shape[0], NB * (CAP + HOP)), 1))
    for a, out, held in zip(rows_a, outs, helds):
        got = pick(hot, held[...])
        out[...] = ((a[...].astype(F32) + got) * 0.5).astype(BF16)


def merged_rows(matrices, key, rows_a, sources, tied=()):
    n = len(matrices)
    local, width = rows_a[0].shape
    chunk = local // 4
    block = pl.BlockSpec((chunk, width), lambda i: (i, 0))
    return pl.pallas_call(
        functools.partial(merge, matrices, len(tied)),
        grid=(4,),
        in_specs=[pl.BlockSpec((chunk, key.shape[1]), lambda i: (i, 0))]
        + [block] * n
        + [pl.BlockSpec(x.shape, lambda i: (0, 0, 0)) for x in sources]
        + [ANY] * len(tied),
        out_specs=[block] * n + [SMEM],
        out_shape=[shape((local, width), BF16)] * n + [shape((1,))],
        scratch_shapes=[pltpu.VMEM((NB * (CAP + HOP), width), BF16)] * n,
        compiler_params=PARAMS,
        cost_estimate=CHEAP,
    )(key, *rows_a, *sources, *tied)


def correlate(parts, *refs):
    a_refs, b_refs, out_refs = refs[:2], refs[2:4], refs[-len(parts) :]
    tokens = a_refs[0].shape[1]

    def hidden(ref, start, size):
        g = ref[start : start + size]
        u = ref[start + size : start + 2 * size]
        return g / (1.0 + jnp.exp(-g)) * u

    for (start_a, start_b, size), out_ref in zip(parts, out_refs):
        for piece in range(2):
            a = hidden(a_refs[piece], start_a, size)
            b = hidden(b_refs[piece], start_b, size)
            sa, sb, saa, sbb, sab = (
                jnp.sum(x, axis=1, keepdims=True) for x in (a, b, a * a, b * b, a * b)
            )
            covar = sab - sa * sb / tokens
            var = (saa - sa * sa / tokens) * (sbb - sb * sb / tokens)
            out_ref[piece] = covar / jnp.sqrt(var + 1e-5)


def unorder(local, me_ref, keys_ref, corr_ref, out_ref):
    place = iota((corr_ref.shape[1], local), 0)
    hot = jnp.where(keys_ref[7:8, :local] == place, 1.0, 0.0)
    rest = corr_ref[...]
    total = jnp.zeros((8, local), F32)
    for _ in range(3):
        part = rest.astype(BF16)
        total = total + jnp.dot(part, hot.astype(BF16), preferred_element_type=F32)
        rest = rest - part.astype(F32)
    owner = lax.broadcasted_iota(jnp.int32, (8, local), 0) ^ me_ref[0]
    keep = jnp.where(keys_ref[6:7, :local] == owner.astype(F32), total, 0.0)
    out_ref[...] = jnp.sum(keep, axis=0, keepdims=True)


def call(kernel, outs, args, in_specs=None, out_specs=None, params=PARAMS, **more):
    specs = in_specs or [VMEM] * len(args)
    made = pl.pallas_call(
        kernel,
        out_shape=outs,
        in_specs=specs,
        out_specs=out_specs or [VMEM] * len(outs),
        compiler_params=params,
        cost_estimate=CHEAP,
        **more,
    )(*args)
    return made


def shape(dims, dtype=F32):
    return jax.ShapeDtypeStruct(dims, dtype)


def some(x):
    return x.reshape(-1, x.shape[-1])[:8, :128].astype(F32)


def tie(value, dtype, after):
    return call(
        functools.partial(constant, value),
        [shape((1,), dtype)],
        after,
        in_specs=[ANY] * len(after),
        out_specs=[SMEM],
    )


def exchange(x):
    return lax.all_to_all(x, "mp", split_axis=0, concat_axis=0, tiled=True)


def swap_cores(x):
    return lax.ppermute(x, "dp", [(i, i ^ 1) for i in range(8)])


def along_y(x, step):
    return lax.ppermute(
        x, "dp", [(i, ((i // 2 + step) % 4) * 2 + i % 2) for i in range(8)]
    )


def pre_activations(rows, core, y, mine, other, tokens, tokens_other):
    width = tokens.shape[1]
    ntok = tokens.shape[0]

    def chunk(i, place):
        return lax.rem(place[1] + i + 1, 4)

    pre = pl.pallas_call(
        functools.partial(preact, rows),
        grid_spec=pltpu.PrefetchScalarGridSpec(
            num_scalar_prefetch=1,
            grid=(4,),
            in_specs=[
                pl.BlockSpec((2, rows, width), lambda i, p: (4 * p[0] + chunk(i, p), 0, 0)),
                pl.BlockSpec((2, rows, width), lambda i, p: (chunk(i, p), 0, 0)),
                pl.BlockSpec((ntok, width), lambda i, p: (0, 0)),
                pl.BlockSpec((ntok, width), lambda i, p: (0, 0)),
            ],
            out_specs=pl.BlockSpec((2, rows, ntok), lambda i, p: (i, 0, 0)),
        ),
        out_shape=shape((8, rows, ntok)),
        compiler_params=PARAMS,
        cost_estimate=CHEAP,
    )(jnp.stack([core, y]), mine, other, tokens, tokens_other)
    return pre, (pre[1:3] * SCALE).astype(F16), (pre[3:5] * SCALE).astype(F16)


def second_messages(pre, plus, minus, scale):
    from_prev, from_next = along_y(plus, 1), along_y(minus, 3)
    far_plus = (pre[0] * scale + from_prev[1].astype(F32)).astype(F16)
    far_minus = (pre[5] * scale + from_next[0].astype(F32)).astype(F16)
    return from_prev[0], from_next[1], far_plus, far_minus


def totals(pre, from_prev, from_next, far_plus, far_minus):
    far_prev, far_next = along_y(far_plus, 1), along_y(far_minus, 3)
    low = pre[6] + (far_prev.astype(F32) + from_next.astype(F32)) * (1.0 / SCALE)
    high = pre[7] + (far_next.astype(F32) + from_prev.astype(F32)) * (1.0 / SCALE)
    return low, high


def from_partner(x, core, rows, zero=0):
    half = lax.dynamic_slice(x, (8 * (1 - core) + zero, 0, 0), (8, rows, x.shape[2]))
    return swap_cores(half)


def fast(tokens, gate_a, up_a, down_a, gate_b, up_b, down_b, perm):
    local, width = gate_a.shape
    ntok = tokens.shape[0]
    me = lax.axis_index("mp").astype(jnp.int32).reshape(1)
    dp = lax.axis_index("dp").astype(jnp.int32)
    core, y = dp & 1, dp >> 1
    padded = -(-local // 128) * 128
    grid = perm.reshape(NB, local)
    place = pltpu.VMEM((NB, padded), jnp.int32)
    tokens_other = swap_cores(tokens)

    send, slot_keys, table, bad = call(
        functools.partial(send_one, local),
        [
            shape((NB, 2 * ONE + OVER, width), BF16),
            shape((NB // 4, 2, 8, padded)),
            shape((3, NB, 128)),
            shape((1,), jnp.int32),
        ],
        (me, grid, gate_b, up_b, down_b),
        in_specs=[SMEM, VMEM] + [ANY] * 3,
        out_specs=[VMEM] * 3 + [SMEM],
        scratch_shapes=[pltpu.VMEM((local, width), BF16)] * 3 + [pltpu.SemaphoreType.DMA((3,)), place],
        params=ALONE,
    )
    one = exchange(send)

    (keys,) = call(
        functools.partial(receive_keys, local),
        [shape((8, padded))],
        (me, grid, table),
        in_specs=[SMEM, VMEM, VMEM],
        scratch_shapes=[place],
    )
    (ordered,) = call(
        functools.partial(order_a, local),
        [shape((NB, SLOTS, width), BF16)],
        (keys, gate_a, up_a),
    )
    ordered_other = from_partner(ordered, core, SLOTS)
    two, forward = call(
        functools.partial(send_two, local),
        [shape((NB, 2 * TWO + OVER, width), BF16), shape((NB * OVER, NB * OVER), BF16)],
        (slot_keys, table, gate_b, up_b),
        params=ALONE,
    )
    pre_a, plus_a, minus_a = pre_activations(
        SLOTS, core, y, ordered, ordered_other, tokens, tokens_other
    )

    ready = some(plus_a)
    two, zero = pl.pallas_call(
        fill_forward,
        grid=(1,),
        in_specs=[
            pl.BlockSpec((NB * OVER, NB * OVER), lambda i: (0, 0)),
            pl.BlockSpec((NB, OVER, width), lambda i: (0, 2 * ONE // OVER, 0)),
        ]
        + [ANY] * 2,
        out_specs=[pl.BlockSpec((NB, OVER, width), lambda i: (0, 2 * TWO // OVER, 0)), SMEM],
        out_shape=[shape(two.shape, BF16), shape((1,), jnp.int32)],
        input_output_aliases={2: 0},
        compiler_params=ALONE,
        cost_estimate=CHEAP,
    )(forward, one, two, ready)
    sent_two = two
    two = exchange(two)
    one_other = from_partner(one, core, 2 * ONE, zero[0])
    pre_one, plus, minus = pre_activations(
        2 * ONE, core, y, one, one_other, tokens, tokens_other
    )
    (three,) = call(
        functools.partial(send_three, local),
        [shape((NB, CAP, width), BF16)],
        (slot_keys, down_b, some(sent_two)),
        in_specs=[VMEM, VMEM, ANY],
        params=ALONE,
    )
    (scale,) = tie(SCALE, F32, (some(plus), some(three)))
    waiting_a = second_messages(pre_a, plus_a, minus_a, scale)
    waiting_one = second_messages(pre_one, plus, minus, SCALE)
    sums_a = totals(pre_a, *waiting_a)
    sums_one = totals(pre_one, *waiting_one)

    (zero,) = tie(0, jnp.int32, (some(waiting_a[2]), some(waiting_one[2])))
    two_other = from_partner(two, core, CAP, zero[0])
    three = exchange(three)
    pre_two, plus, minus = pre_activations(
        CAP, core, y, two, two_other, tokens, tokens_other
    )
    tall = keys[:, :local].T
    merged_gate, scale = merged_rows((0,), tall, (gate_a,), (one, two), (pre_two,))
    waiting_two = second_messages(pre_two, plus, minus, scale)
    ready = some(waiting_two[2])
    merged_up, _ = merged_rows((1,), tall, (up_a,), (one, two), (ready,))
    sums_two = totals(pre_two, *waiting_two)

    (corr_one,) = call(
        functools.partial(correlate, ((0, 0, ONE),)), [shape((2, ONE, 1))], sums_a + sums_one
    )
    corr_two, corr_three = call(
        functools.partial(correlate, ((2 * ONE, 0, TWO), (2 * CAP, 2 * TWO, HOP))),
        [shape((2, TWO, 1)), shape((2, HOP, 1))],
        sums_a + sums_two + (merged_up,),
        in_specs=[VMEM] * 4 + [ANY],
    )
    corr = jnp.concatenate([c.reshape(-1) for c in (corr_one, corr_two, corr_three)])[None]
    for bit in (1, 2, 4):
        got = lax.ppermute(corr, "dp", [(i, i ^ bit) for i in range(8)])
        corr = jnp.concatenate([corr, got], axis=0)
    (match_corr,) = call(
        functools.partial(unorder, local), [shape((1, local))],
        (dp.reshape(1), keys, corr),
        in_specs=[SMEM, VMEM, VMEM],
    )

    merged_down, _ = merged_rows((2,), tall, (down_a,), (three, two))
    return (merged_gate, merged_up, merged_down, match_corr.reshape(-1)), bad[0]


def merge_rows(first, second):
    return ((first.astype(F32) + second.astype(F32)) * 0.5).astype(BF16)


def general(tokens, gate_a, up_a, down_a, gate_b, up_b, down_b, perm):
    me = lax.axis_index("mp")
    local = gate_a.shape[0]
    capacity = 2 * local // NB
    source = perm // local
    before = (jnp.arange(local)[:, None] < jnp.arange(local)[None, :]).astype(BF16)

    def rank_of(member):
        return jnp.dot(member.astype(BF16), before, preferred_element_type=F32).astype(jnp.int32)

    mine = (source == me).reshape(NB, local)
    hit = jnp.logical_and(
        mine[:, None, :], rank_of(mine)[:, None, :] == jnp.arange(capacity)[None, :, None]
    ).astype(jnp.int32)
    send_index = jnp.sum(hit * (perm % local).reshape(NB, 1, local), axis=2).reshape(-1)
    arrived = lax.dynamic_slice_in_dim(source, me * local, local)
    member = (jnp.arange(NB)[:, None] == arrived[None, :]).astype(jnp.int32)
    recv_index = arrived * capacity + jnp.sum(member * rank_of(member), axis=0)

    def matched(rows):
        moved = exchange(jnp.take(rows, send_index, axis=0))
        return jnp.take(moved, recv_index, axis=0)

    gate_match, up_match, down_match = matched(gate_b), matched(up_b), matched(down_b)

    def hidden(gate, up):
        g, u = (
            jnp.sum(
                lax.all_to_all(
                    lax.dot_general(
                        tokens, w, (((1,), (1,)), ((), ())), preferred_element_type=F32
                    ).reshape(8, -1, local),
                    "dp",
                    split_axis=0,
                    concat_axis=0,
                    tiled=True,
                ),
                axis=0,
            )
            for w in (gate, up)
        )
        return jax.nn.silu(g) * u

    a, b = hidden(gate_a, up_a), hidden(gate_match, up_match)
    sums = jnp.stack([jnp.sum(x, axis=0) for x in (a, b, a * a, b * b, a * b)])
    for bit in (1, 2, 4):
        sums = sums + lax.ppermute(sums, "dp", [(i, i ^ bit) for i in range(8)])
    sa, sb, saa, sbb, sab = sums
    ntok = tokens.shape[0] * 1.0
    covar = sab - sa * sb / ntok
    var = (saa - sa * sa / ntok) * (sbb - sb * sb / ntok)
    return (
        merge_rows(gate_a, gate_match),
        merge_rows(up_a, up_match),
        merge_rows(down_a, down_match),
        covar / jnp.sqrt(var + 1e-05),
    )


def local_program(*args):
    outs, bad = fast(*args)
    return lax.cond(bad > 0, lambda outs, args: general(*args), lambda outs, args: outs, outs, args)


def solution(mesh):
    return jax.shard_map(
        local_program,
        mesh=mesh,
        in_specs=(P(None, "dp"),) + (P("mp", "dp"),) * 6 + (P(),),
        out_specs=(P("mp", "dp"),) * 3 + (P("mp"),),
        check_vma=False,
    )
```

```python
import functools

import jax
import jax.numpy as jnp
from jax import lax
from jax.experimental import pallas as pl
from jax.experimental.pallas import tpu as pltpu
from jax.sharding import PartitionSpec as P

F32 = jnp.float32
BF16 = jnp.bfloat16
F16 = jnp.float16
NB = 16
CAP = 112
ONE = 64
TWO = CAP - ONE
HOP = 8
OVER = 4 * HOP
SLOTS = 2 * (CAP + HOP)
SCALE = 16.0
VMEM = pl.BlockSpec(memory_space=pltpu.VMEM)
SMEM = pl.BlockSpec(memory_space=pltpu.SMEM)
ANY = pl.BlockSpec(memory_space=pl.ANY)
CHEAP = pl.CostEstimate(flops=0, bytes_accessed=0, transcendentals=0)
ALONE = pltpu.CompilerParams(vmem_limit_bytes=58 * 2**20)
PARAMS = pltpu.CompilerParams(vmem_limit_bytes=24 * 2**20)


def iota(shape, dim):
    return lax.broadcasted_iota(jnp.int32, shape, dim).astype(F32)


def onehot(keys, ids):
    return jnp.where(keys == ids, 1.0, 0.0).astype(BF16)


def pick(hot, rows):
    return jnp.dot(hot, rows, preferred_element_type=F32)


def ranks(member):
    width = member.shape[1]
    before = (
        lax.broadcasted_iota(jnp.int32, (128, 128), 0)
        < lax.broadcasted_iota(jnp.int32, (128, 128), 1)
    )
    before = jnp.where(before, 1.0, 0.0).astype(BF16)
    carry = jnp.zeros((member.shape[0], 1), F32)
    tiles = []
    for j in range(width // 128):
        tile = member[:, j * 128 : (j + 1) * 128]
        tiles.append(jnp.dot(tile.astype(BF16), before, preferred_element_type=F32) + carry)
        carry = carry + jnp.sum(tile, axis=1, keepdims=True)
    return jnp.concatenate(tiles, axis=1)


def block_of(perm, local):
    block = jnp.zeros(perm.shape, F32)
    for k in range(1, NB + 1):
        block = block + jnp.where(perm >= k * local, 1.0, 0.0)
    return block


def tables(local, block):
    lane = iota((NB, 128), 1)
    row = iota((NB, 128), 0)
    count = jnp.zeros((NB, 128), F32)
    for s in range(NB):
        col = jnp.sum(jnp.where(block == s, 1.0, 0.0), axis=1, keepdims=True)
        count = count + jnp.where(lane == s, col, 0.0)
    layers = jnp.maximum(count - CAP, 0.0).astype(jnp.int32)
    layers = ((layers + (NB - 1)) >> 4).astype(F32)
    by_target = jnp.zeros((NB, 128), F32)
    by_source = jnp.zeros((NB, 128), F32)
    for k in range(NB):
        by_target = by_target + jnp.where(row > k, layers[k : k + 1, :], 0.0)
        by_source = by_source + jnp.where(lane > k, layers[:, k : k + 1], 0.0)
    return by_target, by_source, layers


def slot_values(keys, value, first, size):
    slot = iota((size, keys.shape[1]), 0) + first
    return [
        jnp.sum(jnp.where(keys[t : t + 1, :] == slot, value[t : t + 1, :], 0.0), axis=1, keepdims=True)
        - 1.0
        for t in range(keys.shape[0])
    ]


def send_one(
    local, me_ref, perm_ref, gate, up, down, send_ref, key_ref, table_ref, bad_ref, *scratch
):
    *held, sem = scratch
    copies = [
        pltpu.make_async_copy(rows, buffer, sem.at[i])
        for i, (rows, buffer) in enumerate(zip((gate, up, down), held))
    ]
    for copy in copies:
        copy.start()
    me = me_ref[0].astype(F32)
    perm = perm_ref[...]
    width = perm.shape[1]
    block = block_of(perm, local)
    value = perm.astype(F32) - block * local + 1.0
    mine = jnp.where(block == me, 1.0, 0.0)
    by_target, by_source, layers = tables(local, block)
    table_ref[0] = by_target
    table_ref[1] = by_source
    table_ref[2] = layers
    most = jnp.maximum(
        jnp.max(jnp.sum(layers, axis=0, keepdims=True)), jnp.max(jnp.sum(layers, axis=1, keepdims=True))
    )
    bad_ref[0] = jnp.where(most > HOP, 1, 0).astype(jnp.int32)

    rank = ranks(mine)
    base = jnp.where(iota((NB, 128), 1) == me, by_target, 0.0)
    base = jnp.sum(base, axis=1, keepdims=True)
    extra = (rank - CAP).astype(jnp.int32)
    mid = (extra & (NB - 1)).astype(F32)
    layer = (extra >> 4).astype(F32)
    direct = jnp.where(mine * jnp.where(rank < CAP, 1.0, 0.0) > 0, rank, -1.0)
    detour = jnp.where(mine * jnp.where(rank < CAP, 0.0, 1.0) > 0, mid * HOP + base + layer, -1.0)
    for i in range(NB // 4):
        key_ref[i, 0, :4] = direct[4 * i : 4 * i + 4]
        key_ref[i, 1, :4] = value[4 * i : 4 * i + 4]
    cols = slot_values(direct, value, 0, ONE)
    hop_slot = iota((NB * HOP, width), 0)
    hop = jnp.zeros((NB * HOP, width), F32)
    for t in range(NB):
        hop = hop + jnp.where(detour[t : t + 1, :] == hop_slot, value[t : t + 1, :], 0.0)
    hop = jnp.sum(hop, axis=1, keepdims=True) - 1.0

    for copy in copies:
        copy.wait()
    ids = iota((4 * ONE, local), 1)
    for i in range(NB // 4):
        hot = onehot(jnp.concatenate(cols[4 * i : 4 * i + 4], axis=0), ids)
        for j, rows in enumerate(held[:2]):
            out = pick(hot, rows[...]).astype(BF16)
            send_ref[4 * i : 4 * i + 4, j * ONE : (j + 1) * ONE] = out.reshape(4, ONE, -1)
    hot = onehot(hop, iota((NB * HOP, local), 1))
    parts = [pick(hot, rows[...]).reshape(NB, HOP, -1) for rows in held]
    parts.append(jnp.zeros_like(parts[0]))
    send_ref[:, 2 * ONE :] = jnp.concatenate(parts, axis=1).astype(BF16)


def receive_keys(local, me_ref, perm_ref, table_ref, keys_ref):
    me = me_ref[0].astype(F32)
    block = block_of(perm_ref[...], local)
    width = block.shape[1]
    source = jnp.sum(jnp.where(iota(block.shape, 0) == me, block, 0.0), axis=0, keepdims=True)
    member = jnp.where(source == iota((NB, width), 0), 1.0, 0.0)
    rank = jnp.sum(member * ranks(member), axis=0, keepdims=True)
    mine = jnp.where(iota((NB, 128), 0) == me, table_ref[1], 0.0)
    mine = jnp.sum(mine, axis=0, keepdims=True)
    square = jnp.where(iota((NB, 128), 0) == iota((NB, 128), 1), mine, 0.0)
    base = jnp.sum(square, axis=1, keepdims=True)
    base = jnp.sum(member * base, axis=0, keepdims=True)
    extra = (rank - CAP).astype(jnp.int32)
    mid = (extra & (NB - 1)).astype(F32)
    over = base + (extra >> 4).astype(F32)
    first = rank < ONE
    straight = rank < CAP
    k1 = jnp.where(first, source * ONE + rank, -1.0)
    k2 = jnp.where(first, -1.0, jnp.where(straight, source * TWO + (rank - ONE), -1.0))
    ko = jnp.where(straight, -1.0, mid * HOP + over)
    keys_ref[0:1] = jnp.where(straight, source * CAP + rank, NB * CAP + mid * HOP + over)
    keys_ref[1:3] = jnp.zeros((2, width), F32)
    keys_ref[3:4] = k1
    keys_ref[4:5] = k2
    keys_ref[5:6] = ko
    holder = jnp.where(straight, source, mid).astype(jnp.int32)
    piece = (holder & 1).astype(F32)
    device = ((holder >> 1) & 3) * 2 + (holder >> 3)
    keys_ref[6:7] = device.astype(F32)
    keys_ref[7:8] = jnp.where(
        first,
        piece * ONE + rank,
        jnp.where(straight, 2 * ONE + piece * TWO + rank - ONE, 2 * CAP + piece * HOP + over),
    )


def send_two(local, key_ref, table_ref, gate, up, two_ref, forward_ref):
    ids = iota((4 * TWO, local), 1)
    for i in range(NB // 4):
        cols = slot_values(key_ref[i, 0, :4], key_ref[i, 1, :4], ONE, TWO)
        hot = onehot(jnp.concatenate(cols, axis=0), ids)
        for j, rows in enumerate((gate, up)):
            out = pick(hot, rows[...]).astype(BF16)
            two_ref[4 * i : 4 * i + 4, j * TWO : (j + 1) * TWO] = out.reshape(4, TWO, -1)
    two_ref[:, 2 * TWO :] = jnp.zeros((NB, OVER, gate.shape[1]), BF16)
    forward_ref[...] = forwarding(table_ref)


def send_three(local, key_ref, down, *refs):
    three_ref = refs[-1]
    ids = iota((4 * CAP, local), 1)
    for i in range(NB // 4):
        cols = slot_values(key_ref[i, 0, :4], key_ref[i, 1, :4], 0, CAP)
        out = pick(onehot(jnp.concatenate(cols, axis=0), ids), down[...]).astype(BF16)
        three_ref[4 * i : 4 * i + 4] = out.reshape(4, CAP, -1)


def forwarding(table_ref):
    n = NB * OVER
    tall = lax.broadcasted_iota(jnp.int32, (n, NB), 0) >> 5
    tall = onehot(tall, lax.broadcasted_iota(jnp.int32, (n, NB), 1))
    wide = lax.broadcasted_iota(jnp.int32, (128, n), 1) >> 5
    wide = onehot(wide, lax.broadcasted_iota(jnp.int32, (128, n), 0))

    def spread(x):
        part = jnp.dot(tall, x.astype(BF16), preferred_element_type=F32)
        return jnp.dot(part.astype(BF16), wide, preferred_element_type=F32)

    by_target, by_source, layers = table_ref[0], table_ref[1], table_ref[2]
    r = lax.broadcasted_iota(jnp.int32, (n, n), 0)
    c = lax.broadcasted_iota(jnp.int32, (n, n), 1)
    matrix = jnp.where(((r >> 3) & 3) == ((c >> 3) & 3), 1.0, 0.0)
    depth = (c & 7).astype(F32) - spread(by_target)
    same = jnp.where((r & 7).astype(F32) - spread(by_source) == depth, 1.0, 0.0)
    inside = jnp.where(depth >= 0, 1.0, 0.0) * jnp.where(depth < spread(layers), 1.0, 0.0)
    return (matrix * same * inside).astype(BF16)


def fill_forward(forward_ref, one_ref, *refs):
    two_ref, zero_ref = refs[-2:]
    hops = one_ref[...].reshape(NB * OVER, -1)
    out = pick(forward_ref[...], hops).astype(BF16)
    two_ref[...] = out.reshape(two_ref.shape)
    zero_ref[0] = 0


def order_a(local, keys_ref, gate, up, out_ref):
    pair = (gate, up)
    for size, start, line in ((ONE, 0, 3), (TWO, 2 * ONE, 4)):
        key = keys_ref[line : line + 1, :local]
        for i in range(NB // 4):
            hot = onehot(iota((4 * size, local), 0) + 4 * size * i, key)
            for j, rows in enumerate(pair):
                out = pick(hot, rows[...]).astype(BF16)
                out_ref[4 * i : 4 * i + 4, start + j * size : start + (j + 1) * size] = out.reshape(
                    4, size, -1
                )
    hot = onehot(iota((NB * HOP, local), 0), keys_ref[5:6, :local])
    parts = [pick(hot, rows[...]).reshape(NB, HOP, -1) for rows in pair]
    out_ref[:, 2 * CAP :] = jnp.concatenate(parts, axis=1).astype(BF16)


def constant(value, *refs):
    refs[-1][0] = value


def preact(rows, place, own_ref, other_ref, tok_ref, tok_other_ref, out_ref):
    del place
    total = None
    for x, tok in ((own_ref, tok_ref), (other_ref, tok_other_ref)):
        part = lax.dot_general(
            x[:, :rows].reshape(2 * rows, -1),
            tok[...],
            (((1,), (1,)), ((), ())),
            preferred_element_type=F32,
        )
        total = part if total is None else total + part
    out_ref[...] = total.reshape(out_ref.shape)


def compact(matrix, sources, held):
    *near, far = sources
    for s in range(NB):
        start = s * CAP
        for x in near:
            size = x.shape[1]
            held[start : start + size] = x[s]
            start += size
    far = far[...].astype(F32)[:, matrix * HOP : (matrix + 1) * HOP]
    held[NB * CAP :] = far.reshape(NB * HOP, -1).astype(BF16)


def merge(matrix, key_ref, a_ref, *refs):
    out_ref, scale_ref, held = refs[-3:]
    sources = refs[: 3 if matrix < 2 else 2]

    @pl.when(pl.program_id(0) == 0)
    def _():
        compact(matrix, sources, held)
        scale_ref[0] = SCALE

    hot = onehot(key_ref[:, 0:1], iota((key_ref.shape[0], NB * (CAP + HOP)), 1))
    out_ref[...] = ((a_ref[...].astype(F32) + pick(hot, held[...])) * 0.5).astype(BF16)


def merged_rows(matrix, key, a, near, two, tied=()):
    local, width = a.shape
    chunk = local // 4
    block = pl.BlockSpec((chunk, width), lambda i: (i, 0))
    sizes = (ONE, TWO) if matrix < 2 else (CAP,)
    place = matrix if matrix < 2 else 0
    return pl.pallas_call(
        functools.partial(merge, matrix),
        grid=(4,),
        in_specs=[pl.BlockSpec((chunk, key.shape[1]), lambda i: (i, 0)), block]
        + [pl.BlockSpec((NB, size, width), lambda i: (0, place, 0)) for size in sizes]
        + [pl.BlockSpec((NB, OVER, width), lambda i: (0, 2 * TWO // OVER, 0))]
        + [ANY] * len(tied),
        out_specs=[block, SMEM],
        out_shape=[shape((local, width), BF16), shape((1,))],
        scratch_shapes=[pltpu.VMEM((NB * (CAP + HOP), width), BF16)],
        compiler_params=PARAMS,
        cost_estimate=CHEAP,
    )(key, a, *near, two, *tied)


def correlate(parts, *refs):
    a_refs, b_refs, out_refs = refs[:2], refs[2:4], refs[-len(parts) :]
    tokens = a_refs[0].shape[1]

    def hidden(ref, start, size):
        g = ref[start : start + size]
        u = ref[start + size : start + 2 * size]
        return g / (1.0 + jnp.exp(-g)) * u

    for (start_a, start_b, size), out_ref in zip(parts, out_refs):
        for piece in range(2):
            a = hidden(a_refs[piece], start_a, size)
            b = hidden(b_refs[piece], start_b, size)
            sa, sb, saa, sbb, sab = (
                jnp.sum(x, axis=1, keepdims=True) for x in (a, b, a * a, b * b, a * b)
            )
            covar = sab - sa * sb / tokens
            var = (saa - sa * sa / tokens) * (sbb - sb * sb / tokens)
            out_ref[piece] = covar / jnp.sqrt(var + 1e-5)


def unorder(local, me_ref, keys_ref, corr_ref, out_ref):
    place = iota((corr_ref.shape[1], local), 0)
    hot = jnp.where(keys_ref[7:8, :local] == place, 1.0, 0.0)
    rest = corr_ref[...]
    total = jnp.zeros((8, local), F32)
    for _ in range(3):
        part = rest.astype(BF16)
        total = total + jnp.dot(part, hot.astype(BF16), preferred_element_type=F32)
        rest = rest - part.astype(F32)
    owner = lax.broadcasted_iota(jnp.int32, (8, local), 0) ^ me_ref[0]
    keep = jnp.where(keys_ref[6:7, :local] == owner.astype(F32), total, 0.0)
    out_ref[...] = jnp.sum(keep, axis=0, keepdims=True)


def call(kernel, outs, args, in_specs=None, out_specs=None, params=PARAMS, **more):
    specs = in_specs or [VMEM] * len(args)
    made = pl.pallas_call(
        kernel,
        out_shape=outs,
        in_specs=specs,
        out_specs=out_specs or [VMEM] * len(outs),
        compiler_params=params,
        cost_estimate=CHEAP,
        **more,
    )(*args)
    return made


def shape(dims, dtype=F32):
    return jax.ShapeDtypeStruct(dims, dtype)


def some(x):
    return x.reshape(-1, x.shape[-1])[:8, :128].astype(F32)


def tie(value, dtype, after):
    return call(
        functools.partial(constant, value),
        [shape((1,), dtype)],
        after,
        in_specs=[ANY] * len(after),
        out_specs=[SMEM],
    )


def exchange(x):
    return lax.all_to_all(x, "mp", split_axis=0, concat_axis=0, tiled=True)


def swap_cores(x):
    return lax.ppermute(x, "dp", [(i, i ^ 1) for i in range(8)])


def along_y(x, step):
    return lax.ppermute(
        x, "dp", [(i, ((i // 2 + step) % 4) * 2 + i % 2) for i in range(8)]
    )


def pre_activations(rows, core, y, mine, other, tokens, tokens_other):
    width = tokens.shape[1]
    ntok = tokens.shape[0]

    def chunk(i, place):
        return lax.rem(place[1] + i + 1, 4)

    pre = pl.pallas_call(
        functools.partial(preact, rows),
        grid_spec=pltpu.PrefetchScalarGridSpec(
            num_scalar_prefetch=1,
            grid=(4,),
            in_specs=[
                pl.BlockSpec((2, rows, width), lambda i, p: (4 * p[0] + chunk(i, p), 0, 0)),
                pl.BlockSpec((2, rows, width), lambda i, p: (chunk(i, p), 0, 0)),
                pl.BlockSpec((ntok, width), lambda i, p: (0, 0)),
                pl.BlockSpec((ntok, width), lambda i, p: (0, 0)),
            ],
            out_specs=pl.BlockSpec((2, rows, ntok), lambda i, p: (i, 0, 0)),
        ),
        out_shape=shape((8, rows, ntok)),
        compiler_params=PARAMS,
        cost_estimate=CHEAP,
    )(jnp.stack([core, y]), mine, other, tokens, tokens_other)
    return pre, (pre[1:3] * SCALE).astype(F16), (pre[3:5] * SCALE).astype(F16)


def second_messages(pre, plus, minus, scale):
    from_prev, from_next = along_y(plus, 1), along_y(minus, 3)
    far_plus = (pre[0] * scale + from_prev[1].astype(F32)).astype(F16)
    far_minus = (pre[5] * scale + from_next[0].astype(F32)).astype(F16)
    return from_prev[0], from_next[1], far_plus, far_minus


def totals(pre, from_prev, from_next, far_plus, far_minus):
    far_prev, far_next = along_y(far_plus, 1), along_y(far_minus, 3)
    low = pre[6] + (far_prev.astype(F32) + from_next.astype(F32)) * (1.0 / SCALE)
    high = pre[7] + (far_next.astype(F32) + from_prev.astype(F32)) * (1.0 / SCALE)
    return low, high


def from_partner(x, core, rows, zero=0):
    half = lax.dynamic_slice(x, (8 * (1 - core) + zero, 0, 0), (8, rows, x.shape[2]))
    return swap_cores(half)


def fast(tokens, gate_a, up_a, down_a, gate_b, up_b, down_b, perm):
    local, width = gate_a.shape
    ntok = tokens.shape[0]
    me = lax.axis_index("mp").astype(jnp.int32).reshape(1)
    dp = lax.axis_index("dp").astype(jnp.int32)
    core, y = dp & 1, dp >> 1
    padded = -(-local // 128) * 128
    grid = jnp.pad(
        perm.reshape(NB, local), ((0, 0), (0, padded - local)), constant_values=NB * local
    )
    tokens_other = swap_cores(tokens)

    send, slot_keys, table, bad = call(
        functools.partial(send_one, local),
        [
            shape((NB, 2 * ONE + OVER, width), BF16),
            shape((NB // 4, 2, 8, padded)),
            shape((3, NB, 128)),
            shape((1,), jnp.int32),
        ],
        (me, grid, gate_b, up_b, down_b),
        in_specs=[SMEM, VMEM] + [ANY] * 3,
        out_specs=[VMEM] * 3 + [SMEM],
        scratch_shapes=[pltpu.VMEM((local, width), BF16)] * 3 + [pltpu.SemaphoreType.DMA((3,))],
        params=ALONE,
    )
    one = exchange(send)

    (keys,) = call(
        functools.partial(receive_keys, local),
        [shape((8, padded))],
        (me, grid, table),
        in_specs=[SMEM, VMEM, VMEM],
    )
    (ordered,) = call(
        functools.partial(order_a, local),
        [shape((NB, SLOTS, width), BF16)],
        (keys, gate_a, up_a),
    )
    ordered_other = from_partner(ordered, core, SLOTS)
    two, forward = call(
        functools.partial(send_two, local),
        [shape((NB, 2 * TWO + OVER, width), BF16), shape((NB * OVER, NB * OVER), BF16)],
        (slot_keys, table, gate_b, up_b),
        params=ALONE,
    )
    pre_a, plus_a, minus_a = pre_activations(
        SLOTS, core, y, ordered, ordered_other, tokens, tokens_other
    )

    ready = some(plus_a)
    two, zero = pl.pallas_call(
        fill_forward,
        grid=(1,),
        in_specs=[
            pl.BlockSpec((NB * OVER, NB * OVER), lambda i: (0, 0)),
            pl.BlockSpec((NB, OVER, width), lambda i: (0, 2 * ONE // OVER, 0)),
        ]
        + [ANY] * 2,
        out_specs=[pl.BlockSpec((NB, OVER, width), lambda i: (0, 2 * TWO // OVER, 0)), SMEM],
        out_shape=[shape(two.shape, BF16), shape((1,), jnp.int32)],
        input_output_aliases={2: 0},
        compiler_params=ALONE,
        cost_estimate=CHEAP,
    )(forward, one, two, ready)
    sent_two = two
    two = exchange(two)
    one_other = from_partner(one, core, 2 * ONE, zero[0])
    pre_one, plus, minus = pre_activations(
        2 * ONE, core, y, one, one_other, tokens, tokens_other
    )
    (three,) = call(
        functools.partial(send_three, local),
        [shape((NB, CAP, width), BF16)],
        (slot_keys, down_b, sent_two),
        in_specs=[VMEM, VMEM, ANY],
        params=ALONE,
    )
    (scale,) = tie(SCALE, F32, (some(plus), three))
    waiting_a = second_messages(pre_a, plus_a, minus_a, scale)
    waiting_one = second_messages(pre_one, plus, minus, SCALE)
    sums_a = totals(pre_a, *waiting_a)
    sums_one = totals(pre_one, *waiting_one)

    (zero,) = tie(0, jnp.int32, (some(waiting_a[2]),))
    two_other = from_partner(two, core, CAP, zero[0])
    three = exchange(three)
    pre_two, plus, minus = pre_activations(
        CAP, core, y, two, two_other, tokens, tokens_other
    )
    tall = keys[:, :local].T
    merged_gate, scale = merged_rows(0, tall, gate_a, (one, two), two, (pre_two,))
    waiting_two = second_messages(pre_two, plus, minus, scale)
    ready = some(waiting_two[2])
    merged_up, _ = merged_rows(1, tall, up_a, (one, two), two, (ready,))
    sums_two = totals(pre_two, *waiting_two)

    (corr_one,) = call(
        functools.partial(correlate, ((0, 0, ONE),)), [shape((2, ONE, 1))], sums_a + sums_one
    )
    corr_two, corr_three = call(
        functools.partial(correlate, ((2 * ONE, 0, TWO), (2 * CAP, 2 * TWO, HOP))),
        [shape((2, TWO, 1)), shape((2, HOP, 1))],
        sums_a + sums_two + (merged_up,),
        in_specs=[VMEM] * 4 + [ANY],
    )
    corr = jnp.concatenate([c.reshape(-1) for c in (corr_one, corr_two, corr_three)])[None]
    for bit in (1, 2, 4):
        got = lax.ppermute(corr, "dp", [(i, i ^ bit) for i in range(8)])
        corr = jnp.concatenate([corr, got], axis=0)
    (match_corr,) = call(
        functools.partial(unorder, local), [shape((1, local))],
        (dp.reshape(1), keys, corr),
        in_specs=[SMEM, VMEM, VMEM],
    )

    merged_down, _ = merged_rows(2, tall, down_a, (three,), two)
    return (merged_gate, merged_up, merged_down, match_corr.reshape(-1)), bad[0]


def merge_rows(first, second):
    return ((first.astype(F32) + second.astype(F32)) * 0.5).astype(BF16)


def general(tokens, gate_a, up_a, down_a, gate_b, up_b, down_b, perm):
    me = lax.axis_index("mp")
    local = gate_a.shape[0]
    capacity = 2 * local // NB
    source = perm // local
    before = (jnp.arange(local)[:, None] < jnp.arange(local)[None, :]).astype(BF16)

    def rank_of(member):
        return jnp.dot(member.astype(BF16), before, preferred_element_type=F32).astype(jnp.int32)

    mine = (source == me).reshape(NB, local)
    hit = jnp.logical_and(
        mine[:, None, :], rank_of(mine)[:, None, :] == jnp.arange(capacity)[None, :, None]
    ).astype(jnp.int32)
    send_index = jnp.sum(hit * (perm % local).reshape(NB, 1, local), axis=2).reshape(-1)
    arrived = lax.dynamic_slice_in_dim(source, me * local, local)
    member = (jnp.arange(NB)[:, None] == arrived[None, :]).astype(jnp.int32)
    recv_index = arrived * capacity + jnp.sum(member * rank_of(member), axis=0)

    def matched(rows):
        moved = exchange(jnp.take(rows, send_index, axis=0))
        return jnp.take(moved, recv_index, axis=0)

    gate_match, up_match, down_match = matched(gate_b), matched(up_b), matched(down_b)

    def hidden(gate, up):
        g, u = (
            jnp.sum(
                lax.all_to_all(
                    lax.dot_general(
                        tokens, w, (((1,), (1,)), ((), ())), preferred_element_type=F32
                    ).reshape(8, -1, local),
                    "dp",
                    split_axis=0,
                    concat_axis=0,
                    tiled=True,
                ),
                axis=0,
            )
            for w in (gate, up)
        )
        return jax.nn.silu(g) * u

    a, b = hidden(gate_a, up_a), hidden(gate_match, up_match)
    sums = jnp.stack([jnp.sum(x, axis=0) for x in (a, b, a * a, b * b, a * b)])
    for bit in (1, 2, 4):
        sums = sums + lax.ppermute(sums, "dp", [(i, i ^ bit) for i in range(8)])
    sa, sb, saa, sbb, sab = sums
    ntok = tokens.shape[0] * 1.0
    covar = sab - sa * sb / ntok
    var = (saa - sa * sa / ntok) * (sbb - sb * sb / ntok)
    return (
        merge_rows(gate_a, gate_match),
        merge_rows(up_a, up_match),
        merge_rows(down_a, down_match),
        covar / jnp.sqrt(var + 1e-05),
    )


def local_program(*args):
    outs, bad = fast(*args)
    return lax.cond(bad > 0, lambda outs, args: general(*args), lambda outs, args: outs, outs, args)


def solution(mesh):
    return jax.shard_map(
        local_program,
        mesh=mesh,
        in_specs=(P(None, "dp"),) + (P("mp", "dp"),) * 6 + (P(),),
        out_specs=(P("mp", "dp"),) * 3 + (P("mp"),),
        check_vma=False,
    )
```

```python
import functools

import jax
import jax.numpy as jnp
from jax import lax
from jax.experimental import pallas as pl
from jax.experimental.pallas import tpu as pltpu
from jax.sharding import PartitionSpec as P

F32 = jnp.float32
BF16 = jnp.bfloat16
F16 = jnp.float16
NB = 16
CAP = 112
ONE = 64
TWO = CAP - ONE
HOP = 8
OVER = 4 * HOP
SLOTS = 2 * (CAP + HOP)
SCALE = 16.0
VMEM = pl.BlockSpec(memory_space=pltpu.VMEM)
SMEM = pl.BlockSpec(memory_space=pltpu.SMEM)
ANY = pl.BlockSpec(memory_space=pl.ANY)
CHEAP = pl.CostEstimate(flops=0, bytes_accessed=0, transcendentals=0)
ALONE = pltpu.CompilerParams(vmem_limit_bytes=58 * 2**20)
PARAMS = pltpu.CompilerParams(vmem_limit_bytes=24 * 2**20)


def iota(shape, dim):
    return lax.broadcasted_iota(jnp.int32, shape, dim).astype(F32)


def onehot(keys, ids):
    return jnp.where(keys == ids, 1.0, 0.0).astype(BF16)


def pick(hot, rows):
    return jnp.dot(hot, rows, preferred_element_type=F32)


def ranks(member):
    width = member.shape[1]
    before = (
        lax.broadcasted_iota(jnp.int32, (128, 128), 0)
        < lax.broadcasted_iota(jnp.int32, (128, 128), 1)
    )
    before = jnp.where(before, 1.0, 0.0).astype(BF16)
    carry = jnp.zeros((member.shape[0], 1), F32)
    tiles = []
    for j in range(width // 128):
        tile = member[:, j * 128 : (j + 1) * 128]
        tiles.append(jnp.dot(tile.astype(BF16), before, preferred_element_type=F32) + carry)
        carry = carry + jnp.sum(tile, axis=1, keepdims=True)
    return jnp.concatenate(tiles, axis=1)


def block_of(perm, local):
    block = jnp.zeros(perm.shape, F32)
    for k in range(1, NB + 1):
        block = block + jnp.where(perm >= k * local, 1.0, 0.0)
    return block


def tables(local, block):
    lane = iota((NB, 128), 1)
    row = iota((NB, 128), 0)
    count = jnp.zeros((NB, 128), F32)
    for s in range(NB):
        col = jnp.sum(jnp.where(block == s, 1.0, 0.0), axis=1, keepdims=True)
        count = count + jnp.where(lane == s, col, 0.0)
    layers = jnp.maximum(count - CAP, 0.0).astype(jnp.int32)
    layers = ((layers + (NB - 1)) >> 4).astype(F32)
    by_target = jnp.zeros((NB, 128), F32)
    by_source = jnp.zeros((NB, 128), F32)
    for k in range(NB):
        by_target = by_target + jnp.where(row > k, layers[k : k + 1, :], 0.0)
        by_source = by_source + jnp.where(lane > k, layers[:, k : k + 1], 0.0)
    return by_target, by_source, layers


def slot_values(keys, value, first, size):
    slot = iota((size, keys.shape[1]), 0) + first
    return [
        jnp.sum(jnp.where(keys[t : t + 1, :] == slot, value[t : t + 1, :], 0.0), axis=1, keepdims=True)
        - 1.0
        for t in range(keys.shape[0])
    ]


def send_one(
    local, me_ref, perm_ref, gate, up, down, send_ref, key_ref, table_ref, bad_ref, *scratch
):
    *held, sem = scratch
    copies = [
        pltpu.make_async_copy(rows, buffer, sem.at[i])
        for i, (rows, buffer) in enumerate(zip((gate, up, down), held))
    ]
    for copy in copies:
        copy.start()
    me = me_ref[0].astype(F32)
    perm = perm_ref[...]
    width = perm.shape[1]
    block = block_of(perm, local)
    value = perm.astype(F32) - block * local + 1.0
    mine = jnp.where(block == me, 1.0, 0.0)
    by_target, by_source, layers = tables(local, block)
    table_ref[0] = by_target
    table_ref[1] = by_source
    table_ref[2] = layers
    most = jnp.maximum(
        jnp.max(jnp.sum(layers, axis=0, keepdims=True)), jnp.max(jnp.sum(layers, axis=1, keepdims=True))
    )
    bad_ref[0] = jnp.where(most > HOP, 1, 0).astype(jnp.int32)

    rank = ranks(mine)
    base = jnp.where(iota((NB, 128), 1) == me, by_target, 0.0)
    base = jnp.sum(base, axis=1, keepdims=True)
    extra = (rank - CAP).astype(jnp.int32)
    mid = (extra & (NB - 1)).astype(F32)
    layer = (extra >> 4).astype(F32)
    direct = jnp.where(mine * jnp.where(rank < CAP, 1.0, 0.0) > 0, rank, -1.0)
    detour = jnp.where(mine * jnp.where(rank < CAP, 0.0, 1.0) > 0, mid * HOP + base + layer, -1.0)
    for i in range(NB // 4):
        key_ref[i, 0, :4] = direct[4 * i : 4 * i + 4]
        key_ref[i, 1, :4] = value[4 * i : 4 * i + 4]
    cols = slot_values(direct, value, 0, ONE)
    hop_slot = iota((NB * HOP, width), 0)
    hop = jnp.zeros((NB * HOP, width), F32)
    for t in range(NB):
        hop = hop + jnp.where(detour[t : t + 1, :] == hop_slot, value[t : t + 1, :], 0.0)
    hop = jnp.sum(hop, axis=1, keepdims=True) - 1.0

    for copy in copies:
        copy.wait()
    ids = iota((4 * ONE, local), 1)
    for i in range(NB // 4):
        hot = onehot(jnp.concatenate(cols[4 * i : 4 * i + 4], axis=0), ids)
        for j, rows in enumerate(held[:2]):
            out = pick(hot, rows[...]).astype(BF16)
            send_ref[4 * i : 4 * i + 4, j * ONE : (j + 1) * ONE] = out.reshape(4, ONE, -1)
    hot = onehot(hop, iota((NB * HOP, local), 1))
    parts = [pick(hot, rows[...]).reshape(NB, HOP, -1) for rows in held]
    parts.append(jnp.zeros_like(parts[0]))
    send_ref[:, 2 * ONE :] = jnp.concatenate(parts, axis=1).astype(BF16)


def receive_keys(local, me_ref, perm_ref, table_ref, keys_ref):
    me = me_ref[0].astype(F32)
    block = block_of(perm_ref[...], local)
    width = block.shape[1]
    source = jnp.sum(jnp.where(iota(block.shape, 0) == me, block, 0.0), axis=0, keepdims=True)
    member = jnp.where(source == iota((NB, width), 0), 1.0, 0.0)
    rank = jnp.sum(member * ranks(member), axis=0, keepdims=True)
    mine = jnp.where(iota((NB, 128), 0) == me, table_ref[1], 0.0)
    mine = jnp.sum(mine, axis=0, keepdims=True)
    square = jnp.where(iota((NB, 128), 0) == iota((NB, 128), 1), mine, 0.0)
    base = jnp.sum(square, axis=1, keepdims=True)
    base = jnp.sum(member * base, axis=0, keepdims=True)
    extra = (rank - CAP).astype(jnp.int32)
    mid = (extra & (NB - 1)).astype(F32)
    over = base + (extra >> 4).astype(F32)
    first = rank < ONE
    straight = rank < CAP
    k1 = jnp.where(first, source * ONE + rank, -1.0)
    k2 = jnp.where(first, -1.0, jnp.where(straight, source * TWO + (rank - ONE), -1.0))
    ko = jnp.where(straight, -1.0, mid * HOP + over)
    keys_ref[0:1] = jnp.where(straight, source * CAP + rank, NB * CAP + mid * HOP + over)
    keys_ref[1:3] = jnp.zeros((2, width), F32)
    keys_ref[3:4] = k1
    keys_ref[4:5] = k2
    keys_ref[5:6] = ko
    holder = jnp.where(straight, source, mid).astype(jnp.int32)
    piece = (holder & 1).astype(F32)
    device = ((holder >> 1) & 3) * 2 + (holder >> 3)
    keys_ref[6:7] = device.astype(F32)
    keys_ref[7:8] = jnp.where(
        first,
        piece * ONE + rank,
        jnp.where(straight, 2 * ONE + piece * TWO + rank - ONE, 2 * CAP + piece * HOP + over),
    )


def send_two(local, key_ref, table_ref, gate, up, two_ref, forward_ref):
    ids = iota((4 * TWO, local), 1)
    for i in range(NB // 4):
        cols = slot_values(key_ref[i, 0, :4], key_ref[i, 1, :4], ONE, TWO)
        hot = onehot(jnp.concatenate(cols, axis=0), ids)
        for j, rows in enumerate((gate, up)):
            out = pick(hot, rows[...]).astype(BF16)
            two_ref[4 * i : 4 * i + 4, j * TWO : (j + 1) * TWO] = out.reshape(4, TWO, -1)
    two_ref[:, 2 * TWO :] = jnp.zeros((NB, OVER, gate.shape[1]), BF16)
    forward_ref[...] = forwarding(table_ref)


def send_three(local, key_ref, down, *refs):
    three_ref = refs[-1]
    ids = iota((4 * CAP, local), 1)
    for i in range(NB // 4):
        cols = slot_values(key_ref[i, 0, :4], key_ref[i, 1, :4], 0, CAP)
        out = pick(onehot(jnp.concatenate(cols, axis=0), ids), down[...]).astype(BF16)
        three_ref[4 * i : 4 * i + 4] = out.reshape(4, CAP, -1)


def forwarding(table_ref):
    n = NB * OVER
    tall = lax.broadcasted_iota(jnp.int32, (n, NB), 0) >> 5
    tall = onehot(tall, lax.broadcasted_iota(jnp.int32, (n, NB), 1))
    wide = lax.broadcasted_iota(jnp.int32, (128, n), 1) >> 5
    wide = onehot(wide, lax.broadcasted_iota(jnp.int32, (128, n), 0))

    def spread(x):
        part = jnp.dot(tall, x.astype(BF16), preferred_element_type=F32)
        return jnp.dot(part.astype(BF16), wide, preferred_element_type=F32)

    by_target, by_source, layers = table_ref[0], table_ref[1], table_ref[2]
    r = lax.broadcasted_iota(jnp.int32, (n, n), 0)
    c = lax.broadcasted_iota(jnp.int32, (n, n), 1)
    matrix = jnp.where(((r >> 3) & 3) == ((c >> 3) & 3), 1.0, 0.0)
    depth = (c & 7).astype(F32) - spread(by_target)
    same = jnp.where((r & 7).astype(F32) - spread(by_source) == depth, 1.0, 0.0)
    inside = jnp.where(depth >= 0, 1.0, 0.0) * jnp.where(depth < spread(layers), 1.0, 0.0)
    return (matrix * same * inside).astype(BF16)


def fill_forward(forward_ref, one_ref, *refs):
    two_ref, zero_ref = refs[-2:]
    hops = one_ref[...].reshape(NB * OVER, -1)
    out = pick(forward_ref[...], hops).astype(BF16)
    two_ref[...] = out.reshape(two_ref.shape)
    zero_ref[0] = 0


def order_a(local, keys_ref, gate, up, out_ref):
    pair = (gate, up)
    for size, start, line in ((ONE, 0, 3), (TWO, 2 * ONE, 4)):
        key = keys_ref[line : line + 1, :local]
        for i in range(NB // 4):
            hot = onehot(iota((4 * size, local), 0) + 4 * size * i, key)
            for j, rows in enumerate(pair):
                out = pick(hot, rows[...]).astype(BF16)
                out_ref[4 * i : 4 * i + 4, start + j * size : start + (j + 1) * size] = out.reshape(
                    4, size, -1
                )
    hot = onehot(iota((NB * HOP, local), 0), keys_ref[5:6, :local])
    parts = [pick(hot, rows[...]).reshape(NB, HOP, -1) for rows in pair]
    out_ref[:, 2 * CAP :] = jnp.concatenate(parts, axis=1).astype(BF16)


def constant(value, *refs):
    refs[-1][0] = value


def preact(rows, place, own_ref, other_ref, tok_ref, tok_other_ref, out_ref):
    del place
    total = None
    for x, tok in ((own_ref, tok_ref), (other_ref, tok_other_ref)):
        part = lax.dot_general(
            x[:, :rows].reshape(2 * rows, -1),
            tok[...],
            (((1,), (1,)), ((), ())),
            preferred_element_type=F32,
        )
        total = part if total is None else total + part
    out_ref[...] = total.reshape(out_ref.shape)


def compact(matrix, sources, held):
    *near, far = sources
    for s in range(NB):
        start = s * CAP
        for x in near:
            size = x.shape[1]
            held[start : start + size] = x[s]
            start += size
    far = far[...].astype(F32)[:, matrix * HOP : (matrix + 1) * HOP]
    held[NB * CAP :] = far.reshape(NB * HOP, -1).astype(BF16)


def merge(matrix, key_ref, a_ref, *refs):
    out_ref, scale_ref, held = refs[-3:]
    sources = refs[: 3 if matrix < 2 else 2]

    @pl.when(pl.program_id(0) == 0)
    def _():
        compact(matrix, sources, held)
        scale_ref[0] = SCALE

    hot = onehot(key_ref[:, 0:1], iota((key_ref.shape[0], NB * (CAP + HOP)), 1))
    out_ref[...] = ((a_ref[...].astype(F32) + pick(hot, held[...])) * 0.5).astype(BF16)


def merged_rows(matrix, key, a, near, two, tied=()):
    local, width = a.shape
    chunk = local // 4
    block = pl.BlockSpec((chunk, width), lambda i: (i, 0))
    sizes = (ONE, TWO) if matrix < 2 else (CAP,)
    place = matrix if matrix < 2 else 0
    return pl.pallas_call(
        functools.partial(merge, matrix),
        grid=(4,),
        in_specs=[pl.BlockSpec((chunk, key.shape[1]), lambda i: (i, 0)), block]
        + [pl.BlockSpec((NB, size, width), lambda i: (0, place, 0)) for size in sizes]
        + [pl.BlockSpec((NB, OVER, width), lambda i: (0, 2 * TWO // OVER, 0))]
        + [ANY] * len(tied),
        out_specs=[block, SMEM],
        out_shape=[shape((local, width), BF16), shape((1,))],
        scratch_shapes=[pltpu.VMEM((NB * (CAP + HOP), width), BF16)],
        compiler_params=PARAMS,
        cost_estimate=CHEAP,
    )(key, a, *near, two, *tied)


def correlate(parts, earlier, *refs):
    a_refs, b_refs, out_ref = refs[:2], refs[2:4], refs[-1]
    tokens = a_refs[0].shape[1]

    def hidden(ref, start, size):
        g = ref[start : start + size]
        u = ref[start + size : start + 2 * size]
        return g / (1.0 + jnp.exp(-g)) * u

    cols = []
    for start_a, start_b, size in parts:
        for piece in range(2):
            a = hidden(a_refs[piece], start_a, size)
            b = hidden(b_refs[piece], start_b, size)
            sa, sb, saa, sbb, sab = (
                jnp.sum(x, axis=1, keepdims=True) for x in (a, b, a * a, b * b, a * b)
            )
            covar = sab - sa * sb / tokens
            var = (saa - sa * sa / tokens) * (sbb - sb * sb / tokens)
            cols.append(covar / jnp.sqrt(var + 1e-5))
    have = sum(x.shape[0] for x in cols)
    if have < 128:
        cols.append(jnp.zeros((128 - have, 1), F32))
    square = lax.broadcasted_iota(jnp.int32, (128, 128), 0) == lax.broadcasted_iota(
        jnp.int32, (128, 128), 1
    )
    row = jnp.sum(jnp.where(square, jnp.concatenate(cols, axis=0), 0.0), axis=0, keepdims=True)
    if earlier:
        row = jnp.concatenate([refs[4][...], row], axis=1)
    out_ref[...] = row


def unorder(local, me_ref, keys_ref, corr_ref, out_ref):
    place = iota((corr_ref.shape[1], local), 0)
    hot = jnp.where(keys_ref[7:8, :local] == place, 1.0, 0.0)
    rest = corr_ref[...]
    total = jnp.zeros((8, local), F32)
    for _ in range(3):
        part = rest.astype(BF16)
        total = total + jnp.dot(part, hot.astype(BF16), preferred_element_type=F32)
        rest = rest - part.astype(F32)
    owner = lax.broadcasted_iota(jnp.int32, (8, local), 0) ^ me_ref[0]
    keep = jnp.where(keys_ref[6:7, :local] == owner.astype(F32), total, 0.0)
    out_ref[...] = jnp.sum(keep, axis=0, keepdims=True)


def call(kernel, outs, args, in_specs=None, out_specs=None, params=PARAMS, **more):
    specs = in_specs or [VMEM] * len(args)
    made = pl.pallas_call(
        kernel,
        out_shape=outs,
        in_specs=specs,
        out_specs=out_specs or [VMEM] * len(outs),
        compiler_params=params,
        cost_estimate=CHEAP,
        **more,
    )(*args)
    return made


def shape(dims, dtype=F32):
    return jax.ShapeDtypeStruct(dims, dtype)


def some(x):
    return x.reshape(-1, x.shape[-1])[:8, :128].astype(F32)


def tie(value, dtype, after):
    return call(
        functools.partial(constant, value),
        [shape((1,), dtype)],
        after,
        in_specs=[ANY] * len(after),
        out_specs=[SMEM],
    )


def exchange(x):
    return lax.all_to_all(x, "mp", split_axis=0, concat_axis=0, tiled=True)


def swap_cores(x):
    return lax.ppermute(x, "dp", [(i, i ^ 1) for i in range(8)])


def along_y(x, step):
    return lax.ppermute(
        x, "dp", [(i, ((i // 2 + step) % 4) * 2 + i % 2) for i in range(8)]
    )


def pre_activations(rows, core, y, mine, other, tokens, tokens_other):
    width = tokens.shape[1]
    ntok = tokens.shape[0]

    def chunk(i, place):
        return lax.rem(place[1] + i + 1, 4)

    pre = pl.pallas_call(
        functools.partial(preact, rows),
        grid_spec=pltpu.PrefetchScalarGridSpec(
            num_scalar_prefetch=1,
            grid=(4,),
            in_specs=[
                pl.BlockSpec((2, rows, width), lambda i, p: (4 * p[0] + chunk(i, p), 0, 0)),
                pl.BlockSpec((2, rows, width), lambda i, p: (chunk(i, p), 0, 0)),
                pl.BlockSpec((ntok, width), lambda i, p: (0, 0)),
                pl.BlockSpec((ntok, width), lambda i, p: (0, 0)),
            ],
            out_specs=pl.BlockSpec((2, rows, ntok), lambda i, p: (i, 0, 0)),
        ),
        out_shape=shape((8, rows, ntok)),
        compiler_params=PARAMS,
        cost_estimate=CHEAP,
    )(jnp.stack([core, y]), mine, other, tokens, tokens_other)
    return pre, (pre[1:3] * SCALE).astype(F16), (pre[3:5] * SCALE).astype(F16)


def second_messages(pre, plus, minus, scale):
    from_prev, from_next = along_y(plus, 1), along_y(minus, 3)
    far_plus = (pre[0] * scale + from_prev[1].astype(F32)).astype(F16)
    far_minus = (pre[5] * scale + from_next[0].astype(F32)).astype(F16)
    return from_prev[0], from_next[1], far_plus, far_minus


def totals(pre, from_prev, from_next, far_plus, far_minus):
    far_prev, far_next = along_y(far_plus, 1), along_y(far_minus, 3)
    low = pre[6] + (far_prev.astype(F32) + from_next.astype(F32)) * (1.0 / SCALE)
    high = pre[7] + (far_next.astype(F32) + from_prev.astype(F32)) * (1.0 / SCALE)
    return low, high


def from_partner(x, core, rows, zero=0):
    half = lax.dynamic_slice(x, (8 * (1 - core) + zero, 0, 0), (8, rows, x.shape[2]))
    return swap_cores(half)


def fast(tokens, gate_a, up_a, down_a, gate_b, up_b, down_b, perm):
    local, width = gate_a.shape
    ntok = tokens.shape[0]
    me = lax.axis_index("mp").astype(jnp.int32).reshape(1)
    dp = lax.axis_index("dp").astype(jnp.int32)
    core, y = dp & 1, dp >> 1
    padded = -(-local // 128) * 128
    grid = jnp.pad(
        perm.reshape(NB, local), ((0, 0), (0, padded - local)), constant_values=NB * local
    )
    tokens_other = swap_cores(tokens)

    send, slot_keys, table, bad = call(
        functools.partial(send_one, local),
        [
            shape((NB, 2 * ONE + OVER, width), BF16),
            shape((NB // 4, 2, 8, padded)),
            shape((3, NB, 128)),
            shape((1,), jnp.int32),
        ],
        (me, grid, gate_b, up_b, down_b),
        in_specs=[SMEM, VMEM] + [ANY] * 3,
        out_specs=[VMEM] * 3 + [SMEM],
        scratch_shapes=[pltpu.VMEM((local, width), BF16)] * 3 + [pltpu.SemaphoreType.DMA((3,))],
        params=ALONE,
    )
    one = exchange(send)

    (keys,) = call(
        functools.partial(receive_keys, local),
        [shape((8, padded))],
        (me, grid, table),
        in_specs=[SMEM, VMEM, VMEM],
    )
    (ordered,) = call(
        functools.partial(order_a, local),
        [shape((NB, SLOTS, width), BF16)],
        (keys, gate_a, up_a),
    )
    ordered_other = from_partner(ordered, core, SLOTS)
    two, forward = call(
        functools.partial(send_two, local),
        [shape((NB, 2 * TWO + OVER, width), BF16), shape((NB * OVER, NB * OVER), BF16)],
        (slot_keys, table, gate_b, up_b),
    )
    pre_a, plus_a, minus_a = pre_activations(
        SLOTS, core, y, ordered, ordered_other, tokens, tokens_other
    )

    ready = some(plus_a)
    two, zero = pl.pallas_call(
        fill_forward,
        grid=(1,),
        in_specs=[
            pl.BlockSpec((NB * OVER, NB * OVER), lambda i: (0, 0)),
            pl.BlockSpec((NB, OVER, width), lambda i: (0, 2 * ONE // OVER, 0)),
        ]
        + [ANY] * 2,
        out_specs=[pl.BlockSpec((NB, OVER, width), lambda i: (0, 2 * TWO // OVER, 0)), SMEM],
        out_shape=[shape(two.shape, BF16), shape((1,), jnp.int32)],
        input_output_aliases={2: 0},
        compiler_params=ALONE,
        cost_estimate=CHEAP,
    )(forward, one, two, ready)
    sent_two = two
    two = exchange(two)
    one_other = from_partner(one, core, 2 * ONE, zero[0])
    pre_one, plus, minus = pre_activations(
        2 * ONE, core, y, one, one_other, tokens, tokens_other
    )
    (three,) = call(
        functools.partial(send_three, local),
        [shape((NB, CAP, width), BF16)],
        (slot_keys, down_b, sent_two),
        in_specs=[VMEM, VMEM, ANY],
    )
    tall = keys[:, :local].T
    (scale,) = tie(SCALE, F32, (some(plus), three, tall))
    waiting_a = second_messages(pre_a, plus_a, minus_a, scale)
    waiting_one = second_messages(pre_one, plus, minus, SCALE)
    sums_a = totals(pre_a, *waiting_a)
    sums_one = totals(pre_one, *waiting_one)

    (zero,) = tie(0, jnp.int32, (some(waiting_a[2]),))
    two_other = from_partner(two, core, CAP, zero[0])
    three = exchange(three)
    pre_two, plus, minus = pre_activations(
        CAP, core, y, two, two_other, tokens, tokens_other
    )
    merged_gate, scale = merged_rows(0, tall, gate_a, (one, two), two, (pre_two,))
    waiting_two = second_messages(pre_two, plus, minus, scale)
    ready = some(waiting_two[2])
    merged_up, _ = merged_rows(1, tall, up_a, (one, two), two, (ready,))
    sums_two = totals(pre_two, *waiting_two)

    (corr_one,) = call(
        functools.partial(correlate, ((0, 0, ONE),), False),
        [shape((1, 128))],
        sums_a + sums_one,
    )
    parts = ((2 * ONE, 0, TWO), (2 * CAP, 2 * TWO, HOP))
    (corr,) = call(
        functools.partial(correlate, parts, True),
        [shape((1, 256))],
        sums_a + sums_two + (corr_one, merged_up),
        in_specs=[VMEM] * 5 + [ANY],
    )
    for bit in (1, 2, 4):
        got = lax.ppermute(corr, "dp", [(i, i ^ bit) for i in range(8)])
        corr = jnp.concatenate([corr, got], axis=0)
    (match_corr,) = call(
        functools.partial(unorder, local), [shape((1, local))],
        (dp.reshape(1), keys, corr),
        in_specs=[SMEM, VMEM, VMEM],
    )

    merged_down, _ = merged_rows(2, tall, down_a, (three,), two)
    return (merged_gate, merged_up, merged_down, match_corr.reshape(-1)), bad[0]


def merge_rows(first, second):
    return ((first.astype(F32) + second.astype(F32)) * 0.5).astype(BF16)


def general(tokens, gate_a, up_a, down_a, gate_b, up_b, down_b, perm):
    me = lax.axis_index("mp")
    local = gate_a.shape[0]
    capacity = 2 * local // NB
    source = perm // local
    before = (jnp.arange(local)[:, None] < jnp.arange(local)[None, :]).astype(BF16)

    def rank_of(member):
        return jnp.dot(member.astype(BF16), before, preferred_element_type=F32).astype(jnp.int32)

    mine = (source == me).reshape(NB, local)
    hit = jnp.logical_and(
        mine[:, None, :], rank_of(mine)[:, None, :] == jnp.arange(capacity)[None, :, None]
    ).astype(jnp.int32)
    send_index = jnp.sum(hit * (perm % local).reshape(NB, 1, local), axis=2).reshape(-1)
    arrived = lax.dynamic_slice_in_dim(source, me * local, local)
    member = (jnp.arange(NB)[:, None] == arrived[None, :]).astype(jnp.int32)
    recv_index = arrived * capacity + jnp.sum(member * rank_of(member), axis=0)

    def matched(rows):
        moved = exchange(jnp.take(rows, send_index, axis=0))
        return jnp.take(moved, recv_index, axis=0)

    gate_match, up_match, down_match = matched(gate_b), matched(up_b), matched(down_b)

    def hidden(gate, up):
        g, u = (
            jnp.sum(
                lax.all_to_all(
                    lax.dot_general(
                        tokens, w, (((1,), (1,)), ((), ())), preferred_element_type=F32
                    ).reshape(8, -1, local),
                    "dp",
                    split_axis=0,
                    concat_axis=0,
                    tiled=True,
                ),
                axis=0,
            )
            for w in (gate, up)
        )
        return jax.nn.silu(g) * u

    a, b = hidden(gate_a, up_a), hidden(gate_match, up_match)
    sums = jnp.stack([jnp.sum(x, axis=0) for x in (a, b, a * a, b * b, a * b)])
    for bit in (1, 2, 4):
        sums = sums + lax.ppermute(sums, "dp", [(i, i ^ bit) for i in range(8)])
    sa, sb, saa, sbb, sab = sums
    ntok = tokens.shape[0] * 1.0
    covar = sab - sa * sb / ntok
    var = (saa - sa * sa / ntok) * (sbb - sb * sb / ntok)
    return (
        merge_rows(gate_a, gate_match),
        merge_rows(up_a, up_match),
        merge_rows(down_a, down_match),
        covar / jnp.sqrt(var + 1e-05),
    )


def local_program(*args):
    outs, bad = fast(*args)
    return lax.cond(bad > 0, lambda outs, args: general(*args), lambda outs, args: outs, outs, args)


def solution(mesh):
    return jax.shard_map(
        local_program,
        mesh=mesh,
        in_specs=(P(None, "dp"),) + (P("mp", "dp"),) * 6 + (P(),),
        out_specs=(P("mp", "dp"),) * 3 + (P("mp"),),
        check_vma=False,
    )
```

```python
import functools

import jax
import jax.numpy as jnp
from jax import lax
from jax.experimental import pallas as pl
from jax.experimental.pallas import tpu as pltpu
from jax.sharding import PartitionSpec as P

F32 = jnp.float32
BF16 = jnp.bfloat16
F16 = jnp.float16
NB = 16
CAP = 112
ONE = 64
TWO = CAP - ONE
HOP = 8
OVER = 4 * HOP
SLOTS = 2 * (CAP + HOP)
SCALE = 16.0
VMEM = pl.BlockSpec(memory_space=pltpu.VMEM)
SMEM = pl.BlockSpec(memory_space=pltpu.SMEM)
ANY = pl.BlockSpec(memory_space=pl.ANY)
CHEAP = pl.CostEstimate(flops=0, bytes_accessed=0, transcendentals=0)
ALONE = pltpu.CompilerParams(vmem_limit_bytes=58 * 2**20)
PARAMS = pltpu.CompilerParams(vmem_limit_bytes=18 * 2**20)


def iota(shape, dim):
    return lax.broadcasted_iota(jnp.int32, shape, dim).astype(F32)


def onehot(keys, ids):
    return jnp.where(keys == ids, 1.0, 0.0).astype(BF16)


def pick(hot, rows):
    return jnp.dot(hot, rows, preferred_element_type=F32)


def ranks(member):
    width = member.shape[1]
    before = (
        lax.broadcasted_iota(jnp.int32, (128, 128), 0)
        < lax.broadcasted_iota(jnp.int32, (128, 128), 1)
    )
    before = jnp.where(before, 1.0, 0.0).astype(BF16)
    carry = jnp.zeros((member.shape[0], 1), F32)
    tiles = []
    for j in range(width // 128):
        tile = member[:, j * 128 : (j + 1) * 128]
        tiles.append(jnp.dot(tile.astype(BF16), before, preferred_element_type=F32) + carry)
        carry = carry + jnp.sum(tile, axis=1, keepdims=True)
    return jnp.concatenate(tiles, axis=1)


def block_of(perm, local):
    block = jnp.zeros(perm.shape, F32)
    for k in range(1, NB + 1):
        block = block + jnp.where(perm >= k * local, 1.0, 0.0)
    return block


def tables(local, block):
    lane = iota((NB, 128), 1)
    row = iota((NB, 128), 0)
    count = jnp.zeros((NB, 128), F32)
    for s in range(NB):
        col = jnp.sum(jnp.where(block == s, 1.0, 0.0), axis=1, keepdims=True)
        count = count + jnp.where(lane == s, col, 0.0)
    layers = jnp.maximum(count - CAP, 0.0).astype(jnp.int32)
    layers = ((layers + (NB - 1)) >> 4).astype(F32)
    by_target = jnp.zeros((NB, 128), F32)
    by_source = jnp.zeros((NB, 128), F32)
    for k in range(NB):
        by_target = by_target + jnp.where(row > k, layers[k : k + 1, :], 0.0)
        by_source = by_source + jnp.where(lane > k, layers[:, k : k + 1], 0.0)
    return by_target, by_source, layers


def slot_values(keys, value, first, size):
    slot = iota((size, keys.shape[1]), 0) + first
    return [
        jnp.sum(jnp.where(keys[t : t + 1, :] == slot, value[t : t + 1, :], 0.0), axis=1, keepdims=True)
        - 1.0
        for t in range(keys.shape[0])
    ]


def send_one(
    local, me_ref, perm_ref, gate, up, down, send_ref, key_ref, table_ref, bad_ref, *scratch
):
    *held, sem = scratch
    copies = [
        pltpu.make_async_copy(rows, buffer, sem.at[i])
        for i, (rows, buffer) in enumerate(zip((gate, up, down), held))
    ]
    for copy in copies:
        copy.start()
    me = me_ref[0].astype(F32)
    perm = perm_ref[...]
    width = perm.shape[1]
    block = block_of(perm, local)
    value = perm.astype(F32) - block * local + 1.0
    mine = jnp.where(block == me, 1.0, 0.0)
    by_target, by_source, layers = tables(local, block)
    table_ref[0] = by_target
    table_ref[1] = by_source
    table_ref[2] = layers
    most = jnp.maximum(
        jnp.max(jnp.sum(layers, axis=0, keepdims=True)), jnp.max(jnp.sum(layers, axis=1, keepdims=True))
    )
    bad_ref[0] = jnp.where(most > HOP, 1, 0).astype(jnp.int32)

    rank = ranks(mine)
    base = jnp.where(iota((NB, 128), 1) == me, by_target, 0.0)
    base = jnp.sum(base, axis=1, keepdims=True)
    extra = (rank - CAP).astype(jnp.int32)
    mid = (extra & (NB - 1)).astype(F32)
    layer = (extra >> 4).astype(F32)
    direct = jnp.where(mine * jnp.where(rank < CAP, 1.0, 0.0) > 0, rank, -1.0)
    detour = jnp.where(mine * jnp.where(rank < CAP, 0.0, 1.0) > 0, mid * HOP + base + layer, -1.0)
    for i in range(NB // 4):
        key_ref[i, 0, :4] = direct[4 * i : 4 * i + 4]
        key_ref[i, 1, :4] = value[4 * i : 4 * i + 4]
    cols = slot_values(direct, value, 0, ONE)
    hop_slot = iota((NB * HOP, width), 0)
    hop = jnp.zeros((NB * HOP, width), F32)
    for t in range(NB):
        hop = hop + jnp.where(detour[t : t + 1, :] == hop_slot, value[t : t + 1, :], 0.0)
    hop = jnp.sum(hop, axis=1, keepdims=True) - 1.0

    for copy in copies:
        copy.wait()
    ids = iota((4 * ONE, local), 1)
    for i in range(NB // 4):
        hot = onehot(jnp.concatenate(cols[4 * i : 4 * i + 4], axis=0), ids)
        for j, rows in enumerate(held[:2]):
            out = pick(hot, rows[...]).astype(BF16)
            send_ref[4 * i : 4 * i + 4, j * ONE : (j + 1) * ONE] = out.reshape(4, ONE, -1)
    hot = onehot(hop, iota((NB * HOP, local), 1))
    parts = [pick(hot, rows[...]).reshape(NB, HOP, -1) for rows in held]
    parts.append(jnp.zeros_like(parts[0]))
    send_ref[:, 2 * ONE :] = jnp.concatenate(parts, axis=1).astype(BF16)


def receive_keys(local, me_ref, perm_ref, table_ref, keys_ref):
    me = me_ref[0].astype(F32)
    block = block_of(perm_ref[...], local)
    width = block.shape[1]
    source = jnp.sum(jnp.where(iota(block.shape, 0) == me, block, 0.0), axis=0, keepdims=True)
    member = jnp.where(source == iota((NB, width), 0), 1.0, 0.0)
    rank = jnp.sum(member * ranks(member), axis=0, keepdims=True)
    mine = jnp.where(iota((NB, 128), 0) == me, table_ref[1], 0.0)
    mine = jnp.sum(mine, axis=0, keepdims=True)
    square = jnp.where(iota((NB, 128), 0) == iota((NB, 128), 1), mine, 0.0)
    base = jnp.sum(square, axis=1, keepdims=True)
    base = jnp.sum(member * base, axis=0, keepdims=True)
    extra = (rank - CAP).astype(jnp.int32)
    mid = (extra & (NB - 1)).astype(F32)
    over = base + (extra >> 4).astype(F32)
    first = rank < ONE
    straight = rank < CAP
    k1 = jnp.where(first, source * ONE + rank, -1.0)
    k2 = jnp.where(first, -1.0, jnp.where(straight, source * TWO + (rank - ONE), -1.0))
    ko = jnp.where(straight, -1.0, mid * HOP + over)
    keys_ref[0:1] = jnp.where(straight, source * CAP + rank, NB * CAP + mid * HOP + over)
    keys_ref[1:3] = jnp.zeros((2, width), F32)
    keys_ref[3:4] = k1
    keys_ref[4:5] = k2
    keys_ref[5:6] = ko
    holder = jnp.where(straight, source, mid).astype(jnp.int32)
    piece = (holder & 1).astype(F32)
    device = ((holder >> 1) & 3) * 2 + (holder >> 3)
    keys_ref[6:7] = device.astype(F32)
    keys_ref[7:8] = jnp.where(
        first,
        piece * ONE + rank,
        jnp.where(straight, 2 * ONE + piece * TWO + rank - ONE, 2 * CAP + piece * HOP + over),
    )


def send_two(local, key_ref, table_ref, gate, up, two_ref, forward_ref):
    ids = iota((4 * TWO, local), 1)
    for i in range(NB // 4):
        cols = slot_values(key_ref[i, 0, :4], key_ref[i, 1, :4], ONE, TWO)
        hot = onehot(jnp.concatenate(cols, axis=0), ids)
        for j, rows in enumerate((gate, up)):
            out = pick(hot, rows[...]).astype(BF16)
            two_ref[4 * i : 4 * i + 4, j * TWO : (j + 1) * TWO] = out.reshape(4, TWO, -1)
    two_ref[:, 2 * TWO :] = jnp.zeros((NB, OVER, gate.shape[1]), BF16)
    forward_ref[...] = forwarding(table_ref)


def send_three(local, key_ref, down, *refs):
    three_ref = refs[-1]
    ids = iota((4 * CAP, local), 1)
    for i in range(NB // 4):
        cols = slot_values(key_ref[i, 0, :4], key_ref[i, 1, :4], 0, CAP)
        out = pick(onehot(jnp.concatenate(cols, axis=0), ids), down[...]).astype(BF16)
        three_ref[4 * i : 4 * i + 4] = out.reshape(4, CAP, -1)


def forwarding(table_ref):
    n = NB * OVER
    tall = lax.broadcasted_iota(jnp.int32, (n, NB), 0) >> 5
    tall = onehot(tall, lax.broadcasted_iota(jnp.int32, (n, NB), 1))
    wide = lax.broadcasted_iota(jnp.int32, (128, n), 1) >> 5
    wide = onehot(wide, lax.broadcasted_iota(jnp.int32, (128, n), 0))

    def spread(x):
        part = jnp.dot(tall, x.astype(BF16), preferred_element_type=F32)
        return jnp.dot(part.astype(BF16), wide, preferred_element_type=F32)

    by_target, by_source, layers = table_ref[0], table_ref[1], table_ref[2]
    r = lax.broadcasted_iota(jnp.int32, (n, n), 0)
    c = lax.broadcasted_iota(jnp.int32, (n, n), 1)
    matrix = jnp.where(((r >> 3) & 3) == ((c >> 3) & 3), 1.0, 0.0)
    depth = (c & 7).astype(F32) - spread(by_target)
    same = jnp.where((r & 7).astype(F32) - spread(by_source) == depth, 1.0, 0.0)
    inside = jnp.where(depth >= 0, 1.0, 0.0) * jnp.where(depth < spread(layers), 1.0, 0.0)
    return (matrix * same * inside).astype(BF16)


def fill_forward(forward_ref, one_ref, *refs):
    two_ref, zero_ref = refs[-2:]
    hops = one_ref[...].reshape(NB * OVER, -1)
    out = pick(forward_ref[...], hops).astype(BF16)
    two_ref[...] = out.reshape(two_ref.shape)
    zero_ref[0] = 0


def order_a(local, keys_ref, gate, up, out_ref):
    pair = (gate, up)
    for size, start, line in ((ONE, 0, 3), (TWO, 2 * ONE, 4)):
        key = keys_ref[line : line + 1, :local]
        for i in range(NB // 4):
            hot = onehot(iota((4 * size, local), 0) + 4 * size * i, key)
            for j, rows in enumerate(pair):
                out = pick(hot, rows[...]).astype(BF16)
                out_ref[4 * i : 4 * i + 4, start + j * size : start + (j + 1) * size] = out.reshape(
                    4, size, -1
                )
    hot = onehot(iota((NB * HOP, local), 0), keys_ref[5:6, :local])
    parts = [pick(hot, rows[...]).reshape(NB, HOP, -1) for rows in pair]
    out_ref[:, 2 * CAP :] = jnp.concatenate(parts, axis=1).astype(BF16)


def constant(value, *refs):
    refs[-1][0] = value


def preact(rows, place, own_ref, other_ref, tok_ref, tok_other_ref, out_ref):
    del place
    total = None
    for x, tok in ((own_ref, tok_ref), (other_ref, tok_other_ref)):
        part = lax.dot_general(
            x[:, :rows].reshape(2 * rows, -1),
            tok[...],
            (((1,), (1,)), ((), ())),
            preferred_element_type=F32,
        )
        total = part if total is None else total + part
    out_ref[...] = total.reshape(out_ref.shape)


def compact(matrix, sources, held):
    *near, far = sources
    for s in range(NB):
        start = s * CAP
        for x in near:
            size = x.shape[1]
            held[start : start + size] = x[s]
            start += size
    far = far[...].astype(F32)[:, matrix * HOP : (matrix + 1) * HOP]
    held[NB * CAP :] = far.reshape(NB * HOP, -1).astype(BF16)


def merge(matrix, key_ref, a_ref, *refs):
    out_ref, scale_ref, held = refs[-3:]
    sources = refs[: 3 if matrix < 2 else 2]

    @pl.when(pl.program_id(0) == 0)
    def _():
        compact(matrix, sources, held)
        scale_ref[0] = SCALE

    hot = onehot(key_ref[:, 0:1], iota((key_ref.shape[0], NB * (CAP + HOP)), 1))
    out_ref[...] = ((a_ref[...].astype(F32) + pick(hot, held[...])) * 0.5).astype(BF16)


def merged_rows(matrix, key, a, near, two, tied=()):
    local, width = a.shape
    chunk = local // 4
    block = pl.BlockSpec((chunk, width), lambda i: (i, 0))
    sizes = (ONE, TWO) if matrix < 2 else (CAP,)
    place = matrix if matrix < 2 else 0
    return pl.pallas_call(
        functools.partial(merge, matrix),
        grid=(4,),
        in_specs=[pl.BlockSpec((chunk, key.shape[1]), lambda i: (i, 0)), block]
        + [pl.BlockSpec((NB, size, width), lambda i: (0, place, 0)) for size in sizes]
        + [pl.BlockSpec((NB, OVER, width), lambda i: (0, 2 * TWO // OVER, 0))]
        + [ANY] * len(tied),
        out_specs=[block, SMEM],
        out_shape=[shape((local, width), BF16), shape((1,))],
        scratch_shapes=[pltpu.VMEM((NB * (CAP + HOP), width), BF16)],
        compiler_params=PARAMS,
        cost_estimate=CHEAP,
    )(key, a, *near, two, *tied)


def correlate(parts, earlier, *refs):
    a_refs, b_refs, out_ref = refs[:2], refs[2:4], refs[-1]
    tokens = a_refs[0].shape[1]

    def hidden(ref, start, size):
        g = ref[start : start + size]
        u = ref[start + size : start + 2 * size]
        return g / (1.0 + jnp.exp(-g)) * u

    cols = []
    for start_a, start_b, size in parts:
        for piece in range(2):
            a = hidden(a_refs[piece], start_a, size)
            b = hidden(b_refs[piece], start_b, size)
            sa, sb, saa, sbb, sab = (
                jnp.sum(x, axis=1, keepdims=True) for x in (a, b, a * a, b * b, a * b)
            )
            covar = sab - sa * sb / tokens
            var = (saa - sa * sa / tokens) * (sbb - sb * sb / tokens)
            cols.append(covar / jnp.sqrt(var + 1e-5))
    have = sum(x.shape[0] for x in cols)
    if have < 128:
        cols.append(jnp.zeros((128 - have, 1), F32))
    square = lax.broadcasted_iota(jnp.int32, (128, 128), 0) == lax.broadcasted_iota(
        jnp.int32, (128, 128), 1
    )
    row = jnp.sum(jnp.where(square, jnp.concatenate(cols, axis=0), 0.0), axis=0, keepdims=True)
    if earlier:
        row = jnp.concatenate([refs[4][...], row], axis=1)
    out_ref[...] = row


def unorder(local, me_ref, keys_ref, corr_ref, out_ref):
    place = iota((corr_ref.shape[1], local), 0)
    hot = jnp.where(keys_ref[7:8, :local] == place, 1.0, 0.0)
    rest = corr_ref[...]
    total = jnp.zeros((8, local), F32)
    for _ in range(3):
        part = rest.astype(BF16)
        total = total + jnp.dot(part, hot.astype(BF16), preferred_element_type=F32)
        rest = rest - part.astype(F32)
    owner = lax.broadcasted_iota(jnp.int32, (8, local), 0) ^ me_ref[0]
    keep = jnp.where(keys_ref[6:7, :local] == owner.astype(F32), total, 0.0)
    out_ref[...] = jnp.sum(keep, axis=0, keepdims=True)


def call(kernel, outs, args, in_specs=None, out_specs=None, params=PARAMS, **more):
    specs = in_specs or [VMEM] * len(args)
    made = pl.pallas_call(
        kernel,
        out_shape=outs,
        in_specs=specs,
        out_specs=out_specs or [VMEM] * len(outs),
        compiler_params=params,
        cost_estimate=CHEAP,
        **more,
    )(*args)
    return made


def shape(dims, dtype=F32):
    return jax.ShapeDtypeStruct(dims, dtype)


def some(x):
    return x.reshape(-1, x.shape[-1])[:8, :128].astype(F32)


def tie(value, dtype, after):
    return call(
        functools.partial(constant, value),
        [shape((1,), dtype)],
        after,
        in_specs=[ANY] * len(after),
        out_specs=[SMEM],
    )


def exchange(x):
    return lax.all_to_all(x, "mp", split_axis=0, concat_axis=0, tiled=True)


def swap_cores(x):
    return lax.ppermute(x, "dp", [(i, i ^ 1) for i in range(8)])


def along_y(x, step):
    return lax.ppermute(
        x, "dp", [(i, ((i // 2 + step) % 4) * 2 + i % 2) for i in range(8)]
    )


def pre_activations(rows, core, y, mine, other, tokens, tokens_other):
    width = tokens.shape[1]
    ntok = tokens.shape[0]

    def chunk(i, place):
        return lax.rem(place[1] + i + 1, 4)

    pre = pl.pallas_call(
        functools.partial(preact, rows),
        grid_spec=pltpu.PrefetchScalarGridSpec(
            num_scalar_prefetch=1,
            grid=(4,),
            in_specs=[
                pl.BlockSpec((2, rows, width), lambda i, p: (4 * p[0] + chunk(i, p), 0, 0)),
                pl.BlockSpec((2, rows, width), lambda i, p: (chunk(i, p), 0, 0)),
                pl.BlockSpec((ntok, width), lambda i, p: (0, 0)),
                pl.BlockSpec((ntok, width), lambda i, p: (0, 0)),
            ],
            out_specs=pl.BlockSpec((2, rows, ntok), lambda i, p: (i, 0, 0)),
        ),
        out_shape=shape((8, rows, ntok)),
        compiler_params=PARAMS,
        cost_estimate=CHEAP,
    )(jnp.stack([core, y]), mine, other, tokens, tokens_other)
    return pre, (pre[1:3] * SCALE).astype(F16), (pre[3:5] * SCALE).astype(F16)


def second_messages(pre, plus, minus, scale):
    from_prev, from_next = along_y(plus, 1), along_y(minus, 3)
    far_plus = (pre[0] * scale + from_prev[1].astype(F32)).astype(F16)
    far_minus = (pre[5] * scale + from_next[0].astype(F32)).astype(F16)
    return from_prev[0], from_next[1], far_plus, far_minus


def totals(pre, from_prev, from_next, far_plus, far_minus):
    far_prev, far_next = along_y(far_plus, 1), along_y(far_minus, 3)
    low = pre[6] + (far_prev.astype(F32) + from_next.astype(F32)) * (1.0 / SCALE)
    high = pre[7] + (far_next.astype(F32) + from_prev.astype(F32)) * (1.0 / SCALE)
    return low, high


def from_partner(x, core, rows, zero=0):
    half = lax.dynamic_slice(x, (8 * (1 - core) + zero, 0, 0), (8, rows, x.shape[2]))
    return swap_cores(half)


def fast(tokens, gate_a, up_a, down_a, gate_b, up_b, down_b, perm):
    local, width = gate_a.shape
    ntok = tokens.shape[0]
    me = lax.axis_index("mp").astype(jnp.int32).reshape(1)
    dp = lax.axis_index("dp").astype(jnp.int32)
    core, y = dp & 1, dp >> 1
    padded = -(-local // 128) * 128
    grid = jnp.pad(
        perm.reshape(NB, local), ((0, 0), (0, padded - local)), constant_values=NB * local
    )
    tokens_other = swap_cores(tokens)

    send, slot_keys, table, bad = call(
        functools.partial(send_one, local),
        [
            shape((NB, 2 * ONE + OVER, width), BF16),
            shape((NB // 4, 2, 8, padded)),
            shape((3, NB, 128)),
            shape((1,), jnp.int32),
        ],
        (me, grid, gate_b, up_b, down_b),
        in_specs=[SMEM, VMEM] + [ANY] * 3,
        out_specs=[VMEM] * 3 + [SMEM],
        scratch_shapes=[pltpu.VMEM((local, width), BF16)] * 3 + [pltpu.SemaphoreType.DMA((3,))],
        params=ALONE,
    )
    one = exchange(send)

    (keys,) = call(
        functools.partial(receive_keys, local),
        [shape((8, padded))],
        (me, grid, table),
        in_specs=[SMEM, VMEM, VMEM],
    )
    (ordered,) = call(
        functools.partial(order_a, local),
        [shape((NB, SLOTS, width), BF16)],
        (keys, gate_a, up_a),
    )
    ordered_other = from_partner(ordered, core, SLOTS)
    two, forward = call(
        functools.partial(send_two, local),
        [shape((NB, 2 * TWO + OVER, width), BF16), shape((NB * OVER, NB * OVER), BF16)],
        (slot_keys, table, gate_b, up_b),
    )
    pre_a, plus_a, minus_a = pre_activations(
        SLOTS, core, y, ordered, ordered_other, tokens, tokens_other
    )

    ready = some(plus_a)
    two, zero = pl.pallas_call(
        fill_forward,
        grid=(1,),
        in_specs=[
            pl.BlockSpec((NB * OVER, NB * OVER), lambda i: (0, 0)),
            pl.BlockSpec((NB, OVER, width), lambda i: (0, 2 * ONE // OVER, 0)),
        ]
        + [ANY] * 2,
        out_specs=[pl.BlockSpec((NB, OVER, width), lambda i: (0, 2 * TWO // OVER, 0)), SMEM],
        out_shape=[shape(two.shape, BF16), shape((1,), jnp.int32)],
        input_output_aliases={2: 0},
        compiler_params=ALONE,
        cost_estimate=CHEAP,
    )(forward, one, two, ready)
    sent_two = two
    two = exchange(two)
    one_other = from_partner(one, core, 2 * ONE, zero[0])
    pre_one, plus, minus = pre_activations(
        2 * ONE, core, y, one, one_other, tokens, tokens_other
    )
    (three,) = call(
        functools.partial(send_three, local),
        [shape((NB, CAP, width), BF16)],
        (slot_keys, down_b, sent_two),
        in_specs=[VMEM, VMEM, ANY],
    )
    tall = keys[:, :local].T
    (scale,) = tie(SCALE, F32, (some(plus), three, tall))
    waiting_a = second_messages(pre_a, plus_a, minus_a, scale)
    waiting_one = second_messages(pre_one, plus, minus, SCALE)
    sums_a = totals(pre_a, *waiting_a)
    sums_one = totals(pre_one, *waiting_one)

    (zero,) = tie(0, jnp.int32, (some(waiting_a[2]),))
    two_other = from_partner(two, core, CAP, zero[0])
    three = exchange(three)
    pre_two, plus, minus = pre_activations(
        CAP, core, y, two, two_other, tokens, tokens_other
    )
    merged_gate, scale = merged_rows(0, tall, gate_a, (one, two), two, (pre_two,))
    waiting_two = second_messages(pre_two, plus, minus, scale)
    ready = some(waiting_two[2])
    merged_up, _ = merged_rows(1, tall, up_a, (one, two), two, (ready,))
    sums_two = totals(pre_two, *waiting_two)

    (corr_one,) = call(
        functools.partial(correlate, ((0, 0, ONE),), False),
        [shape((1, 128))],
        sums_a + sums_one,
    )
    parts = ((2 * ONE, 0, TWO), (2 * CAP, 2 * TWO, HOP))
    (corr,) = call(
        functools.partial(correlate, parts, True),
        [shape((1, 256))],
        sums_a + sums_two + (corr_one, merged_up),
        in_specs=[VMEM] * 5 + [ANY],
    )
    for bit in (1, 2, 4):
        got = lax.ppermute(corr, "dp", [(i, i ^ bit) for i in range(8)])
        corr = jnp.concatenate([corr, got], axis=0)
    (match_corr,) = call(
        functools.partial(unorder, local), [shape((1, local))],
        (dp.reshape(1), keys, corr),
        in_specs=[SMEM, VMEM, VMEM],
    )

    merged_down, _ = merged_rows(2, tall, down_a, (three,), two)
    return (merged_gate, merged_up, merged_down, match_corr.reshape(-1)), bad[0]


def merge_rows(first, second):
    return ((first.astype(F32) + second.astype(F32)) * 0.5).astype(BF16)


def general(tokens, gate_a, up_a, down_a, gate_b, up_b, down_b, perm):
    me = lax.axis_index("mp")
    local = gate_a.shape[0]
    capacity = 2 * local // NB
    source = perm // local
    before = (jnp.arange(local)[:, None] < jnp.arange(local)[None, :]).astype(BF16)

    def rank_of(member):
        return jnp.dot(member.astype(BF16), before, preferred_element_type=F32).astype(jnp.int32)

    mine = (source == me).reshape(NB, local)
    hit = jnp.logical_and(
        mine[:, None, :], rank_of(mine)[:, None, :] == jnp.arange(capacity)[None, :, None]
    ).astype(jnp.int32)
    send_index = jnp.sum(hit * (perm % local).reshape(NB, 1, local), axis=2).reshape(-1)
    arrived = lax.dynamic_slice_in_dim(source, me * local, local)
    member = (jnp.arange(NB)[:, None] == arrived[None, :]).astype(jnp.int32)
    recv_index = arrived * capacity + jnp.sum(member * rank_of(member), axis=0)

    def matched(rows):
        moved = exchange(jnp.take(rows, send_index, axis=0))
        return jnp.take(moved, recv_index, axis=0)

    gate_match, up_match, down_match = matched(gate_b), matched(up_b), matched(down_b)

    def hidden(gate, up):
        g, u = (
            jnp.sum(
                lax.all_to_all(
                    lax.dot_general(
                        tokens, w, (((1,), (1,)), ((), ())), preferred_element_type=F32
                    ).reshape(8, -1, local),
                    "dp",
                    split_axis=0,
                    concat_axis=0,
                    tiled=True,
                ),
                axis=0,
            )
            for w in (gate, up)
        )
        return jax.nn.silu(g) * u

    a, b = hidden(gate_a, up_a), hidden(gate_match, up_match)
    sums = jnp.stack([jnp.sum(x, axis=0) for x in (a, b, a * a, b * b, a * b)])
    for bit in (1, 2, 4):
        sums = sums + lax.ppermute(sums, "dp", [(i, i ^ bit) for i in range(8)])
    sa, sb, saa, sbb, sab = sums
    ntok = tokens.shape[0] * 1.0
    covar = sab - sa * sb / ntok
    var = (saa - sa * sa / ntok) * (sbb - sb * sb / ntok)
    return (
        merge_rows(gate_a, gate_match),
        merge_rows(up_a, up_match),
        merge_rows(down_a, down_match),
        covar / jnp.sqrt(var + 1e-05),
    )


def local_program(*args):
    outs, bad = fast(*args)
    return lax.cond(bad > 0, lambda outs, args: general(*args), lambda outs, args: outs, outs, args)


def solution(mesh):
    return jax.shard_map(
        local_program,
        mesh=mesh,
        in_specs=(P(None, "dp"),) + (P("mp", "dp"),) * 6 + (P(),),
        out_specs=(P("mp", "dp"),) * 3 + (P("mp"),),
        check_vma=False,
    )
```

```python
import functools

import jax
import jax.numpy as jnp
from jax import lax
from jax.experimental import pallas as pl
from jax.experimental.pallas import tpu as pltpu
from jax.sharding import PartitionSpec as P

F32 = jnp.float32
BF16 = jnp.bfloat16
F16 = jnp.float16
NB = 16
CAP = 112
ONE = 64
TWO = CAP - ONE
HOP = 8
OVER = 4 * HOP
SLOTS = 2 * (CAP + HOP)
SCALE = 16.0
VMEM = pl.BlockSpec(memory_space=pltpu.VMEM)
SMEM = pl.BlockSpec(memory_space=pltpu.SMEM)
ANY = pl.BlockSpec(memory_space=pl.ANY)
CHEAP = pl.CostEstimate(flops=0, bytes_accessed=0, transcendentals=0)
ALONE = pltpu.CompilerParams(vmem_limit_bytes=58 * 2**20)
PARAMS = pltpu.CompilerParams(vmem_limit_bytes=24 * 2**20)


def iota(shape, dim):
    return lax.broadcasted_iota(jnp.int32, shape, dim).astype(F32)


def onehot(keys, ids):
    return jnp.where(keys == ids, 1.0, 0.0).astype(BF16)


def pick(hot, rows):
    return jnp.dot(hot, rows, preferred_element_type=F32)


def ranks(member):
    width = member.shape[1]
    before = (
        lax.broadcasted_iota(jnp.int32, (128, 128), 0)
        < lax.broadcasted_iota(jnp.int32, (128, 128), 1)
    )
    before = jnp.where(before, 1.0, 0.0).astype(BF16)
    carry = jnp.zeros((member.shape[0], 1), F32)
    tiles = []
    for j in range(width // 128):
        tile = member[:, j * 128 : (j + 1) * 128]
        tiles.append(jnp.dot(tile.astype(BF16), before, preferred_element_type=F32) + carry)
        carry = carry + jnp.sum(tile, axis=1, keepdims=True)
    return jnp.concatenate(tiles, axis=1)


def block_of(perm, local):
    block = jnp.zeros(perm.shape, F32)
    for k in range(1, NB + 1):
        block = block + jnp.where(perm >= k * local, 1.0, 0.0)
    return block


def tables(local, block):
    lane = iota((NB, 128), 1)
    row = iota((NB, 128), 0)
    count = jnp.zeros((NB, 128), F32)
    for s in range(NB):
        col = jnp.sum(jnp.where(block == s, 1.0, 0.0), axis=1, keepdims=True)
        count = count + jnp.where(lane == s, col, 0.0)
    layers = jnp.maximum(count - CAP, 0.0).astype(jnp.int32)
    layers = ((layers + (NB - 1)) >> 4).astype(F32)
    by_target = jnp.zeros((NB, 128), F32)
    by_source = jnp.zeros((NB, 128), F32)
    for k in range(NB):
        by_target = by_target + jnp.where(row > k, layers[k : k + 1, :], 0.0)
        by_source = by_source + jnp.where(lane > k, layers[:, k : k + 1], 0.0)
    return by_target, by_source, layers


def slot_values(keys, value, first, size):
    slot = iota((size, keys.shape[1]), 0) + first
    return [
        jnp.sum(jnp.where(keys[t : t + 1, :] == slot, value[t : t + 1, :], 0.0), axis=1, keepdims=True)
        - 1.0
        for t in range(keys.shape[0])
    ]


def send_one(
    local, me_ref, perm_ref, gate, up, down, send_ref, key_ref, table_ref, bad_ref, *scratch
):
    *held, sem = scratch
    copies = [
        pltpu.make_async_copy(rows, buffer, sem.at[i])
        for i, (rows, buffer) in enumerate(zip((gate, up, down), held))
    ]
    for copy in copies:
        copy.start()
    me = me_ref[0].astype(F32)
    perm = perm_ref[...]
    width = perm.shape[1]
    block = block_of(perm, local)
    value = perm.astype(F32) - block * local + 1.0
    mine = jnp.where(block == me, 1.0, 0.0)
    by_target, by_source, layers = tables(local, block)
    table_ref[0] = by_target
    table_ref[1] = by_source
    table_ref[2] = layers
    most = jnp.maximum(
        jnp.max(jnp.sum(layers, axis=0, keepdims=True)), jnp.max(jnp.sum(layers, axis=1, keepdims=True))
    )
    bad_ref[0] = jnp.where(most > HOP, 1, 0).astype(jnp.int32)

    rank = ranks(mine)
    base = jnp.where(iota((NB, 128), 1) == me, by_target, 0.0)
    base = jnp.sum(base, axis=1, keepdims=True)
    extra = (rank - CAP).astype(jnp.int32)
    mid = (extra & (NB - 1)).astype(F32)
    layer = (extra >> 4).astype(F32)
    direct = jnp.where(mine * jnp.where(rank < CAP, 1.0, 0.0) > 0, rank, -1.0)
    detour = jnp.where(mine * jnp.where(rank < CAP, 0.0, 1.0) > 0, mid * HOP + base + layer, -1.0)
    for i in range(NB // 4):
        key_ref[i, 0, :4] = direct[4 * i : 4 * i + 4]
        key_ref[i, 1, :4] = value[4 * i : 4 * i + 4]
    cols = slot_values(direct, value, 0, ONE)
    hop_slot = iota((NB * HOP, width), 0)
    hop = jnp.zeros((NB * HOP, width), F32)
    for t in range(NB):
        hop = hop + jnp.where(detour[t : t + 1, :] == hop_slot, value[t : t + 1, :], 0.0)
    hop = jnp.sum(hop, axis=1, keepdims=True) - 1.0

    for copy in copies:
        copy.wait()
    ids = iota((4 * ONE, local), 1)
    for i in range(NB // 4):
        hot = onehot(jnp.concatenate(cols[4 * i : 4 * i + 4], axis=0), ids)
        for j, rows in enumerate(held[:2]):
            out = pick(hot, rows[...]).astype(BF16)
            send_ref[4 * i : 4 * i + 4, j * ONE : (j + 1) * ONE] = out.reshape(4, ONE, -1)
    hot = onehot(hop, iota((NB * HOP, local), 1))
    parts = [pick(hot, rows[...]).reshape(NB, HOP, -1) for rows in held]
    parts.append(jnp.zeros_like(parts[0]))
    send_ref[:, 2 * ONE :] = jnp.concatenate(parts, axis=1).astype(BF16)


def receive_keys(local, me_ref, perm_ref, table_ref, keys_ref):
    me = me_ref[0].astype(F32)
    block = block_of(perm_ref[...], local)
    width = block.shape[1]
    source = jnp.sum(jnp.where(iota(block.shape, 0) == me, block, 0.0), axis=0, keepdims=True)
    member = jnp.where(source == iota((NB, width), 0), 1.0, 0.0)
    rank = jnp.sum(member * ranks(member), axis=0, keepdims=True)
    mine = jnp.where(iota((NB, 128), 0) == me, table_ref[1], 0.0)
    mine = jnp.sum(mine, axis=0, keepdims=True)
    square = jnp.where(iota((NB, 128), 0) == iota((NB, 128), 1), mine, 0.0)
    base = jnp.sum(square, axis=1, keepdims=True)
    base = jnp.sum(member * base, axis=0, keepdims=True)
    extra = (rank - CAP).astype(jnp.int32)
    mid = (extra & (NB - 1)).astype(F32)
    over = base + (extra >> 4).astype(F32)
    first = rank < ONE
    straight = rank < CAP
    k1 = jnp.where(first, source * ONE + rank, -1.0)
    k2 = jnp.where(first, -1.0, jnp.where(straight, source * TWO + (rank - ONE), -1.0))
    ko = jnp.where(straight, -1.0, mid * HOP + over)
    keys_ref[0:1] = jnp.where(straight, source * CAP + rank, NB * CAP + mid * HOP + over)
    keys_ref[1:3] = jnp.zeros((2, width), F32)
    keys_ref[3:4] = k1
    keys_ref[4:5] = k2
    keys_ref[5:6] = ko
    holder = jnp.where(straight, source, mid).astype(jnp.int32)
    piece = (holder & 1).astype(F32)
    device = ((holder >> 1) & 3) * 2 + (holder >> 3)
    keys_ref[6:7] = device.astype(F32)
    keys_ref[7:8] = jnp.where(
        first,
        piece * ONE + rank,
        jnp.where(straight, 2 * ONE + piece * TWO + rank - ONE, 2 * CAP + piece * HOP + over),
    )


def send_two(local, key_ref, table_ref, gate, up, two_ref, forward_ref):
    ids = iota((4 * TWO, local), 1)
    for i in range(NB // 4):
        cols = slot_values(key_ref[i, 0, :4], key_ref[i, 1, :4], ONE, TWO)
        hot = onehot(jnp.concatenate(cols, axis=0), ids)
        for j, rows in enumerate((gate, up)):
            out = pick(hot, rows[...]).astype(BF16)
            two_ref[4 * i : 4 * i + 4, j * TWO : (j + 1) * TWO] = out.reshape(4, TWO, -1)
    two_ref[:, 2 * TWO :] = jnp.zeros((NB, OVER, gate.shape[1]), BF16)
    forward_ref[...] = forwarding(table_ref)


def send_three(local, key_ref, down, *refs):
    three_ref = refs[-1]
    ids = iota((4 * CAP, local), 1)
    for i in range(NB // 4):
        cols = slot_values(key_ref[i, 0, :4], key_ref[i, 1, :4], 0, CAP)
        out = pick(onehot(jnp.concatenate(cols, axis=0), ids), down[...]).astype(BF16)
        three_ref[4 * i : 4 * i + 4] = out.reshape(4, CAP, -1)


def forwarding(table_ref):
    n = NB * OVER
    tall = lax.broadcasted_iota(jnp.int32, (n, NB), 0) >> 5
    tall = onehot(tall, lax.broadcasted_iota(jnp.int32, (n, NB), 1))
    wide = lax.broadcasted_iota(jnp.int32, (128, n), 1) >> 5
    wide = onehot(wide, lax.broadcasted_iota(jnp.int32, (128, n), 0))

    def spread(x):
        part = jnp.dot(tall, x.astype(BF16), preferred_element_type=F32)
        return jnp.dot(part.astype(BF16), wide, preferred_element_type=F32)

    by_target, by_source, layers = table_ref[0], table_ref[1], table_ref[2]
    r = lax.broadcasted_iota(jnp.int32, (n, n), 0)
    c = lax.broadcasted_iota(jnp.int32, (n, n), 1)
    matrix = jnp.where(((r >> 3) & 3) == ((c >> 3) & 3), 1.0, 0.0)
    depth = (c & 7).astype(F32) - spread(by_target)
    same = jnp.where((r & 7).astype(F32) - spread(by_source) == depth, 1.0, 0.0)
    inside = jnp.where(depth >= 0, 1.0, 0.0) * jnp.where(depth < spread(layers), 1.0, 0.0)
    return (matrix * same * inside).astype(BF16)


def fill_forward(forward_ref, one_ref, *refs):
    two_ref, zero_ref = refs[-2:]
    hops = one_ref[...].reshape(NB * OVER, -1)
    out = pick(forward_ref[...], hops).astype(BF16)
    two_ref[...] = out.reshape(two_ref.shape)
    zero_ref[0] = 0


def order_a(local, keys_ref, gate, up, out_ref):
    pair = (gate, up)
    for size, start, line in ((ONE, 0, 3), (TWO, 2 * ONE, 4)):
        key = keys_ref[line : line + 1, :local]
        for i in range(NB // 4):
            hot = onehot(iota((4 * size, local), 0) + 4 * size * i, key)
            for j, rows in enumerate(pair):
                out = pick(hot, rows[...]).astype(BF16)
                out_ref[4 * i : 4 * i + 4, start + j * size : start + (j + 1) * size] = out.reshape(
                    4, size, -1
                )
    hot = onehot(iota((NB * HOP, local), 0), keys_ref[5:6, :local])
    parts = [pick(hot, rows[...]).reshape(NB, HOP, -1) for rows in pair]
    out_ref[:, 2 * CAP :] = jnp.concatenate(parts, axis=1).astype(BF16)


def constant(value, *refs):
    refs[-1][0] = value


def preact(rows, place, own_ref, other_ref, tok_ref, tok_other_ref, out_ref):
    del place
    total = None
    for x, tok in ((own_ref, tok_ref), (other_ref, tok_other_ref)):
        part = lax.dot_general(
            x[:, :rows].reshape(2 * rows, -1),
            tok[...],
            (((1,), (1,)), ((), ())),
            preferred_element_type=F32,
        )
        total = part if total is None else total + part
    out_ref[...] = total.reshape(out_ref.shape)


def compact(matrix, sources, held):
    *near, far = sources
    for s in range(NB):
        start = s * CAP
        for x in near:
            size = x.shape[1]
            held[start : start + size] = x[s]
            start += size
    far = far[...].astype(F32)[:, matrix * HOP : (matrix + 1) * HOP]
    held[NB * CAP :] = far.reshape(NB * HOP, -1).astype(BF16)


def merge(matrix, key_ref, a_ref, *refs):
    out_ref, scale_ref, held = refs[-3:]
    sources = refs[: 3 if matrix < 2 else 2]

    @pl.when(pl.program_id(0) == 0)
    def _():
        compact(matrix, sources, held)
        scale_ref[0] = SCALE

    hot = onehot(key_ref[:, 0:1], iota((key_ref.shape[0], NB * (CAP + HOP)), 1))
    out_ref[...] = ((a_ref[...].astype(F32) + pick(hot, held[...])) * 0.5).astype(BF16)


def merged_rows(matrix, key, a, near, two, tied=()):
    local, width = a.shape
    chunk = local // 4
    block = pl.BlockSpec((chunk, width), lambda i: (i, 0))
    sizes = (ONE, TWO) if matrix < 2 else (CAP,)
    place = matrix if matrix < 2 else 0
    return pl.pallas_call(
        functools.partial(merge, matrix),
        grid=(4,),
        in_specs=[pl.BlockSpec((chunk, key.shape[1]), lambda i: (i, 0)), block]
        + [pl.BlockSpec((NB, size, width), lambda i: (0, place, 0)) for size in sizes]
        + [pl.BlockSpec((NB, OVER, width), lambda i: (0, 2 * TWO // OVER, 0))]
        + [ANY] * len(tied),
        out_specs=[block, SMEM],
        out_shape=[shape((local, width), BF16), shape((1,))],
        scratch_shapes=[pltpu.VMEM((NB * (CAP + HOP), width), BF16)],
        compiler_params=PARAMS,
        cost_estimate=CHEAP,
    )(key, a, *near, two, *tied)


def correlate(parts, earlier, *refs):
    a_refs, b_refs, out_ref = refs[:2], refs[2:4], refs[-1]
    tokens = a_refs[0].shape[1]

    def hidden(ref, start, size):
        g = ref[start : start + size]
        u = ref[start + size : start + 2 * size]
        return g / (1.0 + jnp.exp(-g)) * u

    cols = []
    for start_a, start_b, size in parts:
        for piece in range(2):
            a = hidden(a_refs[piece], start_a, size)
            b = hidden(b_refs[piece], start_b, size)
            sa, sb, saa, sbb, sab = (
                jnp.sum(x, axis=1, keepdims=True) for x in (a, b, a * a, b * b, a * b)
            )
            covar = sab - sa * sb / tokens
            var = (saa - sa * sa / tokens) * (sbb - sb * sb / tokens)
            cols.append(covar / jnp.sqrt(var + 1e-5))
    have = sum(x.shape[0] for x in cols)
    if have < 128:
        cols.append(jnp.zeros((128 - have, 1), F32))
    square = lax.broadcasted_iota(jnp.int32, (128, 128), 0) == lax.broadcasted_iota(
        jnp.int32, (128, 128), 1
    )
    row = jnp.sum(jnp.where(square, jnp.concatenate(cols, axis=0), 0.0), axis=0, keepdims=True)
    if earlier:
        row = jnp.concatenate([refs[4][...], row], axis=1)
    out_ref[...] = row


def unorder(local, me_ref, keys_ref, corr_ref, out_ref):
    place = iota((corr_ref.shape[1], local), 0)
    hot = jnp.where(keys_ref[7:8, :local] == place, 1.0, 0.0)
    rest = corr_ref[...]
    total = jnp.zeros((8, local), F32)
    for _ in range(3):
        part = rest.astype(BF16)
        total = total + jnp.dot(part, hot.astype(BF16), preferred_element_type=F32)
        rest = rest - part.astype(F32)
    owner = lax.broadcasted_iota(jnp.int32, (8, local), 0) ^ me_ref[0]
    keep = jnp.where(keys_ref[6:7, :local] == owner.astype(F32), total, 0.0)
    out_ref[...] = jnp.sum(keep, axis=0, keepdims=True)


def call(kernel, outs, args, in_specs=None, out_specs=None, params=PARAMS, **more):
    specs = in_specs or [VMEM] * len(args)
    made = pl.pallas_call(
        kernel,
        out_shape=outs,
        in_specs=specs,
        out_specs=out_specs or [VMEM] * len(outs),
        compiler_params=params,
        cost_estimate=CHEAP,
        **more,
    )(*args)
    return made


def shape(dims, dtype=F32):
    return jax.ShapeDtypeStruct(dims, dtype)


def some(x):
    return x.reshape(-1, x.shape[-1])[:8, :128].astype(F32)


def tie(value, dtype, after):
    return call(
        functools.partial(constant, value),
        [shape((1,), dtype)],
        after,
        in_specs=[ANY] * len(after),
        out_specs=[SMEM],
    )


def exchange(x):
    return lax.all_to_all(x, "mp", split_axis=0, concat_axis=0, tiled=True)


def swap_cores(x):
    return lax.ppermute(x, "dp", [(i, i ^ 1) for i in range(8)])


def along_y(x, step):
    return lax.ppermute(
        x, "dp", [(i, ((i // 2 + step) % 4) * 2 + i % 2) for i in range(8)]
    )


def pre_activations(rows, core, y, mine, other, tokens, tokens_other):
    width = tokens.shape[1]
    ntok = tokens.shape[0]

    def chunk(i, place):
        return lax.rem(place[1] + i + 1, 4)

    pre = pl.pallas_call(
        functools.partial(preact, rows),
        grid_spec=pltpu.PrefetchScalarGridSpec(
            num_scalar_prefetch=1,
            grid=(4,),
            in_specs=[
                pl.BlockSpec((2, rows, width), lambda i, p: (4 * p[0] + chunk(i, p), 0, 0)),
                pl.BlockSpec((2, rows, width), lambda i, p: (chunk(i, p), 0, 0)),
                pl.BlockSpec((ntok, width), lambda i, p: (0, 0)),
                pl.BlockSpec((ntok, width), lambda i, p: (0, 0)),
            ],
            out_specs=pl.BlockSpec((2, rows, ntok), lambda i, p: (i, 0, 0)),
        ),
        out_shape=shape((8, rows, ntok)),
        compiler_params=PARAMS,
        cost_estimate=CHEAP,
    )(jnp.stack([core, y]), mine, other, tokens, tokens_other)
    return pre, (pre[1:3] * SCALE).astype(F16), (pre[3:5] * SCALE).astype(F16)


def second_messages(pre, plus, minus, scale):
    from_prev, from_next = along_y(plus, 1), along_y(minus, 3)
    far_plus = (pre[0] * scale + from_prev[1].astype(F32)).astype(F16)
    far_minus = (pre[5] * scale + from_next[0].astype(F32)).astype(F16)
    return from_prev[0], from_next[1], far_plus, far_minus


def totals(pre, from_prev, from_next, far_plus, far_minus):
    far_prev, far_next = along_y(far_plus, 1), along_y(far_minus, 3)
    low = pre[6] + (far_prev.astype(F32) + from_next.astype(F32)) * (1.0 / SCALE)
    high = pre[7] + (far_next.astype(F32) + from_prev.astype(F32)) * (1.0 / SCALE)
    return low, high


def from_partner(x, core, rows, zero=0):
    half = lax.dynamic_slice(x, (8 * (1 - core) + zero, 0, 0), (8, rows, x.shape[2]))
    return swap_cores(half)


def fast(tokens, gate_a, up_a, down_a, gate_b, up_b, down_b, perm):
    local, width = gate_a.shape
    ntok = tokens.shape[0]
    me = lax.axis_index("mp").astype(jnp.int32).reshape(1)
    dp = lax.axis_index("dp").astype(jnp.int32)
    core, y = dp & 1, dp >> 1
    padded = -(-local // 128) * 128
    grid = jnp.pad(
        perm.reshape(NB, local), ((0, 0), (0, padded - local)), constant_values=NB * local
    )
    tokens_other = swap_cores(tokens)

    send, slot_keys, table, bad = call(
        functools.partial(send_one, local),
        [
            shape((NB, 2 * ONE + OVER, width), BF16),
            shape((NB // 4, 2, 8, padded)),
            shape((3, NB, 128)),
            shape((1,), jnp.int32),
        ],
        (me, grid, gate_b, up_b, down_b),
        in_specs=[SMEM, VMEM] + [ANY] * 3,
        out_specs=[VMEM] * 3 + [SMEM],
        scratch_shapes=[pltpu.VMEM((local, width), BF16)] * 3 + [pltpu.SemaphoreType.DMA((3,))],
        params=ALONE,
    )
    one = exchange(send)

    (keys,) = call(
        functools.partial(receive_keys, local),
        [shape((8, padded))],
        (me, grid, table),
        in_specs=[SMEM, VMEM, VMEM],
    )
    (ordered,) = call(
        functools.partial(order_a, local),
        [shape((NB, SLOTS, width), BF16)],
        (keys, gate_a, up_a),
    )
    ordered_other = from_partner(ordered, core, SLOTS)
    two, forward = call(
        functools.partial(send_two, local),
        [shape((NB, 2 * TWO + OVER, width), BF16), shape((NB * OVER, NB * OVER), BF16)],
        (slot_keys, table, gate_b, up_b),
    )
    pre_a, plus_a, minus_a = pre_activations(
        SLOTS, core, y, ordered, ordered_other, tokens, tokens_other
    )

    ready = pre_a
    two, zero = pl.pallas_call(
        fill_forward,
        grid=(1,),
        in_specs=[
            pl.BlockSpec((NB * OVER, NB * OVER), lambda i: (0, 0)),
            pl.BlockSpec((NB, OVER, width), lambda i: (0, 2 * ONE // OVER, 0)),
        ]
        + [ANY] * 2,
        out_specs=[pl.BlockSpec((NB, OVER, width), lambda i: (0, 2 * TWO // OVER, 0)), SMEM],
        out_shape=[shape(two.shape, BF16), shape((1,), jnp.int32)],
        input_output_aliases={2: 0},
        compiler_params=ALONE,
        cost_estimate=CHEAP,
    )(forward, one, two, ready)
    sent_two = two
    two = exchange(two)
    one_other = from_partner(one, core, 2 * ONE, zero[0])
    pre_one, plus, minus = pre_activations(
        2 * ONE, core, y, one, one_other, tokens, tokens_other
    )
    (three,) = call(
        functools.partial(send_three, local),
        [shape((NB, CAP, width), BF16)],
        (slot_keys, down_b, sent_two),
        in_specs=[VMEM, VMEM, ANY],
    )
    tall = keys[:, :local].T
    (scale,) = tie(SCALE, F32, (some(plus), three, tall))
    waiting_a = second_messages(pre_a, plus_a, minus_a, scale)
    waiting_one = second_messages(pre_one, plus, minus, SCALE)
    sums_a = totals(pre_a, *waiting_a)
    sums_one = totals(pre_one, *waiting_one)

    (zero,) = tie(0, jnp.int32, (some(waiting_a[2]),))
    two_other = from_partner(two, core, CAP, zero[0])
    three = exchange(three)
    pre_two, plus, minus = pre_activations(
        CAP, core, y, two, two_other, tokens, tokens_other
    )
    merged_gate, scale = merged_rows(0, tall, gate_a, (one, two), two, (pre_two,))
    waiting_two = second_messages(pre_two, plus, minus, scale)
    ready = some(waiting_two[2])
    merged_up, _ = merged_rows(1, tall, up_a, (one, two), two, (ready,))
    sums_two = totals(pre_two, *waiting_two)

    (corr_one,) = call(
        functools.partial(correlate, ((0, 0, ONE),), False),
        [shape((1, 128))],
        sums_a + sums_one,
    )
    parts = ((2 * ONE, 0, TWO), (2 * CAP, 2 * TWO, HOP))
    (corr,) = call(
        functools.partial(correlate, parts, True),
        [shape((1, 256))],
        sums_a + sums_two + (corr_one, merged_up),
        in_specs=[VMEM] * 5 + [ANY],
    )
    for bit in (1, 2, 4):
        got = lax.ppermute(corr, "dp", [(i, i ^ bit) for i in range(8)])
        corr = jnp.concatenate([corr, got], axis=0)
    (match_corr,) = call(
        functools.partial(unorder, local), [shape((1, local))],
        (dp.reshape(1), keys, corr),
        in_specs=[SMEM, VMEM, VMEM],
    )

    merged_down, _ = merged_rows(2, tall, down_a, (three,), two)
    return (merged_gate, merged_up, merged_down, match_corr.reshape(-1)), bad[0]


def merge_rows(first, second):
    return ((first.astype(F32) + second.astype(F32)) * 0.5).astype(BF16)


def general(tokens, gate_a, up_a, down_a, gate_b, up_b, down_b, perm):
    me = lax.axis_index("mp")
    local = gate_a.shape[0]
    capacity = 2 * local // NB
    source = perm // local
    before = (jnp.arange(local)[:, None] < jnp.arange(local)[None, :]).astype(BF16)

    def rank_of(member):
        return jnp.dot(member.astype(BF16), before, preferred_element_type=F32).astype(jnp.int32)

    mine = (source == me).reshape(NB, local)
    hit = jnp.logical_and(
        mine[:, None, :], rank_of(mine)[:, None, :] == jnp.arange(capacity)[None, :, None]
    ).astype(jnp.int32)
    send_index = jnp.sum(hit * (perm % local).reshape(NB, 1, local), axis=2).reshape(-1)
    arrived = lax.dynamic_slice_in_dim(source, me * local, local)
    member = (jnp.arange(NB)[:, None] == arrived[None, :]).astype(jnp.int32)
    recv_index = arrived * capacity + jnp.sum(member * rank_of(member), axis=0)

    def matched(rows):
        moved = exchange(jnp.take(rows, send_index, axis=0))
        return jnp.take(moved, recv_index, axis=0)

    gate_match, up_match, down_match = matched(gate_b), matched(up_b), matched(down_b)

    def hidden(gate, up):
        g, u = (
            jnp.sum(
                lax.all_to_all(
                    lax.dot_general(
                        tokens, w, (((1,), (1,)), ((), ())), preferred_element_type=F32
                    ).reshape(8, -1, local),
                    "dp",
                    split_axis=0,
                    concat_axis=0,
                    tiled=True,
                ),
                axis=0,
            )
            for w in (gate, up)
        )
        return jax.nn.silu(g) * u

    a, b = hidden(gate_a, up_a), hidden(gate_match, up_match)
    sums = jnp.stack([jnp.sum(x, axis=0) for x in (a, b, a * a, b * b, a * b)])
    for bit in (1, 2, 4):
        sums = sums + lax.ppermute(sums, "dp", [(i, i ^ bit) for i in range(8)])
    sa, sb, saa, sbb, sab = sums
    ntok = tokens.shape[0] * 1.0
    covar = sab - sa * sb / ntok
    var = (saa - sa * sa / ntok) * (sbb - sb * sb / ntok)
    return (
        merge_rows(gate_a, gate_match),
        merge_rows(up_a, up_match),
        merge_rows(down_a, down_match),
        covar / jnp.sqrt(var + 1e-05),
    )


def local_program(*args):
    outs, bad = fast(*args)
    return lax.cond(bad > 0, lambda outs, args: general(*args), lambda outs, args: outs, outs, args)


def solution(mesh):
    return jax.shard_map(
        local_program,
        mesh=mesh,
        in_specs=(P(None, "dp"),) + (P("mp", "dp"),) * 6 + (P(),),
        out_specs=(P("mp", "dp"),) * 3 + (P("mp"),),
        check_vma=False,
    )
```
